32 devices in a mesh: seq: 8 (over y, x, core), exp: 4 (over z).
Axes of the slice: x: 2, y: 2, z: 4, core: 2. Of those that a mesh axis runs over, the one named last changes fastest.
Arguments:
- inputs: bfloat16 [4, 4096, 768], P('exp', 'seq'), may hold values from -6 to 6
- token_ids: int32 [4, 4096], P('exp', 'seq'), may hold values from 0 to 50256, as said below
- hash_table: int32 [50257], replicated, may hold values from 0 to 3
- capacity: int32 [4], replicated, may hold values from 80 to 160, as said below
- ln1_gain: float32 [768], replicated, may hold values from 0.5 to 1.5
- ln1_bias: float32 [768], replicated, may hold values from -0.6 to 0.6
- w_qkv: bfloat16 [768, 2304], replicated, may hold values from -0.21875 to 0.21875
- q_bias: float32 [768], replicated, may hold values from -0.6 to 0.6
- v_bias: float32 [768], replicated, may hold values from -0.6 to 0.6
- w_out: bfloat16 [768, 768], replicated, may hold values from -0.875 to 0.875
- out_bias: float32 [768], replicated, may hold values from -0.6 to 0.6
- ln2_gain: float32 [768], replicated, may hold values from 0.5 to 1.5
- ln2_bias: float32 [768], replicated, may hold values from -0.6 to 0.6
- up_weight: bfloat16 [4, 768, 3072], P('exp'), may hold values from -0.21875 to 0.21875
- up_bias: float32 [4, 3072], P('exp'), may hold values from -0.6 to 0.6
- down_weight: bfloat16 [4, 3072, 768], P('exp'), may hold values from -0.109375 to 0.109375
- down_bias: float32 [4, 768], P('exp'), may hold values from -0.6 to 0.6
- out_grad: bfloat16 [4, 4096, 768], P('exp', 'seq'), may hold values from -6 to 6
Outputs:
- output: bfloat16 [4, 4096, 768], P('exp', 'seq')
- input_grad: float32 [4, 4096, 768], P('exp', 'seq')
- ln1_gain_grad: float32 [768], replicated
- ln1_bias_grad: float32 [768], replicated
- w_qkv_grad: float32 [768, 2304], replicated
- q_bias_grad: float32 [768], replicated
- v_bias_grad: float32 [768], replicated
- w_out_grad: float32 [768, 768], replicated
- out_bias_grad: float32 [768], replicated
- ln2_gain_grad: float32 [768], replicated
- ln2_bias_grad: float32 [768], replicated
- up_weight_grad: float32 [4, 768, 3072], P('exp', None, 'seq')
- up_bias_grad: float32 [4, 3072], P('exp', 'seq')
- down_weight_grad: float32 [4, 3072, 768], P('exp', 'seq')
- down_bias_grad: float32 [4, 768], P('exp', 'seq')
The draws below stay inside these ranges and needn't reach their ends.
Inputs may be any that keep to these rules, and one draw needn't show every extreme that they name: `token_ids`: ids of one device's block are heavy-tailed: one id, which hash_table sends to an expert of capacity 160, fills between 160 and 320 positions of every block. Some expert has capacity exactly 160.
All inputs are finite; a program needn't handle non-finite values.
Results may differ from the reference program's by a relative error of at most 0.025.
Values may be sent and summed in bfloat16 or wider, within the bound.
No kernel may reach another device: no remote copies, remote signals or barrier semaphores. Data moves between devices by JAX's collectives and lax.ppermute only.
A program may use at most 384 MiB of HBM per device.

```python
import math
import jax
import jax.numpy as jnp
from jax import lax

D = 768
HEADS = 12
HEAD_DIM = 64
FF = 3072
VOCAB = 50257
SEQ_LEN = 4096
TOK_DEV = 512
EXPERTS = 4
STRETCH = 512
SEQ_DEV = 1
BATCH = 4
CAP = 160
N_SEQ = 8
N_EXP = 4


def routing_plan(key):
    base = jax.random.fold_in(key, 11)
    hot_id = jax.random.randint(jax.random.fold_in(base, 1), (), 0, VOCAB)
    hot_expert = jax.random.randint(jax.random.fold_in(base, 2), (), 0, EXPERTS)
    return (hot_id, hot_expert)


def draw_hash_table(key, part):
    hot_id, hot_expert = routing_plan(key)
    table = jax.random.randint(jax.random.fold_in(key, 21), (VOCAB,), 0, EXPERTS)
    return table.at[hot_id].set(hot_expert).astype(jnp.int32)


def draw_capacity(key, part):
    hot_id, hot_expert = routing_plan(key)
    limits = jax.random.randint(jax.random.fold_in(key, 31), (EXPERTS,), max(CAP // 2, 1), CAP + 1)
    return limits.at[hot_expert].set(CAP).astype(jnp.int32)


def draw_token_ids(key, part):
    hot_id, hot_expert = routing_plan(key)
    devices = N_EXP * N_SEQ
    hot_count = jax.random.randint(jax.random.fold_in(key, 41), (devices, 1), CAP, 2 * CAP + 1)
    marks = jax.random.randint(jax.random.fold_in(key, 42), (devices, TOK_DEV), 0, TOK_DEV)
    marks = marks * TOK_DEV + lax.iota(jnp.int32, TOK_DEV)[None, :]
    order = jnp.argsort(jnp.argsort(marks, axis=1, stable=True), axis=1, stable=True)
    warm = jax.random.randint(jax.random.fold_in(key, 43), (64,), 0, VOCAB)
    pick = jax.random.randint(jax.random.fold_in(key, 44), (devices, TOK_DEV), 0, 64)
    common = jax.random.randint(jax.random.fold_in(key, 45), (devices, TOK_DEV), 0, 2)
    rare = jax.random.randint(jax.random.fold_in(key, 46), (devices, TOK_DEV), 0, VOCAB)
    ids = jnp.where(order < hot_count, hot_id, jnp.where(common == 0, jnp.take(warm, pick), rare))
    ids = ids.reshape(N_EXP, N_SEQ, SEQ_DEV, STRETCH).transpose(0, 2, 1, 3).reshape(BATCH, SEQ_LEN)
    return ids.astype(jnp.int32)


def block_levels(stream_key, dims, pieces, low, top_value):
    factor_of, own = 1.0, jax.random.fold_in(stream_key, 6)
    for position, blocks in pieces:
        heights = jnp.exp(jax.random.uniform(jax.random.fold_in(own, position), (blocks,), jnp.float32, low / len(pieces), top_value / len(pieces)))
        factor_of = factor_of * jnp.repeat(heights, dims[position] // blocks).reshape([-1 if axis == position else 1 for axis in range(len(dims))])
    return factor_of


def centred(stream_key, extent, deviation, most, cuts=(), kind=jnp.bfloat16):
    values = deviation * jax.random.normal(stream_key, extent, jnp.float32)
    if cuts:
        values = values * block_levels(stream_key, extent, cuts, -0.22, 0.18)
    return jnp.clip(values, -most, most).astype(kind)


def setup_inputs(seed: int = 0) -> dict:
    arg_keys = jax.random.split(jax.random.key(seed), 19)
    inputs = centred(arg_keys[0], (BATCH, SEQ_LEN, D), 1.0, 6.0, ((0, 4), (1, 8)))
    token_ids = draw_token_ids(jax.random.fold_in(arg_keys[18], 71), 0)
    hash_table = draw_hash_table(jax.random.fold_in(arg_keys[18], 71), 0)
    capacity = draw_capacity(jax.random.fold_in(arg_keys[18], 71), 0)
    ln1_gain = jnp.clip(1.0 + 0.1 * jax.random.normal(arg_keys[4], (D,), jnp.float32), 0.5, 1.5)
    ln1_bias = centred(arg_keys[5], (D,), 0.1, 0.6, (), jnp.float32)
    w_qkv = centred(arg_keys[6], (D, 3 * D), D ** -0.5, 0.21875)
    q_bias = centred(arg_keys[7], (D,), 0.1, 0.6, (), jnp.float32)
    v_bias = centred(arg_keys[8], (D,), 0.1, 0.6, (), jnp.float32)
    w_out = centred(arg_keys[9], (D, D), (D // 16) ** -0.5, 0.875)
    out_bias = centred(arg_keys[10], (D,), 0.1, 0.6, (), jnp.float32)
    ln2_gain = jnp.clip(1.0 + 0.1 * jax.random.normal(arg_keys[11], (D,), jnp.float32), 0.5, 1.5)
    ln2_bias = centred(arg_keys[12], (D,), 0.1, 0.6, (), jnp.float32)
    up_weight = centred(arg_keys[13], (EXPERTS, D, FF), D ** -0.5, 0.21875, ((0, 4),))
    up_bias = centred(arg_keys[14], (EXPERTS, FF), 0.1, 0.6, ((0, 4),), jnp.float32)
    down_weight = centred(arg_keys[15], (EXPERTS, FF, D), FF ** -0.5, 0.109375, ((0, 4),))
    down_bias = centred(arg_keys[16], (EXPERTS, D), 0.1, 0.6, ((0, 4),), jnp.float32)
    out_grad = centred(arg_keys[17], (BATCH, SEQ_LEN, D), 1.0, 6.0, ((0, 4), (1, 8)))
    return {"inputs": inputs, "token_ids": token_ids, "hash_table": hash_table, "capacity": capacity, "ln1_gain": ln1_gain, "ln1_bias": ln1_bias, "w_qkv": w_qkv, "q_bias": q_bias, "v_bias": v_bias, "w_out": w_out, "out_bias": out_bias, "ln2_gain": ln2_gain, "ln2_bias": ln2_bias, "up_weight": up_weight, "up_bias": up_bias, "down_weight": down_weight, "down_bias": down_bias, "out_grad": out_grad}


@jax.custom_vjp
def low(v):
    return lax.optimization_barrier(v.astype(jnp.bfloat16)).astype(jnp.float32)

@jax.custom_vjp
def low_back(v):
    return v

def low_keep(v):
    return (low(v), None)

def low_pass(kept, grad):
    return (grad,)

def back_keep(v):
    return (v, None)

def back_low(kept, grad):
    return (low(grad),)
low.defvjp(low_keep, low_pass)
low_back.defvjp(back_keep, back_low)
norm_eps = 1e-05
logit_scale = 0.125
masked_score = -1e+30
full_precision = lax.Precision.HIGHEST

def layer_norm(values, gain, shift):
    centre = lax.optimization_barrier(jnp.mean(values, axis=-1, keepdims=True))
    centered = values - centre
    spread = lax.optimization_barrier(jnp.mean(centered * centered, axis=-1, keepdims=True))
    return centered * lax.rsqrt(spread + norm_eps) * gain + shift

def smooth_unit(values):
    return jax.nn.gelu(values, approximate=False)

def reference(inputs, token_ids, hash_table, capacity, ln1_gain, ln1_bias, w_qkv, q_bias, v_bias, w_out, out_bias, ln2_gain, ln2_bias, up_weight, up_bias, down_weight, down_bias, out_grad):
    devices = N_EXP * N_SEQ
    rows_all = EXPERTS * devices * CAP
    expert_of = jnp.take(hash_table, token_ids).astype(jnp.int32)
    blocks = expert_of.reshape(N_EXP, SEQ_DEV, N_SEQ, STRETCH).transpose(0, 2, 1, 3).reshape(devices, TOK_DEV)
    onehot = (blocks[:, :, None] == jnp.arange(EXPERTS, dtype=jnp.int32)[None, None, :]).astype(jnp.int32)
    running = jnp.cumsum(onehot, axis=1).astype(jnp.int32) - 1
    rank = lax.optimization_barrier(jnp.sum(onehot * running, axis=2)).astype(jnp.int32)
    kept = rank < jnp.take(capacity, blocks)
    owner = jnp.arange(devices, dtype=jnp.int32)[:, None]
    slot = jnp.where(kept, blocks * (devices * CAP) + owner * CAP + rank, rows_all).astype(jnp.int32)

    def unblock(values):
        return values.reshape(N_EXP, N_SEQ, SEQ_DEV, STRETCH).transpose(0, 2, 1, 3).reshape(BATCH * SEQ_LEN)
    kept_rows = unblock(kept)
    slot_rows = unblock(slot)
    fetch = jnp.minimum(slot_rows, rows_all - 1).astype(jnp.int32)
    group = math.gcd(BATCH, max(1, 4096 // SEQ_LEN))
    places = jnp.arange(SEQ_LEN, dtype=jnp.int32)
    visible = places[None, :] <= places[:, None]

    def head_attend(triple):
        query_heads, key_heads, value_heads = triple
        attention_scores = low_back(jnp.einsum('amt,awt->amw', query_heads, key_heads, precision=full_precision) * logit_scale)
        attention_scores = jnp.where(visible, attention_scores, masked_score)
        top = lax.optimization_barrier(jnp.max(attention_scores, axis=-1, keepdims=True))
        lse = top + jnp.log(lax.optimization_barrier(jnp.sum(jnp.exp(attention_scores - top), axis=-1, keepdims=True)))
        attention_probs = low(jnp.exp(attention_scores - lse))
        return jnp.einsum('meg,mgt->met', attention_probs, value_heads, precision=full_precision)

    def forward(x, g1, c1, wqkv, bq, bv, wo, bo, g2, c2, wup, bup, wdown, bdown):

        def attend_group(xg):
            h1 = low(layer_norm(xg, g1, c1))
            proj = jnp.einsum('bld,de->ble', h1, wqkv, precision=full_precision)
            q = low_back(low(proj[..., :D] + bq)).reshape(group, SEQ_LEN, HEADS, HEAD_DIM)
            k = low_back(low(proj[..., D:2 * D])).reshape(group, SEQ_LEN, HEADS, HEAD_DIM)
            v = low_back(low(proj[..., 2 * D:] + bv)).reshape(group, SEQ_LEN, HEADS, HEAD_DIM)
            heads_out = lax.map(jax.checkpoint(head_attend), (q.transpose(2, 0, 1, 3), k.transpose(2, 0, 1, 3), v.transpose(2, 0, 1, 3)))
            o = heads_out.transpose(1, 2, 0, 3).reshape(group, SEQ_LEN, D)
            o = low_back(low(o))
            a = low_back(jnp.einsum('bld,de->ble', o, wo, precision=full_precision) + bo)
            return xg + a
        x2 = lax.map(jax.checkpoint(attend_group), x.reshape(BATCH // group, group, SEQ_LEN, D))
        x2 = x2.reshape(BATCH * SEQ_LEN, D)
        h2 = low_back(low(layer_norm(x2, g2, c2)))
        buffer = jnp.zeros((rows_all, D), jnp.float32).at[slot_rows].set(h2, mode='drop')
        buffer = buffer.reshape(EXPERTS, devices * CAP, D)
        z = low_back(jnp.einsum('erd,edf->erf', buffer, wup, precision=full_precision) + bup[:, None, :])
        hid = low(smooth_unit(z))
        y = low_back(low(jnp.einsum('erf,efd->erd', hid, wdown, precision=full_precision) + bdown[:, None, :]))
        back = jnp.take(y.reshape(rows_all, D), fetch, axis=0)
        f = jnp.where(kept_rows[:, None], back, 0.0)
        return x2 + f
    params = (inputs.astype(jnp.float32).reshape(BATCH, SEQ_LEN, D), ln1_gain, ln1_bias, w_qkv.astype(jnp.float32), q_bias, v_bias, w_out.astype(jnp.float32), out_bias, ln2_gain, ln2_bias, up_weight.astype(jnp.float32), up_bias, down_weight.astype(jnp.float32), down_bias)
    result, pullback = jax.vjp(forward, *params)
    grads = pullback(out_grad.astype(jnp.float32).reshape(BATCH * SEQ_LEN, D))
    output = result.astype(jnp.bfloat16).reshape(BATCH, SEQ_LEN, D)
    return (output, grads[0], grads[1], grads[2], grads[3], grads[4], grads[5], grads[6], grads[7], grads[8], grads[9], grads[10], grads[11], grads[12], grads[13])
```

```python
from functools import partial
import math

import jax
import jax.numpy as jnp
from jax import lax
from jax.experimental import pallas as pl
from jax.experimental.pallas import tpu as pltpu
from jax.sharding import PartitionSpec as P

HEADS = 12
HEAD_DIM = 64
f32 = jnp.float32
bf16 = jnp.bfloat16

norm_eps = 1e-05
logit_scale = 0.125
masked_score = -1e30
LOG2E = math.log2(math.e)

QT = 512
KC = 1024
SUB = 256
VMEM = 56 * 2**20


def rows_of(start, size):
    return pl.ds(pl.multiple_of(start, size), size)


def fwd_kernel(
    n_ref,
    base_ref,
    tile_ref,
    q_ref,
    k_ref,
    vt_ref,
    place_ref,
    o_ref,
    linv_ref,
    p_hbm,
    s_scr,
    p_scr,
    m_scr,
    acc_scr,
    l_scr,
    sem,
):
    i = pl.program_id(0)
    last = pl.num_programs(0) - 1
    a = lax.rem(i, 2)
    b = 1 - a
    before = jnp.maximum(i - 1, 0)
    n1 = n_ref[i]
    n2 = n_ref[before]
    base1 = base_ref[i]
    base2 = base_ref[before]

    def first(c, masked):
        q = q_ref[...]
        m = m_scr[a]
        for j in range(KC // SUB):
            off = c * KC + j * SUB
            s = jnp.dot(k_ref[rows_of(base1 + off, SUB), :], q, preferred_element_type=f32)
            if masked:
                key = lax.broadcasted_iota(jnp.int32, (SUB, QT), 0)
                s = jnp.where(key <= place_ref[...] - off, s, masked_score)
            s_scr[a, rows_of(off, SUB), :] = s
            m = jnp.maximum(m, jnp.max(s.reshape(SUB // 8, 8, QT), axis=0))
        m_scr[a] = m

    def second(c):
        top = jnp.max(m_scr[b], axis=0, keepdims=True) * (logit_scale * LOG2E)
        l = l_scr[...]
        for j in range(KC // SUB):
            off = c * KC + j * SUB
            s = s_scr[b, rows_of(off, SUB), :]
            p = jnp.exp2(s * (logit_scale * LOG2E) - top)
            l = l + jnp.sum(p.reshape(SUB // 8, 8, QT), axis=0)
            low = p.astype(bf16)
            p_scr[b, rows_of(off, SUB), :] = low
            acc_scr[...] += jnp.dot(
                vt_ref[:, rows_of(base2 + off, SUB)], low, preferred_element_type=f32
            )
        l_scr[...] = l
        part = rows_of(c * KC, KC)
        pltpu.make_async_copy(p_scr.at[b, part], p_hbm.at[before, part], sem.at[b]).start()

    def drain(count, slot):
        def wait(c, _):
            part = pl.ds(0, KC)
            pltpu.make_async_copy(p_scr.at[slot, part], p_hbm.at[0, part], sem.at[slot]).wait()
            return 0

        lax.fori_loop(0, count, wait, 0)

    def loop(low, high, do):
        def step(c, _):
            do(c)
            return 0

        lax.fori_loop(low, high, step, 0)

    m_scr[a] = jnp.full((8, QT), -jnp.inf, f32)

    @pl.when(i >= 1)
    def _():
        l_scr[...] = jnp.zeros_like(l_scr)
        acc_scr[...] = jnp.zeros_like(acc_scr)

    @pl.when(i >= 3)
    def _():
        drain(n_ref[jnp.maximum(i - 3, 0)], b)

    @pl.when(i == 0)
    def _():
        loop(0, n1, lambda c: first(c, True))

    @pl.when(jnp.logical_and(i > 0, i < last))
    def _():
        first(n1 - 1, True)
        second(n2 - 1)
        both = jnp.minimum(n1, n2) - 1

        def step(c):
            first(c, False)
            second(c)

        loop(0, both, step)
        loop(both, n1 - 1, lambda c: first(c, False))
        loop(both, n2 - 1, second)

    @pl.when(i == last)
    def _():
        loop(0, n2, second)

    @pl.when(i > 0)
    def _():
        linv = 1.0 / jnp.sum(l_scr[...], axis=0, keepdims=True)
        o_ref[...] = acc_scr[...] * linv
        linv_ref[...] = linv

    @pl.when(i == last)
    def _():
        drain(n_ref[jnp.maximum(i - 2, 0)], a)
        drain(n2, b)


def tile_lists(tiles, nk):
    final = (tiles[-1][0], tiles[-1][1], 0)
    parity = [0]
    for t in tiles:
        parity.append((parity[-1] + t[2]) % 2)
    listed = tiles + [final]
    return (
        jnp.array([t[2] for t in listed], jnp.int32),
        jnp.array([t[1] * nk for t in listed], jnp.int32),
        jnp.array([t[0] for t in listed], jnp.int32),
        jnp.array(parity, jnp.int32),
    )


def pair_units(tiles):
    return sum(t[2] for t in tiles) * KC * QT


def attn_fwd(qt, k, vt, place, tiles, nk):
    count, base, which, _ = tile_lists(tiles, nk)
    nq = qt.shape[1]
    steps = len(tiles)

    def now(r):
        return pl.BlockSpec((r, QT), lambda i, n, b, s: (0, s[i]))

    def prev(r):
        return pl.BlockSpec((r, QT), lambda i, n, b, s: (0, s[jnp.maximum(i - 1, 0)]))

    def whole(x):
        return pl.BlockSpec(x.shape, lambda i, n, b, s: (0, 0))

    work = pair_units(tiles)
    return pl.pallas_call(
        fwd_kernel,
        name="attn_fwd",
        grid_spec=pltpu.PrefetchScalarGridSpec(
            num_scalar_prefetch=3,
            grid=(steps + 1,),
            in_specs=[now(HEAD_DIM), whole(k), whole(vt), now(1)],
            out_specs=[prev(HEAD_DIM), prev(1), pl.BlockSpec(memory_space=pl.ANY)],
            scratch_shapes=[
                pltpu.VMEM((2, nk, QT), f32),
                pltpu.VMEM((2, nk, QT), bf16),
                pltpu.VMEM((2, 8, QT), f32),
                pltpu.VMEM((HEAD_DIM, QT), f32),
                pltpu.VMEM((8, QT), f32),
                pltpu.SemaphoreType.DMA((2,)),
            ],
        ),
        out_shape=[
            jax.ShapeDtypeStruct((HEAD_DIM, nq), f32),
            jax.ShapeDtypeStruct((1, nq), f32),
            jax.ShapeDtypeStruct((steps, nk, QT), bf16),
        ],
        compiler_params=pltpu.CompilerParams(vmem_limit_bytes=VMEM),
        cost_estimate=pl.CostEstimate(
            flops=work * 1024, bytes_accessed=work * 2, transcendentals=work
        ),
    )(count, base, which, qt, k, vt, place)


def bwd_kernel(
    n_ref,
    base_ref,
    tile_ref,
    parity_ref,
    qt_ref,
    dot_ref,
    o_ref,
    linv_ref,
    kt_ref,
    v_ref,
    p_hbm,
    dq_ref,
    dk_ref,
    dv_ref,
    p_scr,
    dp_scr,
    q_scr,
    do_scr,
    de_scr,
    dq_scr,
    sem,
):
    i = pl.program_id(0)
    last = pl.num_programs(0) - 1
    a = lax.rem(i, 2)
    b = 1 - a
    before = jnp.maximum(i - 1, 0)
    n1 = n_ref[i]
    n2 = n_ref[before]
    base1 = base_ref[i]
    base2 = base_ref[before]
    par1 = parity_ref[i]
    par2 = parity_ref[before]

    def fetch(t, slot):
        def start(c, _):
            part = rows_of(c * KC, KC)
            pltpu.make_async_copy(p_hbm.at[t, part], p_scr.at[slot, part], sem.at[slot]).start()
            return 0

        lax.fori_loop(0, n_ref[t], start, 0)

    def dp_of(c):
        for j in range(KC // SUB):
            off = c * KC + j * SUB
            dp_scr[lax.rem(c + par1, 2), pl.ds(j * SUB, SUB), :] = jnp.dot(
                v_ref[rows_of(base1 + off, SUB), :], do_scr[a], preferred_element_type=f32
            )

    def sums(c, slot, base, par):
        qt = q_scr[slot]
        dot = do_scr[slot]
        delta = de_scr[slot]
        dq = dq_scr[...]
        for j in range(KC // SUB):
            off = c * KC + j * SUB
            p = p_scr[slot, rows_of(off, SUB), :]
            dp = dp_scr[lax.rem(c + par, 2), pl.ds(j * SUB, SUB), :]
            ds = (p.astype(f32) * (dp - delta)).astype(bf16)
            keys = rows_of(base + off, SUB)
            dv_ref[:, keys] += lax.dot_general(
                dot, p, (((1,), (1,)), ((), ())), preferred_element_type=f32
            )
            dk_ref[:, keys] += lax.dot_general(
                qt, ds, (((1,), (1,)), ((), ())), preferred_element_type=f32
            )
            dq = dq + jnp.dot(kt_ref[:, keys], ds, preferred_element_type=f32)
        dq_scr[...] = dq

    def load():
        scaled = dot_ref[...].astype(f32) * linv_ref[...]
        de_scr[a] = jnp.sum(scaled * o_ref[...], axis=0, keepdims=True)
        do_scr[a] = scaled.astype(bf16)
        q_scr[a] = qt_ref[...]

    @pl.when(i == 0)
    def _():
        dk_ref[...] = jnp.zeros_like(dk_ref)
        dv_ref[...] = jnp.zeros_like(dv_ref)
        dq_scr[...] = jnp.zeros_like(dq_scr)
        fetch(0, 0)
        load()
        dp_of(0)

    @pl.when(jnp.logical_and(i > 0, i < last))
    def _():
        load()
        dp_of(0)
        sums(n2 - 1, b, base2, par2)

    @pl.when(i == last)
    def _():
        sums(n2 - 1, b, base2, par2)

    @pl.when(i > 0)
    def _():
        dq_ref[...] = dq_scr[...] * logit_scale
        dq_scr[...] = jnp.zeros_like(dq_scr)

    @pl.when(i < last)
    def _():
        def wait(c, _):
            part = pl.ds(0, KC)
            pltpu.make_async_copy(p_hbm.at[0, part], p_scr.at[a, part], sem.at[a]).wait()
            return 0

        lax.fori_loop(0, n1, wait, 0)

        @pl.when(i + 1 < last)
        def _():
            fetch(i + 1, b)

        def step(c, _):
            dp_of(c + 1)
            sums(c, a, base1, par1)
            return 0

        lax.fori_loop(0, n1 - 1, step, 0)


def attn_bwd(qt, dot, o, linv, kt, v, p, tiles, nk):
    count, base, which, parity = tile_lists(tiles, nk)
    nq = qt.shape[1]
    steps = len(tiles)

    def now(r):
        return pl.BlockSpec((r, QT), lambda i, n, b, s, e: (0, s[i]))

    def prev(r):
        return pl.BlockSpec((r, QT), lambda i, n, b, s, e: (0, s[jnp.maximum(i - 1, 0)]))

    def whole(x):
        return pl.BlockSpec(x.shape, lambda i, n, b, s, e: (0, 0))

    sums = jax.ShapeDtypeStruct(kt.shape, f32)
    work = pair_units(tiles)
    return pl.pallas_call(
        bwd_kernel,
        name="attn_bwd",
        grid_spec=pltpu.PrefetchScalarGridSpec(
            num_scalar_prefetch=4,
            grid=(steps + 1,),
            in_specs=[
                now(HEAD_DIM),
                now(HEAD_DIM),
                now(HEAD_DIM),
                now(1),
                whole(kt),
                whole(v),
                pl.BlockSpec(memory_space=pl.ANY),
            ],
            out_specs=[prev(HEAD_DIM), whole(sums), whole(sums)],
            scratch_shapes=[
                pltpu.VMEM((2, nk, QT), bf16),
                pltpu.VMEM((2, KC, QT), f32),
                pltpu.VMEM((2, HEAD_DIM, QT), bf16),
                pltpu.VMEM((2, HEAD_DIM, QT), bf16),
                pltpu.VMEM((2, 1, QT), f32),
                pltpu.VMEM((HEAD_DIM, QT), f32),
                pltpu.SemaphoreType.DMA((2,)),
            ],
        ),
        out_shape=[jax.ShapeDtypeStruct((HEAD_DIM, nq), f32), sums, sums],
        compiler_params=pltpu.CompilerParams(vmem_limit_bytes=VMEM),
        cost_estimate=pl.CostEstimate(
            flops=work * 2048, bytes_accessed=work * 2, transcendentals=0
        ),
    )(count, base, which, parity, qt, dot, o, linv, kt, v, p)


def swap(x, axis, distance):
    return lax.ppermute(x, axis, [(i, i ^ distance) for i in range(lax.axis_size(axis))])


def gather_seq(x):
    cycle = lax.axis_size("seq")
    even = [x] + [swap(x, "seq", d) for d in range(2, cycle, 2)]
    odd = [swap(block, "seq", 1) for block in even]
    blocks = []
    for one, two in zip(even, odd):
        blocks += [one, two]
    return jnp.stack(blocks)


def in_order(stack, axis):
    me = lax.axis_index(axis)
    return jnp.take(stack, me ^ lax.iota(jnp.int32, stack.shape[0]), axis=0)


def scatter_sum_seq(x):
    cycle = lax.axis_size("seq")
    me = lax.axis_index("seq")
    halves = x.reshape(cycle // 2, 2, *x.shape[1:])
    mine = lax.dynamic_index_in_dim(halves, me % 2, 1, keepdims=False)
    other = lax.dynamic_index_in_dim(halves, 1 - me % 2, 1, keepdims=False)
    chip = (mine.astype(f32) + swap(other, "seq", 1).astype(f32)).astype(bf16)
    total = lax.dynamic_index_in_dim(chip, me // 2, 0, keepdims=False).astype(f32)
    for d in range(1, cycle // 2):
        part = lax.dynamic_index_in_dim(chip, (me // 2) ^ d, 0, keepdims=False)
        total = total + swap(part, "seq", 2 * d).astype(f32)
    return total


def sum_small(x):
    for axis in ("exp", "seq"):
        d = 1
        while d < lax.axis_size(axis):
            x = x + swap(x, axis, d)
            d *= 2
    return x


def layer_norm(values, gain, shift):
    centre = jnp.mean(values, axis=-1, keepdims=True)
    centered = values - centre
    spread = jnp.mean(centered * centered, axis=-1, keepdims=True)
    return centered * lax.rsqrt(spread + norm_eps) * gain + shift


def own_quarters(x, parity, cycle):
    cut = x.reshape(*x.shape[:-1], cycle, 4, x.shape[-1] // (4 * cycle))
    outer = jnp.concatenate([cut[..., 0:1, :], cut[..., 3:4, :]], axis=-2)
    picked = jnp.where(parity == 0, outer, cut[..., 1:3, :])
    return picked.reshape(*x.shape[:-1], x.shape[-1] // 2)


def to_owners(units, span):
    quarter = span // 4
    one, mid, two = units[:, 0], units[:, 1], units[:, 2]
    outer = jnp.concatenate([mid[..., :quarter], mid[..., 3 * quarter :]], axis=-1)
    inner = mid[..., quarter : 3 * quarter]
    even = jnp.concatenate([one, outer], axis=-1)
    odd = jnp.concatenate([two, inner], axis=-1)
    both = jnp.stack([even, odd], axis=1)
    return both.reshape(both.shape[0] * 2, *both.shape[2:])


def from_owners(got, span):
    quarter = span // 4
    both = got.reshape(got.shape[0] // 2, 2, *got.shape[1:])
    outer, inner = both[:, 0, ..., span:], both[:, 1, ..., span:]
    mid = jnp.concatenate([outer[..., :quarter], inner, outer[..., quarter:]], axis=-1)
    return jnp.stack([both[:, 0, ..., :span], mid, both[:, 1, ..., :span]], axis=1)


def local(
    inputs,
    token_ids,
    hash_table,
    capacity,
    ln1_gain,
    ln1_bias,
    w_qkv,
    q_bias,
    v_bias,
    w_out,
    out_bias,
    ln2_gain,
    ln2_bias,
    up_weight,
    up_bias,
    down_weight,
    down_bias,
    out_grad,
):
    nseq, span, width = inputs.shape
    tokens = nseq * span
    cycle = lax.axis_size("seq")
    nexp = lax.axis_size("exp")
    me = lax.axis_index("seq")
    parity = me % 2
    pair = me // 2
    pairs = cycle // 2
    nk = cycle * span
    assert nseq * HEADS == 3 * pairs

    experts = capacity.shape[0]
    cap = 5 * tokens // (4 * experts)
    expert_of = jnp.take(hash_table, token_ids.reshape(tokens))
    onehot = (expert_of[:, None] == lax.iota(jnp.int32, experts)[None, :]).astype(jnp.int32)
    rank = jnp.sum(onehot * (jnp.cumsum(onehot, axis=0) - 1), axis=1)
    kept = rank < jnp.take(capacity, expert_of)
    slot = jnp.where(kept, expert_of * cap + rank, experts * cap)
    fetch = jnp.minimum(slot, experts * cap - 1)

    def to_experts(rows):
        sent = jnp.zeros((experts * cap, width), bf16).at[slot].set(rows, mode="drop")
        return lax.all_to_all(sent, "exp", split_axis=0, concat_axis=0, tiled=True)

    def from_experts(rows):
        back = lax.all_to_all(rows, "exp", split_axis=0, concat_axis=0, tiled=True)
        return jnp.where(kept[:, None], jnp.take(back, fetch, axis=0).astype(f32), 0.0)

    grad_rows = out_grad.reshape(tokens, width)

    mine = (3 * pair) // HEADS
    stack = gather_seq(inputs)
    blocks = lax.dynamic_index_in_dim(in_order(stack, "seq"), mine, 1, keepdims=False)
    h1 = layer_norm(blocks.reshape(nk, width).astype(f32), ln1_gain, ln1_bias).astype(bf16)

    head_full = (3 * pair + 2 * parity) % HEADS
    head_half = (3 * pair + 1) % HEADS
    w_heads = w_qkv.reshape(width, 3, HEADS, HEAD_DIM)

    def of_head(x, axis):
        return jnp.stack(
            [
                lax.dynamic_index_in_dim(x, head_full, axis, keepdims=False),
                lax.dynamic_index_in_dim(x, head_half, axis, keepdims=False),
            ]
        )

    w_mine = of_head(w_heads, 2)
    qb = of_head(q_bias.reshape(HEADS, HEAD_DIM), 0)
    vb = of_head(v_bias.reshape(HEADS, HEAD_DIM), 0)
    bias = jnp.stack([qb, jnp.zeros_like(qb), vb], axis=1)
    w_rows = w_mine.transpose(0, 2, 3, 1).reshape(6 * HEAD_DIM, width)
    flat = lax.dot_general(w_rows, h1, (((1,), (1,)), ((), ())), preferred_element_type=f32)
    proj = (flat + bias.reshape(6 * HEAD_DIM, 1)).astype(bf16).reshape(2, 3, HEAD_DIM, nk)
    qt = jnp.concatenate([proj[0, 0], own_quarters(proj[1, 0], parity, cycle)], axis=1)
    kt = jnp.concatenate([proj[0, 1], proj[1, 1]], axis=1)
    vt = jnp.concatenate([proj[0, 2], proj[1, 2]], axis=1)
    k, v = kt.T, vt.T
    order = lax.broadcasted_iota(jnp.int32, (1, nk), 1)
    place = jnp.concatenate([order, own_quarters(order, parity, cycle)], axis=1)
    full = [(i, 0, (i * QT + QT + KC - 1) // KC) for i in range(nk // QT)]
    half = [(nk // QT + i, 1, (2 * (i * QT + QT) + KC - 1) // KC) for i in range(nk // (2 * QT))]
    tiles = sorted(full + half, key=lambda t: t[2])
    attn, linv, p = attn_fwd(qt, k, vt, place, tiles, nk)

    def send_home(full_part, half_part):
        rows = full_part.shape[0]
        joined = jnp.concatenate(
            [full_part.reshape(rows, cycle, span), half_part.reshape(rows, cycle, span // 2)],
            axis=2,
        )
        got = lax.all_to_all(
            joined.transpose(1, 0, 2), "seq", split_axis=0, concat_axis=0, tiled=True
        )
        return from_owners(got, span)

    low = attn.astype(bf16)
    attn_low = send_home(low[:, :nk], low[:, nk:]).reshape(nseq, width, span)
    x_rows = inputs.reshape(tokens, width).astype(f32)
    middle = (
        x_rows
        + jnp.einsum("nht,hd->ntd", attn_low, w_out, preferred_element_type=f32).reshape(
            tokens, width
        )
        + out_bias
    )
    normed2, norm2_back = jax.vjp(layer_norm, middle, ln2_gain, ln2_bias)

    dy = to_experts(grad_rows)
    rows = to_experts(normed2.astype(bf16))
    up, down = up_weight[0], down_weight[0]
    z = jnp.dot(rows, up, preferred_element_type=f32) + up_bias[0]
    phi = 0.5 * (1.0 + lax.erf(z * (1.0 / math.sqrt(2.0))))
    hidden = (z * phi).astype(bf16)
    slope = phi + z * jnp.exp(-0.5 * z * z) * (1.0 / math.sqrt(2.0 * math.pi))
    da = lax.dot_general(dy, down, (((1,), (1,)), ((), ())), preferred_element_type=f32)
    dz = (da * slope).astype(bf16)
    dh2 = lax.dot_general(dz, up, (((1,), (1,)), ((), ())), preferred_element_type=f32)
    grad_normed2 = from_experts(dh2.astype(bf16))
    y = jnp.dot(hidden, down, preferred_element_type=f32) + down_bias[0]
    output = (middle + from_experts(y.astype(bf16))).astype(bf16).reshape(nseq, span, width)
    contract0 = (((0,), (0,)), ((), ()))
    grad_up = lax.dot_general(rows, dz, contract0, preferred_element_type=f32).astype(bf16)
    grad_down = lax.dot_general(hidden, dy, contract0, preferred_element_type=f32).astype(bf16)
    grad_up_bias = jnp.sum(dz, axis=0, dtype=f32)
    grad_down_bias = jnp.sum(dy, axis=0, dtype=f32)
    ff = up.shape[1]
    up_sum = scatter_sum_seq(grad_up.reshape(width, cycle, ff // cycle).transpose(1, 0, 2))
    down_sum = scatter_sum_seq(grad_down.reshape(cycle, ff // cycle, width))
    bias_sum = scatter_sum_seq(
        jnp.concatenate(
            [grad_up_bias.reshape(cycle, ff // cycle), grad_down_bias.reshape(cycle, width // cycle)],
            axis=1,
        )
    )

    grad_mid_norm, grad_ln2_gain, grad_ln2_bias = norm2_back(grad_normed2)
    grad_middle = grad_rows.astype(f32) + grad_mid_norm
    grad_branch = grad_middle.astype(bf16)
    branch = grad_branch.reshape(nseq, span, width)
    do_home = jnp.einsum("hd,ntd->nht", w_out, branch, preferred_element_type=f32).astype(bf16)
    sent = to_owners(do_home.reshape(pairs, 3, HEAD_DIM, span), span)
    got = lax.all_to_all(sent, "seq", split_axis=0, concat_axis=0, tiled=True)
    got = got.transpose(1, 0, 2)
    dot = jnp.concatenate(
        [got[..., :span].reshape(HEAD_DIM, nk), got[..., span:].reshape(HEAD_DIM, nk // 2)], axis=1
    )
    dq, dk, dv = attn_bwd(qt, dot, attn, linv, kt, v, p, tiles, nk)
    dk = dk * logit_scale
    both = jnp.stack([dk[:, nk:], dv[:, nk:]])
    other = swap(own_quarters(both, 1 - parity, cycle).astype(bf16), "seq", 1)
    both = own_quarters(both, parity, cycle) + other.astype(f32)
    part_full = jnp.concatenate([dq[:, :nk], dk[:, :nk], dv[:, :nk]], axis=0).astype(bf16)
    part_half = jnp.concatenate([dq[:, nk:], both[0], both[1]], axis=0).astype(bf16)
    units = send_home(part_full, part_half).reshape(nseq, HEADS, 3, HEAD_DIM, span)
    grad_normed = jnp.einsum(
        "nhcet,dche->ntd", units, w_heads, preferred_element_type=f32
    ).reshape(tokens, width)
    bias_grads = jnp.sum(units, axis=(0, 4), dtype=f32)
    grad_q_bias = bias_grads[:, 0].reshape(width)
    grad_v_bias = bias_grads[:, 2].reshape(width)
    _, norm1_back = jax.vjp(layer_norm, x_rows, ln1_gain, ln1_bias)
    grad_from_norm, grad_ln1_gain, grad_ln1_bias = norm1_back(grad_normed)
    input_grad = (grad_middle + grad_from_norm).reshape(nseq, span, width)

    h1_half = own_quarters(h1.T, parity, cycle).T
    grad_full = jnp.dot(part_full, h1, preferred_element_type=f32).astype(bf16)
    grad_half = jnp.dot(part_half, h1_half, preferred_element_type=f32).astype(bf16)
    cut = 3 * HEAD_DIM // 2
    grad_half = grad_half.reshape(2, cut, width)
    own = lax.dynamic_index_in_dim(grad_half, parity, 0, keepdims=False)
    away = lax.dynamic_index_in_dim(grad_half, 1 - parity, 0, keepdims=False)
    own = (own.astype(f32) + swap(away, "seq", 1).astype(f32)).astype(bf16)
    grad_w = jnp.concatenate([grad_full, own], axis=0)
    grad_w_out = lax.dot_general(
        attn_low.transpose(0, 2, 1).reshape(tokens, width),
        grad_branch,
        contract0,
        preferred_element_type=f32,
    )
    grad_w_out = scatter_sum_seq(
        grad_w_out.astype(bf16).reshape(cycle, width // cycle, width)
    ).astype(bf16)
    piece = jnp.concatenate([grad_w, grad_w_out], axis=0)
    count = piece.shape[0]
    spread = lax.all_to_all(piece, "exp", split_axis=0, concat_axis=0, tiled=True)
    summed = jnp.sum(spread.reshape(nexp, count // nexp, width), axis=0, dtype=f32).astype(bf16)
    column = jnp.stack([summed] + [swap(summed, "exp", d) for d in range(1, nexp)])
    column = in_order(column, "exp").reshape(count, width)
    everyone = in_order(gather_seq(column), "seq")
    g_full = everyone[:, : 3 * HEAD_DIM].reshape(pairs, 2, 3 * HEAD_DIM, width)
    g_half = everyone[:, 3 * HEAD_DIM : 3 * HEAD_DIM + cut].reshape(pairs, 3 * HEAD_DIM, width)
    g_units = jnp.stack([g_full[:, 0], g_half, g_full[:, 1]], axis=1)
    g_units = g_units.reshape(nseq, HEADS, 3, HEAD_DIM, width).astype(f32).sum(axis=0)
    grad_w_qkv = g_units.transpose(3, 1, 0, 2).reshape(width, 3 * width)
    grad_w_out = everyone[:, 3 * HEAD_DIM + cut :].reshape(width, width).astype(f32)

    small = sum_small(
        jnp.stack(
            [
                grad_ln1_gain,
                grad_ln1_bias,
                grad_q_bias,
                grad_v_bias,
                jnp.sum(grad_branch, axis=0, dtype=f32),
                grad_ln2_gain,
                grad_ln2_bias,
            ]
        )
    )
    share = ff // cycle
    return (
        output,
        input_grad,
        small[0],
        small[1],
        grad_w_qkv,
        small[2],
        small[3],
        grad_w_out,
        small[4],
        small[5],
        small[6],
        up_sum[None],
        bias_sum[None, :share],
        down_sum[None],
        bias_sum[None, share:],
    )


def solution(mesh):
    in_specs = (
        P("exp", "seq", None),
        P("exp", "seq"),
        P(),
        P(),
        P(),
        P(),
        P(),
        P(),
        P(),
        P(),
        P(),
        P(),
        P(),
        P("exp", None, None),
        P("exp", None),
        P("exp", None, None),
        P("exp", None),
        P("exp", "seq", None),
    )
    out_specs = (
        P("exp", "seq", None),
        P("exp", "seq", None),
        P(),
        P(),
        P(),
        P(),
        P(),
        P(),
        P(),
        P(),
        P(),
        P("exp", None, "seq"),
        P("exp", "seq"),
        P("exp", "seq", None),
        P("exp", "seq"),
    )
    return jax.shard_map(local, mesh=mesh, in_specs=in_specs, out_specs=out_specs, check_vma=False)
```

```python
from functools import partial
import math

import jax
import jax.numpy as jnp
from jax import lax
from jax.experimental import pallas as pl
from jax.experimental.pallas import tpu as pltpu
from jax.sharding import PartitionSpec as P

HEADS = 12
HEAD_DIM = 64
f32 = jnp.float32
bf16 = jnp.bfloat16

norm_eps = 1e-05
logit_scale = 0.125
masked_score = -1e30
LOG2E = math.log2(math.e)

QT = 512
KC = 1024
SUB = 256
SUBF = 512
VMEM = 56 * 2**20


def rows_of(start, size):
    return pl.ds(pl.multiple_of(start, size), size)


def load_tile(ref, kind, t, span):
    nf, nh = QT // span, 2 * QT // span

    def full():
        return jnp.concatenate([ref[t * nf + j, :, :span] for j in range(nf)], axis=-1)

    def half(t):
        return jnp.concatenate([ref[t * nh + j, :, span:] for j in range(nh)], axis=-1)

    if isinstance(kind, int):
        return half(t) if kind else full()
    return jnp.where(kind == 0, full(), half(jnp.minimum(t, ref.shape[0] // nh - 1)))


def tile_places(kind, t, parity, span):
    col = lax.broadcasted_iota(jnp.int32, (1, QT), 1)
    at = t * QT + col
    block = lax.div(at, span // 2)
    j = at - block * (span // 2)
    quarter = span // 4
    outer = jnp.where(j >= quarter, j + 2 * quarter, j)
    half = block * span + jnp.where(parity == 0, outer, j + quarter)
    return jnp.where(kind == 0, at, half)


def loop(low, high, do):
    def step(c, _):
        do(c)
        return 0

    lax.fori_loop(low, high, step, 0)


def fwd_kernel(
    span,
    n_ref,
    kind_ref,
    tile_ref,
    par_ref,
    q_ref,
    k_ref,
    vt_ref,
    o_ref,
    low_ref,
    linv_ref,
    p_hbm,
    s0,
    s1,
    p0,
    p1,
    m0,
    m1,
    acc_scr,
    l_scr,
    sem0,
    sem1,
):
    i = pl.program_id(0)
    last = pl.num_programs(0) - 1
    before = jnp.maximum(i - 1, 0)
    n1 = n_ref[i]
    n2 = n_ref[before]
    unit1 = kind_ref[i]
    unit2 = kind_ref[before]

    def work(c1, c2, masked, now, old, q, place):
        s_now, m_now = now
        s_old, p_old, m_old = old
        if c1 is not None:
            m = m_now[...]
        if c2 is not None:
            top = jnp.max(m_old[...], axis=0, keepdims=True) * (logit_scale * LOG2E)
            l = l_scr[...]
            o = acc_scr[...]
        for j in range(KC // SUBF):
            if c1 is not None:
                off = c1 * KC + j * SUBF
                s = jnp.dot(k_ref[unit1, rows_of(off, SUBF), :], q, preferred_element_type=f32)
                if masked:
                    key = lax.broadcasted_iota(jnp.int32, (SUBF, QT), 0)
                    s = jnp.where(key <= place - off, s, masked_score)
                s_now[rows_of(off, SUBF), :] = s
                m = jnp.maximum(m, jnp.max(s.reshape(SUBF // 8, 8, QT), axis=0))
            if c2 is not None:
                off = c2 * KC + j * SUBF
                s = s_old[rows_of(off, SUBF), :]
                p = jnp.exp2(s * (logit_scale * LOG2E) - top)
                l = l + jnp.sum(p.reshape(SUBF // 8, 8, QT), axis=0)
                low = p.astype(bf16)
                p_old[rows_of(off, SUBF), :] = low
                o = o + jnp.dot(
                    vt_ref[unit2, :, rows_of(off, SUBF)], low, preferred_element_type=f32
                )
        if c1 is not None:
            m_now[...] = m
        if c2 is not None:
            l_scr[...] = l
            acc_scr[...] = o

    def send(c, p_scr, sem):
        part = rows_of(c * KC, KC)
        pltpu.make_async_copy(p_scr.at[part], p_hbm.at[before, part], sem).start()

    def drain(count, p_scr, sem):
        def wait(c):
            part = pl.ds(0, KC)
            pltpu.make_async_copy(p_scr.at[part], p_hbm.at[0, part], sem).wait()

        loop(0, count, wait)

    @pl.when(i >= 1)
    def _():
        l_scr[...] = jnp.zeros_like(l_scr)
        acc_scr[...] = jnp.zeros_like(acc_scr)

    slots = ((s0, p0, m0, sem0), (s1, p1, m1, sem1))
    for turn in (0, 1):
        s_now, p_now, m_now, sem_now = slots[turn]
        s_old, p_old, m_old, sem_old = slots[1 - turn]

        @pl.when(lax.rem(i, 2) == turn)
        def _(s_now=s_now, p_now=p_now, m_now=m_now, sem_now=sem_now, s_old=s_old, p_old=p_old, m_old=m_old, sem_old=sem_old, turn=turn):
            q = load_tile(q_ref, unit1, tile_ref[i], span)
            place = tile_places(unit1, tile_ref[i], par_ref[0], span)
            m_now[...] = jnp.full((8, QT), -jnp.inf, f32)

            @pl.when(i >= 3)
            def _():
                drain(n_ref[jnp.maximum(i - 3, 0)], p_old, sem_old)

            def go(c1, c2, masked=False):
                work(c1, c2, masked, (s_now, m_now), (s_old, p_old, m_old), q, place)

            if turn == 0:

                @pl.when(i == 0)
                def _():
                    loop(0, n1, lambda c: go(c, None, True))

            @pl.when(jnp.logical_and(i > 0, i < last))
            def _():
                go(n1 - 1, n2 - 1, True)
                send(n2 - 1, p_old, sem_old)
                both = jnp.minimum(n1, n2) - 1

                def step(c):
                    go(c, c)
                    send(c, p_old, sem_old)

                loop(0, both, step)
                loop(both, n1 - 1, lambda c: go(c, None))

            @pl.when(i == last)
            def _():
                def step(c):
                    go(None, c)
                    send(c, p_old, sem_old)

                loop(0, n2, step)
                drain(n_ref[jnp.maximum(i - 2, 0)], p_now, sem_now)
                drain(n2, p_old, sem_old)

    @pl.when(i > 0)
    def _():
        linv = 1.0 / jnp.sum(l_scr[...], axis=0, keepdims=True)
        o = acc_scr[...] * linv
        t = tile_ref[before]
        nf, nh = QT // span, 2 * QT // span
        for count, width, start, unit in ((nf, span, 0, 0), (nh, span // 2, span, 1)):

            @pl.when(unit2 == unit)
            def _(count=count, width=width, start=start):
                for j in range(count):
                    here = slice(j * width, (j + 1) * width)
                    there = pl.ds(start, width)
                    o_ref[t * count + j, :, there] = o[:, here]
                    low_ref[t * count + j, :, there] = o[:, here].astype(bf16)
                    linv_ref[t * count + j, :, there] = linv[:, here]


def table(values):
    return jnp.array(values, jnp.int32)


def pair_units(tiles):
    return sum(t[2] for t in tiles) * KC * QT


def whole(x):
    zeros = (0,) * len(x.shape)
    return pl.BlockSpec(x.shape, lambda *_: zeros)


def attn_fwd(q, k, vt, parity, tiles, span):
    nk = k.shape[1]
    steps = len(tiles)
    listed = tiles + [(tiles[-1][0], tiles[-1][1], 0)]
    linv = jax.ShapeDtypeStruct((q.shape[0], 1, q.shape[2]), f32)
    o = jax.ShapeDtypeStruct(q.shape, f32)
    work = pair_units(tiles)
    return pl.pallas_call(
        partial(fwd_kernel, span),
        name="attn_fwd",
        grid_spec=pltpu.PrefetchScalarGridSpec(
            num_scalar_prefetch=4,
            grid=(steps + 1,),
            in_specs=[whole(q), whole(k), whole(vt)],
            out_specs=[whole(q), whole(q), whole(linv), pl.BlockSpec(memory_space=pl.ANY)],
            scratch_shapes=[
                pltpu.VMEM((nk, QT), f32),
                pltpu.VMEM((nk, QT), f32),
                pltpu.VMEM((nk, QT), bf16),
                pltpu.VMEM((nk, QT), bf16),
                pltpu.VMEM((8, QT), f32),
                pltpu.VMEM((8, QT), f32),
                pltpu.VMEM((HEAD_DIM, QT), f32),
                pltpu.VMEM((8, QT), f32),
                pltpu.SemaphoreType.DMA,
                pltpu.SemaphoreType.DMA,
            ],
        ),
        out_shape=[
            o,
            jax.ShapeDtypeStruct(q.shape, bf16),
            linv,
            jax.ShapeDtypeStruct((steps, nk, QT), bf16),
        ],
        compiler_params=pltpu.CompilerParams(vmem_limit_bytes=VMEM),
        cost_estimate=pl.CostEstimate(
            flops=work * 1024, bytes_accessed=work * 2, transcendentals=work
        ),
    )(
        table([t[2] for t in listed]),
        table([t[0] for t in listed]),
        table([t[1] for t in listed]),
        parity.reshape(1),
        q,
        k,
        vt,
    )


def bwd_kernel(
    unit,
    span,
    n_ref,
    tile_ref,
    slot_ref,
    turn_ref,
    par_ref,
    q_ref,
    do_ref,
    o_ref,
    linv_ref,
    kt_ref,
    v_ref,
    p_hbm,
    *refs,
):
    outs = refs[:-10]
    p_scr, dp0, dp1, q_scr, do_scr, de_scr, dq_scr, dk_scr, dv_scr, sem = refs[-10:]
    dps = (dp0, dp1)
    i = pl.program_id(0)
    last = pl.num_programs(0) - 1
    a = lax.rem(i, 2)
    b = 1 - a
    before = jnp.maximum(i - 1, 0)
    n1 = n_ref[i]
    n2 = n_ref[before]
    turn1 = turn_ref[i]
    turn2 = turn_ref[before]
    devices = kt_ref.shape[2] // span

    def fetch(t, slot):
        def start(c):
            part = rows_of(c * KC, KC)
            pltpu.make_async_copy(
                p_hbm.at[slot_ref[t], part], p_scr.at[slot, part], sem.at[slot]
            ).start()

        loop(0, n_ref[t], start)

    def work(c1, dp_now, c2, slot, dp_old):
        if c1 is not None:
            do_now = do_scr[a]
        if c2 is not None:
            qt = q_scr[slot]
            dot = do_scr[slot]
            delta = de_scr[slot]
            dq = dq_scr[...]
        for j in range(KC // SUB):
            here = pl.ds(j * SUB, SUB)
            if c1 is not None:
                dp_now[here, :] = jnp.dot(
                    v_ref[unit, rows_of(c1 * KC + j * SUB, SUB), :],
                    do_now,
                    preferred_element_type=f32,
                )
            if c2 is not None:
                keys = rows_of(c2 * KC + j * SUB, SUB)
                p = p_scr[slot, keys, :]
                ds = (p.astype(f32) * (dp_old[here, :] - delta)).astype(bf16)
                dv_scr[:, keys] += lax.dot_general(
                    dot, p, (((1,), (1,)), ((), ())), preferred_element_type=f32
                )
                dk_scr[:, keys] += lax.dot_general(
                    qt, ds, (((1,), (1,)), ((), ())), preferred_element_type=f32
                )
                dq = dq + jnp.dot(kt_ref[unit, :, keys], ds, preferred_element_type=f32)
        if c2 is not None:
            dq_scr[...] = dq

    def by_turn(turn, do):
        for t in (0, 1):

            @pl.when(lax.rem(turn, 2) == t)
            def _(t=t):
                do(dps[t], dps[1 - t])

    def load():
        t = tile_ref[i]
        scaled = load_tile(do_ref, unit, t, span).astype(f32) * load_tile(linv_ref, unit, t, span)
        de_scr[a] = jnp.sum(scaled * load_tile(o_ref, unit, t, span), axis=0, keepdims=True)
        do_scr[a] = scaled.astype(bf16)
        q_scr[a] = load_tile(q_ref, unit, t, span)

    @pl.when(i == 0)
    def _():
        dk_scr[...] = jnp.zeros_like(dk_scr)
        dv_scr[...] = jnp.zeros_like(dv_scr)
        dq_scr[...] = jnp.zeros_like(dq_scr)
        fetch(0, 0)
        load()
        work(0, dps[0], None, None, None)

    @pl.when(jnp.logical_and(i > 0, i < last))
    def _():
        load()

        def step(now, other):
            work(0, now, n2 - 1, b, other)

        by_turn(turn1, step)

    @pl.when(i == last)
    def _():
        by_turn(n2 - 1 + turn2, lambda now, other: work(None, None, n2 - 1, b, now))

    @pl.when(i > 0)
    def _():
        dq = (dq_scr[...] * logit_scale).astype(bf16)
        t = tile_ref[before]
        width = span // 2 if unit else span
        count = QT // width
        for j in range(count):
            outs[0][t * count + j, :HEAD_DIM, :] = dq[:, j * width : (j + 1) * width]
        dq_scr[...] = jnp.zeros_like(dq_scr)

    @pl.when(i < last)
    def _():
        def wait(c):
            part = pl.ds(0, KC)
            pltpu.make_async_copy(p_hbm.at[0, part], p_scr.at[a, part], sem.at[a]).wait()

        loop(0, n1, wait)

        @pl.when(i + 1 < last)
        def _():
            fetch(i + 1, b)

        def step(c):
            def both(now, other):
                work(c + 1, other, c, a, now)

            by_turn(c + turn1, both)

        loop(0, n1 - 1, step)

    @pl.when(i == last)
    def _():
        quarter = span // 4
        for d in range(devices):
            keys = pl.ds(d * span, span)
            dk = dk_scr[:, keys] * logit_scale
            dv = dv_scr[:, keys]
            if not unit:
                outs[0][d, HEAD_DIM : 2 * HEAD_DIM, :] = dk.astype(bf16)
                outs[0][d, 2 * HEAD_DIM :, :] = dv.astype(bf16)
            else:
                both = jnp.concatenate([dk, dv], axis=0)
                outer = jnp.concatenate([both[:, :quarter], both[:, 3 * quarter :]], axis=1)
                inner = both[:, quarter : 3 * quarter]
                even = par_ref[0] == 0
                outs[1][d] = jnp.where(even, outer, inner)
                outs[2][d] = jnp.where(even, inner, outer).astype(bf16)


def attn_bwd(unit, q, do, o, linv, kt, v, p, parity, tiles, slots, span):
    nk = kt.shape[2]
    steps = len(tiles)
    listed = tiles + [(unit, tiles[-1][1], 0)]
    turns = [0]
    for t in tiles:
        turns.append((turns[-1] + t[2]) % 2)
    devices = nk // span
    if unit:
        outs = [
            jax.ShapeDtypeStruct((devices, HEAD_DIM, span // 2), bf16),
            jax.ShapeDtypeStruct((devices, 2 * HEAD_DIM, span // 2), f32),
            jax.ShapeDtypeStruct((devices, 2 * HEAD_DIM, span // 2), bf16),
        ]
    else:
        outs = [jax.ShapeDtypeStruct((devices, 3 * HEAD_DIM, span), bf16)]
    work = pair_units(tiles)
    return pl.pallas_call(
        partial(bwd_kernel, unit, span),
        name="attn_bwd_half" if unit else "attn_bwd_full",
        grid_spec=pltpu.PrefetchScalarGridSpec(
            num_scalar_prefetch=5,
            grid=(steps + 1,),
            in_specs=[
                whole(q),
                whole(do),
                whole(o),
                whole(linv),
                whole(kt),
                whole(v),
                pl.BlockSpec(memory_space=pl.ANY),
            ],
            out_specs=[whole(x) for x in outs],
            scratch_shapes=[
                pltpu.VMEM((2, nk, QT), bf16),
                pltpu.VMEM((KC, QT), f32),
                pltpu.VMEM((KC, QT), f32),
                pltpu.VMEM((2, HEAD_DIM, QT), bf16),
                pltpu.VMEM((2, HEAD_DIM, QT), bf16),
                pltpu.VMEM((2, 1, QT), f32),
                pltpu.VMEM((HEAD_DIM, QT), f32),
                pltpu.VMEM((HEAD_DIM, nk), f32),
                pltpu.VMEM((HEAD_DIM, nk), f32),
                pltpu.SemaphoreType.DMA((2,)),
            ],
        ),
        out_shape=outs,
        compiler_params=pltpu.CompilerParams(vmem_limit_bytes=VMEM),
        cost_estimate=pl.CostEstimate(
            flops=work * 2048, bytes_accessed=work * 2, transcendentals=0
        ),
    )(
        table([t[2] for t in listed]),
        table([t[1] for t in listed]),
        table(slots + [slots[-1]]),
        table(turns),
        parity.reshape(1),
        q,
        do,
        o,
        linv,
        kt,
        v,
        p,
    )


def pick_quarters(x, parity, axis):
    q = x.shape[axis] // 4

    def cut(low, high):
        return x[low * q : high * q] if axis == 0 else x[:, low * q : high * q]

    outer = jnp.concatenate([cut(0, 1), cut(3, 4)], axis=axis)
    return jnp.where(parity == 0, outer, cut(1, 3))


def prep_kernel(count, pos_ref, par_ref, *refs):
    blocks = refs[:count]
    gain_ref, shift_ref, wt_ref, bt_ref, wn_ref, bn_ref = refs[count : count + 6]
    h_ref, q_ref, kt_ref, vt_ref, k_ref, v_ref, x_scr = refs[count + 6 :]
    i = pl.program_id(0)
    for j in range(count):

        @pl.when(i == j)
        def _(j=j):
            x_scr[...] = blocks[j][...].astype(f32)

    x = x_scr[...]
    span = x.shape[0]
    x = x - jnp.mean(x, axis=-1, keepdims=True)
    spread = jnp.mean(x * x, axis=-1, keepdims=True)
    h = (x * lax.rsqrt(spread + norm_eps) * gain_ref[...] + shift_ref[...]).astype(bf16)
    h_ref[...] = h
    over = lax.dot_general(
        wt_ref[...], h, (((1,), (1,)), ((), ())), preferred_element_type=f32
    )
    over = (over + bt_ref[...]).astype(bf16)
    d = HEAD_DIM
    q_ref[0, :, :span] = over[:d]
    q_ref[0, :, span:] = pick_quarters(over[3 * d : 4 * d], par_ref[0], 1)
    for unit in (0, 1):
        kt_ref[unit] = over[(3 * unit + 1) * d : (3 * unit + 2) * d]
        vt_ref[unit] = over[(3 * unit + 2) * d : (3 * unit + 3) * d]
    flat = (jnp.dot(h, wn_ref[...], preferred_element_type=f32) + bn_ref[...]).astype(bf16)
    for unit in (0, 1):
        k_ref[unit] = flat[:, 2 * unit * d : (2 * unit + 1) * d]
        v_ref[unit] = flat[:, (2 * unit + 1) * d : (2 * unit + 2) * d]


def prep(blocks, pos, parity, gain, shift, wt, bt, wn, bn):
    count = len(blocks)
    span, width = blocks[0].shape
    devices = lax.axis_size("seq")
    nk = devices * span
    d = HEAD_DIM
    shapes = [
        ((nk, width), (span, width), lambda i, s, _: (s[i], 0)),
        ((devices, d, 3 * span // 2), (1, d, 3 * span // 2), lambda i, s, _: (s[i], 0, 0)),
        ((2, d, nk), (2, d, span), lambda i, s, _: (0, 0, s[i])),
        ((2, d, nk), (2, d, span), lambda i, s, _: (0, 0, s[i])),
        ((2, nk, d), (2, span, d), lambda i, s, _: (0, s[i], 0)),
        ((2, nk, d), (2, span, d), lambda i, s, _: (0, s[i], 0)),
    ]
    params = (gain, shift, wt, bt, wn, bn)
    return pl.pallas_call(
        partial(prep_kernel, count),
        name="prep",
        grid_spec=pltpu.PrefetchScalarGridSpec(
            num_scalar_prefetch=2,
            grid=(count,),
            in_specs=[whole(b) for b in blocks]
            + [whole(x) for x in params],
            out_specs=[pl.BlockSpec(block, index) for _, block, index in shapes],
            scratch_shapes=[pltpu.VMEM((span, width), f32)],
        ),
        out_shape=[jax.ShapeDtypeStruct(shape, bf16) for shape, _, _ in shapes],
        compiler_params=pltpu.CompilerParams(vmem_limit_bytes=VMEM),
        cost_estimate=pl.CostEstimate(
            flops=count * span * width * 640 * 2,
            bytes_accessed=count * span * width * 4,
            transcendentals=count * span,
        ),
    )(pos, parity.reshape(1), *blocks, *params)


def pull_kernel(
    back_ref, pick_ref, grad_ref, mid_ref, gain_ref, w_ref, gm_ref, br_ref, do_ref, small_ref
):
    dh = jnp.dot(pick_ref[...], back_ref[...], preferred_element_type=f32)
    x = mid_ref[...]
    x = x - jnp.mean(x, axis=-1, keepdims=True)
    inv = lax.rsqrt(jnp.mean(x * x, axis=-1, keepdims=True) + norm_eps)
    x = x * inv
    d = dh * gain_ref[...]
    dx = inv * (
        d - jnp.mean(d, axis=-1, keepdims=True) - x * jnp.mean(d * x, axis=-1, keepdims=True)
    )
    gm = grad_ref[...].astype(f32) + dx
    branch = gm.astype(bf16)
    gm_ref[...] = gm
    br_ref[...] = branch
    small_ref[0:1] = jnp.sum(branch.astype(f32), axis=0, keepdims=True)
    small_ref[1:2] = jnp.sum(dh * x, axis=0, keepdims=True)
    small_ref[2:3] = jnp.sum(dh, axis=0, keepdims=True)
    do_ref[...] = lax.dot_general(
        w_ref[...], branch, (((1,), (1,)), ((), ())), preferred_element_type=f32
    ).astype(bf16)


def pull(back, pick, grad, mid, gain, w_out):
    tokens, width = grad.shape
    return pl.pallas_call(
        pull_kernel,
        name="pull",
        out_shape=[
            jax.ShapeDtypeStruct((tokens, width), f32),
            jax.ShapeDtypeStruct((tokens, width), bf16),
            jax.ShapeDtypeStruct((w_out.shape[0], tokens), bf16),
            jax.ShapeDtypeStruct((3, width), f32),
        ],
        compiler_params=pltpu.CompilerParams(vmem_limit_bytes=VMEM),
        cost_estimate=pl.CostEstimate(
            flops=4 * tokens * width * width, bytes_accessed=tokens * width * 16, transcendentals=0
        ),
    )(back, pick, grad, mid, gain, w_out)


def weight_kernel(half, par_ref, part_ref, h_ref, g_ref):
    i = pl.program_id(0)
    devices, rows, tokens = part_ref.shape
    stretch = h_ref.shape[0] // devices
    width = h_ref.shape[1]
    g = jnp.zeros((rows, width), f32)
    count = jnp.zeros((16, rows), f32)
    ones = jnp.ones((16, tokens), bf16)
    for d in range(devices):
        h = h_ref[pl.ds(d * stretch, stretch), :]
        if half:
            h = pick_quarters(h, par_ref[0], 0)
        part = part_ref[d]
        g += jnp.dot(part, h, preferred_element_type=f32)
        count += lax.dot_general(
            ones, part, (((1,), (1,)), ((), ())), preferred_element_type=f32
        )
    count = jnp.concatenate([count, jnp.zeros((16, width - rows), f32)], axis=1)

    @pl.when(i == 0)
    def _():
        g_ref[:rows] = g
        g_ref[rows:] = count

    @pl.when(i > 0)
    def _():
        g_ref[:rows] += g
        g_ref[rows:] += count


def head_weights(part, h1, parity, half):
    devices, rows, _ = part.shape
    nk, width = h1.shape
    steps = 4
    return pl.pallas_call(
        partial(weight_kernel, half),
        name="head_weights",
        grid_spec=pltpu.PrefetchScalarGridSpec(
            num_scalar_prefetch=1,
            grid=(steps,),
            in_specs=[
                pl.BlockSpec((devices // steps, *part.shape[1:]), lambda i, _: (i, 0, 0)),
                pl.BlockSpec((nk // steps, width), lambda i, _: (i, 0)),
            ],
            out_specs=pl.BlockSpec((rows + 16, width), lambda i, _: (0, 0)),
        ),
        out_shape=jax.ShapeDtypeStruct((rows + 16, width), f32),
        compiler_params=pltpu.CompilerParams(vmem_limit_bytes=VMEM),
        cost_estimate=pl.CostEstimate(
            flops=2 * nk * rows * width, bytes_accessed=nk * width * 2, transcendentals=0
        ),
    )(parity.reshape(1), part, h1)


def pack_kernel(at_ref, part_ref, h_ref, keep_ref, out_ref, sums_ref, piece_ref, acc, cnt):
    i = pl.program_id(0)
    devices, rows, tokens = part_ref.shape
    stretch, width = h_ref.shape[0] // devices, h_ref.shape[1]
    g = jnp.zeros((rows, width), f32)
    count = jnp.zeros((16, rows), f32)
    ones = jnp.ones((16, tokens), bf16)
    for d in range(devices):
        part = part_ref[d]
        g += jnp.dot(part, h_ref[pl.ds(d * stretch, stretch), :], preferred_element_type=f32)
        count += lax.dot_general(
            ones, part, (((1,), (1,)), ((), ())), preferred_element_type=f32
        )

    @pl.when(i == 0)
    def _():
        acc[...] = g
        cnt[...] = count

    @pl.when(i > 0)
    def _():
        acc[...] += g
        cnt[...] += count

    @pl.when(i == pl.num_programs(0) - 1)
    def _():
        nexp, share, _ = piece_ref.shape
        line = jnp.concatenate(
            [cnt[...], sums_ref[...], jnp.zeros((16, width - 2 * rows), f32)], axis=1
        ).astype(bf16)
        filled = rows + keep_ref.shape[0] + out_ref.shape[0] + 16
        piece = jnp.concatenate(
            [
                acc[...].astype(bf16),
                keep_ref[...],
                out_ref[...],
                line,
                jnp.zeros((nexp * share - filled, width), bf16),
            ],
            axis=0,
        )
        for e in range(nexp):
            piece_ref[at_ref[0] ^ e] = piece[e * share : (e + 1) * share]


def pack(part, h1, keep, w_out_part, half_sums):
    devices, rows, _ = part.shape
    nk, width = h1.shape
    nexp = lax.axis_size("exp")
    filled = rows + keep.shape[0] + w_out_part.shape[0] + 16
    share = -(-filled // (16 * nexp)) * 16
    steps = 4
    return pl.pallas_call(
        pack_kernel,
        name="pack",
        grid_spec=pltpu.PrefetchScalarGridSpec(
            num_scalar_prefetch=1,
            grid=(steps,),
            in_specs=[
                pl.BlockSpec((devices // steps, *part.shape[1:]), lambda i, _: (i, 0, 0)),
                pl.BlockSpec((nk // steps, width), lambda i, _: (i, 0)),
                whole(keep),
                whole(w_out_part),
                whole(half_sums),
            ],
            out_specs=pl.BlockSpec((nexp, share, width), lambda i, _: (0, 0, 0)),
            scratch_shapes=[pltpu.VMEM((rows, width), f32), pltpu.VMEM((16, rows), f32)],
        ),
        out_shape=jax.ShapeDtypeStruct((nexp, share, width), bf16),
        compiler_params=pltpu.CompilerParams(vmem_limit_bytes=VMEM),
        cost_estimate=pl.CostEstimate(
            flops=2 * nk * rows * width, bytes_accessed=nk * width * 2, transcendentals=0
        ),
    )(lax.axis_index("exp").reshape(1), part, h1, keep, w_out_part, half_sums)


def home_kernel(nseq, span, full_ref, half_ref, w_ref, x_ref, gain_ref, gm_ref, dx_ref, u_scr):
    pairs = full_ref.shape[0] // 2
    quarter = span // 4
    for n in range(nseq):
        here = pairs // nseq
        for j in range(here):
            p = n * here + j
            outer, inner = half_ref[2 * p], half_ref[2 * p + 1]
            mid = jnp.concatenate([outer[:, :quarter], inner, outer[:, quarter:]], axis=1)
            for role, unit in enumerate((full_ref[2 * p], mid, full_ref[2 * p + 1])):
                for c in range(3):
                    at = c * HEADS + 3 * j + role
                    u_scr[pl.ds(at * HEAD_DIM, HEAD_DIM), :] = unit[
                        c * HEAD_DIM : (c + 1) * HEAD_DIM
                    ]
        dh = jnp.dot(w_ref[...], u_scr[...], preferred_element_type=f32).T
        x = x_ref[n].astype(f32)
        x = x - jnp.mean(x, axis=-1, keepdims=True)
        inv = lax.rsqrt(jnp.mean(x * x, axis=-1, keepdims=True) + norm_eps)
        x = x * inv
        d = dh * gain_ref[...]
        dx_ref[n] = gm_ref[n] + inv * (
            d - jnp.mean(d, axis=-1, keepdims=True) - x * jnp.mean(d * x, axis=-1, keepdims=True)
        )


def home(full, half, w_qkv, x, gain, grad_middle):
    nseq, span, width = x.shape
    return pl.pallas_call(
        partial(home_kernel, nseq, span),
        name="home",
        out_shape=jax.ShapeDtypeStruct((nseq, span, width), f32),
        scratch_shapes=[pltpu.VMEM((3 * width, span), bf16)],
        compiler_params=pltpu.CompilerParams(vmem_limit_bytes=VMEM),
        cost_estimate=pl.CostEstimate(
            flops=6 * nseq * span * width * width,
            bytes_accessed=nseq * span * width * 16,
            transcendentals=0,
        ),
    )(full, half, w_qkv, x, gain, grad_middle)


def build_kernel(nseq, nexp, at_ref, *refs):
    blocks = refs[: -11]
    w_ref, gain_ref, shift_ref, g_ref, b_ref, ln_ref, out_ref, small_ref, got, acc, sem = refs[-11:]
    devices = len(blocks)
    me, z = at_ref[0], at_ref[1]
    d = HEAD_DIM
    rows = 3 * d
    cut = rows // 2
    width = g_ref.shape[0]
    share = got.shape[1] // nexp
    for j in range(devices):
        for e in range(nexp):
            pltpu.make_async_copy(
                blocks[j].at[pl.ds(pl.multiple_of((z ^ e) * share, 16), share)],
                got.at[j, pl.ds(e * share, share)],
                sem,
            ).start()
    acc[...] = jnp.zeros_like(acc)
    pltpu.make_async_copy(got, got, sem).wait()
    out_rows = width // devices
    line = rows + cut + out_rows + 16

    def unit_rows(u, c):
        p, role = u // 3, u % 3
        if role != 1:
            return got[me ^ (2 * p + role // 2), pl.ds(c * d, d), :].astype(f32)
        parts = []
        low, high = c * d, (c + 1) * d
        for core in (0, 1):
            a, b = max(low, core * cut), min(high, (core + 1) * cut)
            if a < b:
                parts.append(got[me ^ (2 * p + core), pl.ds(rows + a - core * cut, b - a), :])
        return jnp.concatenate([part.astype(f32) for part in parts], axis=0)

    def unit_sums(u, c):
        p, role = u // 3, u % 3
        here = pl.ds(line, 16)
        if role != 1:
            return got[me ^ (2 * p + role // 2), here, pl.ds(c * d, d)].astype(f32)
        at = pl.ds(rows + c * d, d)
        return sum(got[me ^ (2 * p + core), here, at].astype(f32) for core in (0, 1))

    for c in range(3):
        for two in range(HEADS // 2):
            heads = (2 * two, 2 * two + 1)
            grads = [sum(unit_rows(n * HEADS + h, c) for n in range(nseq)) for h in heads]
            sums = [sum(unit_sums(n * HEADS + h, c) for n in range(nseq)) for h in heads]
            at = pl.ds(c * width + two * 2 * d, 2 * d)
            block = jnp.concatenate(grads, axis=0).T
            total = jnp.concatenate(sums, axis=1)
            g_ref[:, at] = block
            b_ref[:, at] = total[:8]
            w = w_ref[:, at].astype(f32)
            acc[0] += w * block
            acc[1] += w * total[:1]
    gained = jnp.sum(acc[0].T, axis=0, keepdims=True)
    shifted = jnp.sum(acc[1].T, axis=0, keepdims=True)
    ln_ref[0:1] = (gained - shift_ref[...] * shifted) / gain_ref[...]
    ln_ref[1:2] = shifted
    for i in range(devices):
        out_ref[pl.ds(i * out_rows, out_rows), :] = got[
            me ^ i, pl.ds(rows + cut, out_rows), :
        ].astype(f32)
    small_ref[...] = got[0, pl.ds(rows + cut + out_rows, 16), :].astype(f32)


def build(blocks, w_qkv, gain, shift, nseq):
    count, width = blocks[0].shape
    nexp = lax.axis_size("exp")
    at = jnp.stack([lax.axis_index("seq"), lax.axis_index("exp")])
    vmem = pl.BlockSpec(memory_space=pltpu.VMEM)
    away = pl.BlockSpec(memory_space=pl.ANY)
    return pl.pallas_call(
        partial(build_kernel, nseq, nexp),
        name="build",
        in_specs=[pl.BlockSpec(memory_space=pltpu.SMEM)] + [away] * len(blocks) + [vmem] * 3,
        out_shape=[
            jax.ShapeDtypeStruct((width, 3 * width), f32),
            jax.ShapeDtypeStruct((8, 3 * width), f32),
            jax.ShapeDtypeStruct((2, width), f32),
            jax.ShapeDtypeStruct((width, width), f32),
            jax.ShapeDtypeStruct((16, width), f32),
        ],
        scratch_shapes=[
            pltpu.VMEM((len(blocks), count, width), bf16),
            pltpu.VMEM((2, width, 2 * HEAD_DIM), f32),
            pltpu.SemaphoreType.DMA,
        ],
        compiler_params=pltpu.CompilerParams(vmem_limit_bytes=VMEM),
        cost_estimate=pl.CostEstimate(
            flops=0, bytes_accessed=18 * width * width, transcendentals=0
        ),
    )(at, *blocks, w_qkv, gain, shift)


def expert_sums_kernel(rows_ref, dy_ref, dz_ref, hid_ref, out_ref):
    contract = (((0,), (0,)), ((), ()))
    dz = dz_ref[...]
    share = dz.shape[1]
    dy = dy_ref[...]
    out_ref[0, :share] = lax.dot_general(
        dz, rows_ref[...], contract, preferred_element_type=f32
    ).astype(bf16)
    out_ref[0, share : 2 * share] = lax.dot_general(
        hid_ref[...], dy, contract, preferred_element_type=f32
    ).astype(bf16)
    ones = jnp.ones((16, dz.shape[0]), bf16)
    up = jnp.dot(ones, dz, preferred_element_type=f32).astype(bf16)
    fill = jnp.zeros((16, dy.shape[1] - share), bf16)
    out_ref[0, 2 * share : 2 * share + 16] = jnp.concatenate([up, fill], axis=1)
    out_ref[0, 2 * share + 16 :] = jnp.dot(ones, dy, preferred_element_type=f32).astype(bf16)


def expert_sums(rows, dy, dz, hidden):
    devices = lax.axis_size("seq")
    count, width = rows.shape
    ff = dz.shape[1]
    share = ff // devices
    if share % 128:
        contract = (((0,), (0,)), ((), ()))
        up = lax.dot_general(dz, rows, contract, preferred_element_type=f32)
        down = lax.dot_general(hidden, dy, contract, preferred_element_type=f32)
        up_bias = jnp.pad(
            jnp.sum(dz, axis=0, dtype=f32).reshape(devices, 1, share),
            ((0, 0), (0, 15), (0, width - share)),
        )
        down_bias = jnp.broadcast_to(jnp.sum(dy, axis=0, dtype=f32), (devices, 16, width))
        return jnp.concatenate(
            [up.reshape(devices, share, width), down.reshape(devices, share, width), up_bias, down_bias],
            axis=1,
        ).astype(bf16)
    total = 2 * share + 32
    return pl.pallas_call(
        expert_sums_kernel,
        name="expert_sums",
        grid=(devices,),
        in_specs=[
            pl.BlockSpec((count, width), lambda j: (0, 0)),
            pl.BlockSpec((count, width), lambda j: (0, 0)),
            pl.BlockSpec((count, share), lambda j: (0, j)),
            pl.BlockSpec((count, share), lambda j: (0, j)),
        ],
        out_specs=pl.BlockSpec((1, total, width), lambda j: (j, 0, 0)),
        out_shape=jax.ShapeDtypeStruct((devices, total, width), bf16),
        compiler_params=pltpu.CompilerParams(vmem_limit_bytes=VMEM),
        cost_estimate=pl.CostEstimate(
            flops=1, bytes_accessed=1, transcendentals=0
        ),
    )(rows, dy, dz, hidden)


def swap(x, axis, distance):
    return lax.ppermute(x, axis, [(i, i ^ distance) for i in range(lax.axis_size(axis))])


def gather_chips(x):
    chips = lax.axis_size("seq") // 2
    if chips != 4:
        return [x] + [swap(x, "seq", 2 * d) for d in range(1, chips)]
    one, two = swap(x, "seq", 2), swap(x, "seq", 4)
    axis = x.ndim - 2
    half = x.shape[axis] // 2
    low = swap(lax.slice_in_dim(one, 0, half, axis=axis), "seq", 4)
    high = swap(lax.slice_in_dim(two, half, 2 * half, axis=axis), "seq", 2)
    return [x, one, two, jnp.concatenate([low, high], axis=axis)]


def gather_seq(x):
    blocks = []
    for block in gather_chips(x):
        blocks += [block, swap(block, "seq", 1)]
    return blocks


def in_order(stack, axis):
    me = lax.axis_index(axis)
    return jnp.take(stack, me ^ lax.iota(jnp.int32, stack.shape[0]), axis=0)


def sum_exp(parts):
    nexp = parts.shape[0]
    total = parts[0].astype(f32)
    for d in range(1, nexp):
        total = total + swap(parts[d], "exp", d).astype(f32)
    total = total.astype(bf16)
    return jnp.concatenate([total] + [swap(total, "exp", d) for d in range(1, nexp)])


def layer_norm(values, gain, shift):
    centre = jnp.mean(values, axis=-1, keepdims=True)
    centered = values - centre
    spread = jnp.mean(centered * centered, axis=-1, keepdims=True)
    return centered * lax.rsqrt(spread + norm_eps) * gain + shift


def to_owners(units, span):
    quarter = span // 4
    one, mid, two = units[:, 0], units[:, 1], units[:, 2]
    outer = jnp.concatenate([mid[..., :quarter], mid[..., 3 * quarter :]], axis=-1)
    inner = mid[..., quarter : 3 * quarter]
    even = jnp.concatenate([one, outer], axis=-1)
    odd = jnp.concatenate([two, inner], axis=-1)
    both = jnp.stack([even, odd], axis=1)
    return both.reshape(both.shape[0] * 2, *both.shape[2:])


def from_owners(got, span):
    quarter = span // 4
    both = got.reshape(got.shape[0] // 2, 2, *got.shape[1:])
    outer, inner = both[:, 0, ..., span:], both[:, 1, ..., span:]
    mid = jnp.concatenate([outer[..., :quarter], inner, outer[..., quarter:]], axis=-1)
    return jnp.stack([both[:, 0, ..., :span], mid, both[:, 1, ..., :span]], axis=1)


def exchange(x, axis):
    return lax.all_to_all(x, axis, split_axis=0, concat_axis=0, tiled=True)


def exchange_exp(x):
    nexp = lax.axis_size("exp")
    parts = x.reshape(nexp, x.shape[0] // nexp, x.shape[1])
    return jnp.concatenate([parts[0]] + [swap(parts[d], "exp", d) for d in range(1, nexp)])


def local(
    inputs,
    token_ids,
    hash_table,
    capacity,
    ln1_gain,
    ln1_bias,
    w_qkv,
    q_bias,
    v_bias,
    w_out,
    out_bias,
    ln2_gain,
    ln2_bias,
    up_weight,
    up_bias,
    down_weight,
    down_bias,
    out_grad,
):
    nseq, span, width = inputs.shape
    tokens = nseq * span
    cycle = lax.axis_size("seq")
    me = lax.axis_index("seq")
    parity = me % 2
    pair = me // 2
    pairs = cycle // 2
    nk = cycle * span
    assert nseq * HEADS == 3 * pairs
    up, down = up_weight[0], down_weight[0]
    ff = up.shape[1]
    share = ff // cycle
    row = lambda x: x.reshape(1, -1)

    mine = (3 * pair) // HEADS
    def of_sequence(blocks):
        return [lax.dynamic_index_in_dim(b, mine, 0, keepdims=False) for b in blocks]


    experts = capacity.shape[0]
    cap = 5 * tokens // (4 * experts)
    expert_of = jnp.take(hash_table, token_ids.reshape(tokens))
    onehot = (expert_of[:, None] == lax.iota(jnp.int32, experts)[None, :]).astype(jnp.int32)
    rank = jnp.sum(onehot * (jnp.cumsum(onehot, axis=0) - 1), axis=1)
    kept = rank < jnp.take(capacity, expert_of)
    near_expert = expert_of ^ lax.axis_index("exp")
    slot = jnp.where(kept, near_expert * cap + rank, experts * cap)
    slots = lax.iota(jnp.int32, experts * cap)
    place = (slots[:, None] == slot[None, :]).astype(bf16)
    pick = (slots[None, :] == slot[:, None]).astype(bf16)

    def to_experts(rows):
        sent = jnp.dot(place, rows, preferred_element_type=f32).astype(bf16)
        return exchange_exp(sent)

    grad_rows = out_grad.reshape(tokens, width)
    dy = to_experts(grad_rows)
    da = lax.dot_general(dy, down, (((1,), (1,)), ((), ())), preferred_element_type=f32)

    head_full = (3 * pair + 2 * parity) % HEADS
    head_half = (3 * pair + 1) % HEADS
    w_heads = w_qkv.reshape(width, 3, HEADS, HEAD_DIM)

    def of_head(x, axis):
        return jnp.stack(
            [
                lax.dynamic_index_in_dim(x, head_full, axis, keepdims=False),
                lax.dynamic_index_in_dim(x, head_half, axis, keepdims=False),
            ]
        )

    w_mine = of_head(w_heads, 2)
    qb = of_head(q_bias.reshape(HEADS, HEAD_DIM), 0)
    vb = of_head(v_bias.reshape(HEADS, HEAD_DIM), 0)
    bias = jnp.stack([qb, jnp.zeros_like(qb), vb], axis=1)
    wt = w_mine.transpose(0, 2, 3, 1).reshape(6 * HEAD_DIM, width)
    wn = w_mine[:, :, 1:].transpose(1, 0, 2, 3).reshape(width, 4 * HEAD_DIM)
    params = (row(ln1_gain), row(ln1_bias), wt, bias.reshape(-1, 1), wn, row(bias[:, 1:]))
    places = me ^ lax.iota(jnp.int32, cycle)
    blocks = of_sequence(gather_seq(inputs))
    h1, q, kt, vt, k, v = prep(blocks, places, parity, *params)

    full = [(0, i, (i * QT + QT + KC - 1) // KC) for i in range(nk // QT)]
    half = [(1, i, (2 * (i * QT + QT) + KC - 1) // KC) for i in range(nk // (2 * QT))]
    tiles = sorted(full + half, key=lambda t: t[2])
    attn, attn_low, linv, p = attn_fwd(q, k, vt, parity, tiles, span)

    got = from_owners(exchange(attn_low, "seq"), span).reshape(nseq, width, span)
    x_rows = inputs.reshape(tokens, width).astype(f32)
    middle = (
        x_rows
        + jnp.einsum("nht,hd->ntd", got, w_out, preferred_element_type=f32).reshape(tokens, width)
        + out_bias
    )
    h2 = layer_norm(middle, ln2_gain, ln2_bias).astype(bf16)

    h2, da, pick = lax.optimization_barrier((h2, da, pick))
    rows = lax.optimization_barrier(to_experts(h2))
    z = jnp.dot(rows, up, preferred_element_type=f32) + up_bias
    phi = 0.5 * (1.0 + lax.erf(z * (1.0 / math.sqrt(2.0))))
    hidden = (z * phi).astype(bf16)
    slope = phi + z * jnp.exp(-0.5 * z * z) * (1.0 / math.sqrt(2.0 * math.pi))
    dz = (da * slope).astype(bf16)
    dh2 = lax.dot_general(dz, up, (((1,), (1,)), ((), ())), preferred_element_type=f32)
    back = exchange_exp(dh2.astype(bf16))
    shares = expert_sums(rows, dy, dz, hidden)
    y = jnp.dot(hidden, down, preferred_element_type=f32) + down_bias[0]
    back, shares = lax.optimization_barrier((back, shares))

    grad_middle, branch, do_home, small2 = pull(
        back, pick, grad_rows, middle, row(ln2_gain), w_out
    )
    do_units = jnp.swapaxes(do_home.reshape(width, nseq, span), 0, 1)
    do = exchange(to_owners(do_units.reshape(pairs, 3, HEAD_DIM, span), span), "seq")
    low_rows = got.transpose(0, 2, 1).reshape(tokens, width)
    grad_w_out = lax.dot_general(
        low_rows, branch, (((0,), (0,)), ((), ())), preferred_element_type=f32
    ).astype(bf16)
    small2 = jnp.pad(small2, ((0, 13), (0, 0))).astype(bf16)
    do, y, grad_w_out, small2, shares = lax.optimization_barrier(
        (do, y.astype(bf16), grad_w_out, small2, shares)
    )
    shares = lax.psum_scatter(
        shares.reshape(-1, width), "seq", scatter_dimension=0, tiled=True
    )
    y_back = exchange_exp(y)
    w_out_part = jnp.concatenate(
        [
            grad_w_out.reshape(cycle, width // cycle, width),
            jnp.broadcast_to(small2[None], (cycle, 16, width)),
        ],
        axis=1,
    )
    w_out_part = jnp.sum(exchange(w_out_part, "seq"), axis=0, dtype=f32).astype(bf16)

    slot_of = {t[:2]: j for j, t in enumerate(tiles)}
    dq_half, sums_mine, sums_other = attn_bwd(
        1, q, do, attn, linv, kt, v, p, parity, half, [slot_of[t[:2]] for t in half], span
    )
    sums = (sums_mine + swap(sums_other, "seq", 1).astype(f32)).astype(bf16)
    part_half = jnp.concatenate([dq_half, sums], axis=1)
    home_half = exchange(part_half, "seq")
    g_half = head_weights(part_half, h1, parity, True)
    part_full = attn_bwd(
        0, q, do, attn, linv, kt, v, p, parity, full, [slot_of[t[:2]] for t in full], span
    )[0]
    rows_half = 3 * HEAD_DIM
    halves = g_half[:rows_half].astype(bf16).reshape(2, rows_half // 2, width)
    keep = lax.dynamic_index_in_dim(halves, parity, 0, keepdims=False)
    away = lax.dynamic_index_in_dim(halves, 1 - parity, 0, keepdims=False)
    keep = (keep.astype(f32) + swap(away, "seq", 1).astype(f32)).astype(bf16)
    part_full, home_half, keep, y_back, w_out_part = lax.optimization_barrier(
        (part_full, home_half, keep, y_back, w_out_part)
    )

    home_full = exchange(part_full, "seq")
    column = sum_exp(pack(part_full, h1, keep, w_out_part, g_half[rows_half:, :rows_half]))
    input_grad = home(
        home_full,
        home_half,
        w_qkv,
        inputs,
        row(ln1_gain),
        grad_middle.reshape(nseq, span, width),
    )
    output = middle + jnp.dot(pick, y_back, preferred_element_type=f32)
    output = output.astype(bf16).reshape(nseq, span, width)
    input_grad, column, output = lax.optimization_barrier((input_grad, column, output))
    grad_w_qkv, bias_rows, ln1_grads, grad_w_out, small2 = build(
        gather_seq(column), w_qkv, row(ln1_gain), row(ln1_bias), nseq
    )
    shares = shares.astype(f32)
    down_share = lax.dynamic_slice_in_dim(
        shares[2 * share + 16], me * (width // cycle), width // cycle, 0
    )
    return (
        output,
        input_grad,
        ln1_grads[0],
        ln1_grads[1],
        grad_w_qkv,
        bias_rows[0, :width],
        bias_rows[0, 2 * width :],
        grad_w_out,
        small2[0],
        small2[1],
        small2[2],
        shares[:share].T[None],
        shares[2 * share : 2 * share + 1, :share],
        shares[share : 2 * share][None],
        down_share[None],
    )


def solution(mesh):
    in_specs = (
        P("exp", "seq", None),
        P("exp", "seq"),
        P(),
        P(),
        P(),
        P(),
        P(),
        P(),
        P(),
        P(),
        P(),
        P(),
        P(),
        P("exp", None, None),
        P("exp", None),
        P("exp", None, None),
        P("exp", None),
        P("exp", "seq", None),
    )
    out_specs = (
        P("exp", "seq", None),
        P("exp", "seq", None),
        P(),
        P(),
        P(),
        P(),
        P(),
        P(),
        P(),
        P(),
        P(),
        P("exp", None, "seq"),
        P("exp", "seq"),
        P("exp", "seq", None),
        P("exp", "seq"),
    )
    return jax.shard_map(local, mesh=mesh, in_specs=in_specs, out_specs=out_specs, check_vma=False)
```

```python
from functools import partial
import math

import jax
import jax.numpy as jnp
from jax import lax
from jax.experimental import pallas as pl
from jax.experimental.pallas import tpu as pltpu
from jax.sharding import PartitionSpec as P

HEADS = 12
HEAD_DIM = 64
f32 = jnp.float32
bf16 = jnp.bfloat16

norm_eps = 1e-05
logit_scale = 0.125
masked_score = -1e30
LOG2E = math.log2(math.e)

QT = 512
KC = 1024
SUB = 256
SUBF = 512
VMEM = 56 * 2**20


def rows_of(start, size):
    return pl.ds(pl.multiple_of(start, size), size)


def load_tile(ref, kind, t, span):
    nf, nh = QT // span, 2 * QT // span

    def full():
        return jnp.concatenate([ref[t * nf + j, :, :span] for j in range(nf)], axis=-1)

    def half(t):
        return jnp.concatenate([ref[t * nh + j, :, span:] for j in range(nh)], axis=-1)

    if isinstance(kind, int):
        return half(t) if kind else full()
    return jnp.where(kind == 0, full(), half(jnp.minimum(t, ref.shape[0] // nh - 1)))


def tile_places(kind, t, parity, span):
    col = lax.broadcasted_iota(jnp.int32, (1, QT), 1)
    at = t * QT + col
    block = lax.div(at, span // 2)
    j = at - block * (span // 2)
    quarter = span // 4
    outer = jnp.where(j >= quarter, j + 2 * quarter, j)
    half = block * span + jnp.where(parity == 0, outer, j + quarter)
    return jnp.where(kind == 0, at, half)


def loop(low, high, do):
    def step(c, _):
        do(c)
        return 0

    lax.fori_loop(low, high, step, 0)


def fwd_kernel(
    span,
    n_ref,
    kind_ref,
    tile_ref,
    par_ref,
    q_ref,
    k_ref,
    vt_ref,
    o_ref,
    low_ref,
    linv_ref,
    p_hbm,
    s0,
    s1,
    p0,
    p1,
    m0,
    m1,
    acc_scr,
    l_scr,
    sem0,
    sem1,
):
    i = pl.program_id(0)
    last = pl.num_programs(0) - 1
    before = jnp.maximum(i - 1, 0)
    n1 = n_ref[i]
    n2 = n_ref[before]
    unit1 = kind_ref[i]
    unit2 = kind_ref[before]

    def work(c1, c2, masked, now, old, q, place):
        s_now, m_now = now
        s_old, p_old, m_old = old
        if c1 is not None:
            m = m_now[...]
        if c2 is not None:
            top = jnp.max(m_old[...], axis=0, keepdims=True) * (logit_scale * LOG2E)
            l = l_scr[...]
            o = acc_scr[...]
        for j in range(KC // SUBF):
            if c1 is not None:
                off = c1 * KC + j * SUBF
                s = jnp.dot(k_ref[rows_of(off, SUBF), :], q, preferred_element_type=f32)
                if masked:
                    key = lax.broadcasted_iota(jnp.int32, (SUBF, QT), 0)
                    s = jnp.where(key <= place - off, s, masked_score)
                s_now[rows_of(off, SUBF), :] = s
                m = jnp.maximum(m, jnp.max(s.reshape(SUBF // 8, 8, QT), axis=0))
            if c2 is not None:
                off = c2 * KC + j * SUBF
                s = s_old[rows_of(off, SUBF), :]
                p = jnp.exp2(s * (logit_scale * LOG2E) - top)
                l = l + jnp.sum(p.reshape(SUBF // 8, 8, QT), axis=0)
                low = p.astype(bf16)
                p_old[rows_of(off, SUBF), :] = low
                o = o + jnp.dot(
                    vt_ref[unit2, :, rows_of(off, SUBF)], low, preferred_element_type=f32
                )
        if c1 is not None:
            m_now[...] = m
        if c2 is not None:
            l_scr[...] = l
            acc_scr[...] = o

    def send(c, p_scr, sem):
        part = rows_of(c * KC, KC)
        pltpu.make_async_copy(p_scr.at[part], p_hbm.at[before, part], sem).start()

    def drain(count, p_scr, sem):
        def wait(c):
            part = pl.ds(0, KC)
            pltpu.make_async_copy(p_scr.at[part], p_hbm.at[0, part], sem).wait()

        loop(0, count, wait)

    @pl.when(i >= 1)
    def _():
        l_scr[...] = jnp.zeros_like(l_scr)
        acc_scr[...] = jnp.zeros_like(acc_scr)

    slots = ((s0, p0, m0, sem0), (s1, p1, m1, sem1))
    for turn in (0, 1):
        s_now, p_now, m_now, sem_now = slots[turn]
        s_old, p_old, m_old, sem_old = slots[1 - turn]

        @pl.when(lax.rem(i, 2) == turn)
        def _(s_now=s_now, p_now=p_now, m_now=m_now, sem_now=sem_now, s_old=s_old, p_old=p_old, m_old=m_old, sem_old=sem_old, turn=turn):
            q = load_tile(q_ref, unit1, tile_ref[i], span)
            none = jnp.zeros_like(q)
            q = jnp.concatenate(
                [jnp.where(unit1 == 0, q, none), jnp.where(unit1 == 0, none, q)], axis=0
            )
            place = tile_places(unit1, tile_ref[i], par_ref[0], span)
            m_now[...] = jnp.full((8, QT), -jnp.inf, f32)

            @pl.when(i >= 3)
            def _():
                drain(n_ref[jnp.maximum(i - 3, 0)], p_old, sem_old)

            def go(c1, c2, masked=False):
                work(c1, c2, masked, (s_now, m_now), (s_old, p_old, m_old), q, place)

            if turn == 0:

                @pl.when(i == 0)
                def _():
                    loop(0, n1, lambda c: go(c, None, True))

            @pl.when(jnp.logical_and(i > 0, i < last))
            def _():
                go(n1 - 1, n2 - 1, True)
                send(n2 - 1, p_old, sem_old)
                both = jnp.minimum(n1, n2) - 1

                def step(c):
                    go(c, c)
                    send(c, p_old, sem_old)

                loop(0, both, step)
                loop(both, n1 - 1, lambda c: go(c, None))

            @pl.when(i == last)
            def _():
                def step(c):
                    go(None, c)
                    send(c, p_old, sem_old)

                loop(0, n2, step)
                drain(n_ref[jnp.maximum(i - 2, 0)], p_now, sem_now)
                drain(n2, p_old, sem_old)

    @pl.when(i > 0)
    def _():
        linv = 1.0 / jnp.sum(l_scr[...], axis=0, keepdims=True)
        o = acc_scr[...] * linv
        t = tile_ref[before]
        nf, nh = QT // span, 2 * QT // span
        for count, width, start, unit in ((nf, span, 0, 0), (nh, span // 2, span, 1)):

            @pl.when(unit2 == unit)
            def _(count=count, width=width, start=start):
                for j in range(count):
                    here = slice(j * width, (j + 1) * width)
                    there = pl.ds(start, width)
                    o_ref[t * count + j, :, there] = o[:, here]
                    low_ref[t * count + j, :, there] = o[:, here].astype(bf16)
                    linv_ref[t * count + j, :, there] = linv[:, here]


def table(values):
    return jnp.array(values, jnp.int32)


def pair_units(tiles):
    return sum(t[2] for t in tiles) * KC * QT


def whole(x):
    zeros = (0,) * len(x.shape)
    return pl.BlockSpec(x.shape, lambda *_: zeros)


def attn_fwd(q, k, vt, parity, tiles, span):
    nk = k.shape[0]
    steps = len(tiles)
    listed = tiles + [(tiles[-1][0], tiles[-1][1], 0)]
    linv = jax.ShapeDtypeStruct((q.shape[0], 1, q.shape[2]), f32)
    o = jax.ShapeDtypeStruct(q.shape, f32)
    work = pair_units(tiles)
    return pl.pallas_call(
        partial(fwd_kernel, span),
        name="attn_fwd",
        grid_spec=pltpu.PrefetchScalarGridSpec(
            num_scalar_prefetch=4,
            grid=(steps + 1,),
            in_specs=[whole(q), whole(k), whole(vt)],
            out_specs=[whole(q), whole(q), whole(linv), pl.BlockSpec(memory_space=pl.ANY)],
            scratch_shapes=[
                pltpu.VMEM((nk, QT), f32),
                pltpu.VMEM((nk, QT), f32),
                pltpu.VMEM((nk, QT), bf16),
                pltpu.VMEM((nk, QT), bf16),
                pltpu.VMEM((8, QT), f32),
                pltpu.VMEM((8, QT), f32),
                pltpu.VMEM((HEAD_DIM, QT), f32),
                pltpu.VMEM((8, QT), f32),
                pltpu.SemaphoreType.DMA,
                pltpu.SemaphoreType.DMA,
            ],
        ),
        out_shape=[
            o,
            jax.ShapeDtypeStruct(q.shape, bf16),
            linv,
            jax.ShapeDtypeStruct((steps, nk, QT), bf16),
        ],
        compiler_params=pltpu.CompilerParams(vmem_limit_bytes=VMEM),
        cost_estimate=pl.CostEstimate(
            flops=work * 1024, bytes_accessed=work * 2, transcendentals=work
        ),
    )(
        table([t[2] for t in listed]),
        table([t[0] for t in listed]),
        table([t[1] for t in listed]),
        parity.reshape(1),
        q,
        k,
        vt,
    )


def bwd_kernel(
    unit,
    span,
    n_ref,
    tile_ref,
    slot_ref,
    turn_ref,
    par_ref,
    q_ref,
    do_ref,
    o_ref,
    linv_ref,
    kt_ref,
    v_ref,
    p_hbm,
    *refs,
):
    outs = refs[:-10]
    p_scr, dp0, dp1, q_scr, do_scr, de_scr, dq_scr, dk_scr, dv_scr, sem = refs[-10:]
    dps = (dp0, dp1)
    i = pl.program_id(0)
    last = pl.num_programs(0) - 1
    a = lax.rem(i, 2)
    b = 1 - a
    before = jnp.maximum(i - 1, 0)
    n1 = n_ref[i]
    n2 = n_ref[before]
    turn1 = turn_ref[i]
    turn2 = turn_ref[before]
    devices = kt_ref.shape[2] // span

    def fetch(t, slot):
        def start(c):
            part = rows_of(c * KC, KC)
            pltpu.make_async_copy(
                p_hbm.at[slot_ref[t], part], p_scr.at[slot, part], sem.at[slot]
            ).start()

        loop(0, n_ref[t], start)

    def work(c1, dp_now, c2, slot, dp_old):
        if c1 is not None:
            do_now = do_scr[a]
        if c2 is not None:
            qt = q_scr[slot]
            dot = do_scr[slot, unit * HEAD_DIM : (unit + 1) * HEAD_DIM, :]
            delta = de_scr[slot]
            dq = dq_scr[...]
        for j in range(KC // SUB):
            here = pl.ds(j * SUB, SUB)
            if c1 is not None:
                dp_now[here, :] = jnp.dot(
                    v_ref[rows_of(c1 * KC + j * SUB, SUB), :],
                    do_now,
                    preferred_element_type=f32,
                )
            if c2 is not None:
                keys = rows_of(c2 * KC + j * SUB, SUB)
                p = p_scr[slot, keys, :]
                ds = (p.astype(f32) * (dp_old[here, :] - delta)).astype(bf16)
                dv_scr[:, keys] += lax.dot_general(
                    dot, p, (((1,), (1,)), ((), ())), preferred_element_type=f32
                )
                dk_scr[:, keys] += lax.dot_general(
                    qt, ds, (((1,), (1,)), ((), ())), preferred_element_type=f32
                )
                dq = dq + jnp.dot(kt_ref[unit, :, keys], ds, preferred_element_type=f32)
        if c2 is not None:
            dq_scr[...] = dq

    def by_turn(turn, do):
        for t in (0, 1):

            @pl.when(lax.rem(turn, 2) == t)
            def _(t=t):
                do(dps[t], dps[1 - t])

    def load():
        t = tile_ref[i]
        scaled = load_tile(do_ref, unit, t, span).astype(f32) * load_tile(linv_ref, unit, t, span)
        de_scr[a] = jnp.sum(scaled * load_tile(o_ref, unit, t, span), axis=0, keepdims=True)
        do_scr[a, unit * HEAD_DIM : (unit + 1) * HEAD_DIM, :] = scaled.astype(bf16)
        q_scr[a] = load_tile(q_ref, unit, t, span)

    @pl.when(i == 0)
    def _():
        do_scr[...] = jnp.zeros_like(do_scr)
        dk_scr[...] = jnp.zeros_like(dk_scr)
        dv_scr[...] = jnp.zeros_like(dv_scr)
        dq_scr[...] = jnp.zeros_like(dq_scr)
        fetch(0, 0)
        load()
        work(0, dps[0], None, None, None)

    @pl.when(jnp.logical_and(i > 0, i < last))
    def _():
        load()

        def step(now, other):
            work(0, now, n2 - 1, b, other)

        by_turn(turn1, step)

    @pl.when(i == last)
    def _():
        by_turn(n2 - 1 + turn2, lambda now, other: work(None, None, n2 - 1, b, now))

    @pl.when(i > 0)
    def _():
        dq = (dq_scr[...] * logit_scale).astype(bf16)
        t = tile_ref[before]
        width = span // 2 if unit else span
        count = QT // width
        for j in range(count):
            outs[0][t * count + j, :HEAD_DIM, :width] = dq[:, j * width : (j + 1) * width]
        dq_scr[...] = jnp.zeros_like(dq_scr)

    @pl.when(i < last)
    def _():
        def wait(c):
            part = pl.ds(0, KC)
            pltpu.make_async_copy(p_hbm.at[0, part], p_scr.at[a, part], sem.at[a]).wait()

        loop(0, n1, wait)

        @pl.when(i + 1 < last)
        def _():
            fetch(i + 1, b)

        def step(c):
            def both(now, other):
                work(c + 1, other, c, a, now)

            by_turn(c + turn1, both)

        loop(0, n1 - 1, step)

    @pl.when(i == last)
    def _():
        quarter = span // 4
        for d in range(devices):
            keys = pl.ds(d * span, span)
            dk = dk_scr[:, keys] * logit_scale
            dv = dv_scr[:, keys]
            if not unit:
                outs[0][d, HEAD_DIM : 2 * HEAD_DIM, :span] = dk.astype(bf16)
                outs[0][d, 2 * HEAD_DIM :, :span] = dv.astype(bf16)
            else:
                both = jnp.concatenate([dk, dv], axis=0)
                outer = jnp.concatenate([both[:, :quarter], both[:, 3 * quarter :]], axis=1)
                inner = both[:, quarter : 3 * quarter]
                even = par_ref[0] == 0
                outs[1][d] = jnp.where(even, outer, inner)
                outs[2][d] = jnp.where(even, inner, outer).astype(bf16)


def attn_bwd(unit, q, do, o, linv, kt, v, p, parity, tiles, slots, span):
    nk = kt.shape[2]
    steps = len(tiles)
    listed = tiles + [(unit, tiles[-1][1], 0)]
    turns = [0]
    for t in tiles:
        turns.append((turns[-1] + t[2]) % 2)
    devices = nk // span
    if unit:
        outs = [
            jax.ShapeDtypeStruct((devices, HEAD_DIM, span // 2), bf16),
            jax.ShapeDtypeStruct((devices, 2 * HEAD_DIM, span // 2), f32),
            jax.ShapeDtypeStruct((devices, 2 * HEAD_DIM, span // 2), bf16),
        ]
    else:
        outs = [jax.ShapeDtypeStruct((devices, 3 * HEAD_DIM, span), bf16)]
    work = pair_units(tiles)
    return pl.pallas_call(
        partial(bwd_kernel, unit, span),
        name="attn_bwd_half" if unit else "attn_bwd_full",
        grid_spec=pltpu.PrefetchScalarGridSpec(
            num_scalar_prefetch=5,
            grid=(steps + 1,),
            in_specs=[
                whole(q),
                whole(do),
                whole(o),
                whole(linv),
                whole(kt),
                whole(v),
                pl.BlockSpec(memory_space=pl.ANY),
            ],
            out_specs=[whole(x) for x in outs],
            scratch_shapes=[
                pltpu.VMEM((2, nk, QT), bf16),
                pltpu.VMEM((KC, QT), f32),
                pltpu.VMEM((KC, QT), f32),
                pltpu.VMEM((2, HEAD_DIM, QT), bf16),
                pltpu.VMEM((2, 2 * HEAD_DIM, QT), bf16),
                pltpu.VMEM((2, 1, QT), f32),
                pltpu.VMEM((HEAD_DIM, QT), f32),
                pltpu.VMEM((HEAD_DIM, nk), f32),
                pltpu.VMEM((HEAD_DIM, nk), f32),
                pltpu.SemaphoreType.DMA((2,)),
            ],
        ),
        out_shape=outs,
        compiler_params=pltpu.CompilerParams(vmem_limit_bytes=VMEM),
        cost_estimate=pl.CostEstimate(
            flops=work * 2048, bytes_accessed=work * 2, transcendentals=0
        ),
    )(
        table([t[2] for t in listed]),
        table([t[1] for t in listed]),
        table(slots + [slots[-1]]),
        table(turns),
        parity.reshape(1),
        q,
        do,
        o,
        linv,
        kt,
        v,
        p,
    )


def pick_quarters(x, parity, axis):
    q = x.shape[axis] // 4

    def cut(low, high):
        return x[low * q : high * q] if axis == 0 else x[:, low * q : high * q]

    outer = jnp.concatenate([cut(0, 1), cut(3, 4)], axis=axis)
    return jnp.where(parity == 0, outer, cut(1, 3))


def prep_kernel(count, pos_ref, par_ref, *refs):
    blocks = refs[:count]
    gain_ref, shift_ref, wt_ref, bt_ref, wn_ref, bn_ref = refs[count : count + 6]
    h_ref, q_ref, kt_ref, vt_ref, k_ref, v_ref, x_scr = refs[count + 6 :]
    i = pl.program_id(0)
    for j in range(count):

        @pl.when(i == j)
        def _(j=j):
            x_scr[...] = blocks[j][...].astype(f32)

    x = x_scr[...]
    span = x.shape[0]
    x = x - jnp.mean(x, axis=-1, keepdims=True)
    spread = jnp.mean(x * x, axis=-1, keepdims=True)
    h = (x * lax.rsqrt(spread + norm_eps) * gain_ref[...] + shift_ref[...]).astype(bf16)
    h_ref[...] = h
    over = lax.dot_general(
        wt_ref[...], h, (((1,), (1,)), ((), ())), preferred_element_type=f32
    )
    over = (over + bt_ref[...]).astype(bf16)
    d = HEAD_DIM
    q_ref[0, :, :span] = over[:d]
    q_ref[0, :, span:] = pick_quarters(over[3 * d : 4 * d], par_ref[0], 1)
    for unit in (0, 1):
        kt_ref[unit] = over[(3 * unit + 1) * d : (3 * unit + 2) * d]
        vt_ref[unit] = over[(3 * unit + 2) * d : (3 * unit + 3) * d]
    flat = (jnp.dot(h, wn_ref[...], preferred_element_type=f32) + bn_ref[...]).astype(bf16)
    k_ref[...] = flat[:, : 2 * d]
    v_ref[...] = flat[:, 2 * d :]


def prep(blocks, pos, parity, gain, shift, wt, bt, wn, bn):
    count = len(blocks)
    span, width = blocks[0].shape
    devices = lax.axis_size("seq")
    nk = devices * span
    d = HEAD_DIM
    shapes = [
        ((nk, width), (span, width), lambda i, s, _: (s[i], 0)),
        ((devices, d, 3 * span // 2), (1, d, 3 * span // 2), lambda i, s, _: (s[i], 0, 0)),
        ((2, d, nk), (2, d, span), lambda i, s, _: (0, 0, s[i])),
        ((2, d, nk), (2, d, span), lambda i, s, _: (0, 0, s[i])),
        ((nk, 2 * d), (span, 2 * d), lambda i, s, _: (s[i], 0)),
        ((nk, 2 * d), (span, 2 * d), lambda i, s, _: (s[i], 0)),
    ]
    params = (gain, shift, wt, bt, wn, bn)
    return pl.pallas_call(
        partial(prep_kernel, count),
        name="prep",
        grid_spec=pltpu.PrefetchScalarGridSpec(
            num_scalar_prefetch=2,
            grid=(count,),
            in_specs=[whole(b) for b in blocks]
            + [whole(x) for x in params],
            out_specs=[pl.BlockSpec(block, index) for _, block, index in shapes],
            scratch_shapes=[pltpu.VMEM((span, width), f32)],
        ),
        out_shape=[jax.ShapeDtypeStruct(shape, bf16) for shape, _, _ in shapes],
        compiler_params=pltpu.CompilerParams(vmem_limit_bytes=VMEM),
        cost_estimate=pl.CostEstimate(
            flops=1, bytes_accessed=1, transcendentals=0
        ),
    )(pos, parity.reshape(1), *blocks, *params)


def pull_kernel(
    back_ref, pick_ref, grad_ref, mid_ref, gain_ref, w_ref, gm_ref, br_ref, do_ref, small_ref
):
    dh = jnp.dot(pick_ref[...], back_ref[...], preferred_element_type=f32)
    x = mid_ref[...]
    x = x - jnp.mean(x, axis=-1, keepdims=True)
    inv = lax.rsqrt(jnp.mean(x * x, axis=-1, keepdims=True) + norm_eps)
    x = x * inv
    d = dh * gain_ref[...]
    dx = inv * (
        d - jnp.mean(d, axis=-1, keepdims=True) - x * jnp.mean(d * x, axis=-1, keepdims=True)
    )
    gm = grad_ref[...].astype(f32) + dx
    branch = gm.astype(bf16)
    gm_ref[...] = gm
    br_ref[...] = branch
    small_ref[0:1] = jnp.sum(branch.astype(f32), axis=0, keepdims=True)
    small_ref[1:2] = jnp.sum(dh * x, axis=0, keepdims=True)
    small_ref[2:3] = jnp.sum(dh, axis=0, keepdims=True)
    do = lax.dot_general(
        w_ref[...], branch, (((1,), (1,)), ((), ())), preferred_element_type=f32
    ).astype(bf16)
    span = do_ref.shape[2] * 2 // 3
    for u in range(do.shape[1] // span * HEADS):
        n, head = u // HEADS, u % HEADS
        part = do[head * HEAD_DIM : (head + 1) * HEAD_DIM, n * span : (n + 1) * span]
        p, role = u // 3, u % 3
        if role != 1:
            do_ref[2 * p + role // 2, :, :span] = part
        else:
            q = span // 4
            outer = jnp.concatenate([part[:, :q], part[:, 3 * q :]], axis=1)
            do_ref[2 * p, :, span:] = outer
            do_ref[2 * p + 1, :, span:] = part[:, q : 3 * q]


def pull(back, pick, grad, mid, gain, w_out, span):
    tokens, width = grad.shape
    return pl.pallas_call(
        pull_kernel,
        name="pull",
        out_shape=[
            jax.ShapeDtypeStruct((tokens, width), f32),
            jax.ShapeDtypeStruct((tokens, width), bf16),
            jax.ShapeDtypeStruct((lax.axis_size("seq"), HEAD_DIM, 3 * span // 2), bf16),
            jax.ShapeDtypeStruct((3, width), f32),
        ],
        compiler_params=pltpu.CompilerParams(vmem_limit_bytes=VMEM),
        cost_estimate=pl.CostEstimate(
            flops=4 * tokens * width * width, bytes_accessed=tokens * width * 16, transcendentals=0
        ),
    )(back, pick, grad, mid, gain, w_out)


def pack_kernel(half, at_ref, part_ref, h_ref, out_ref, small_ref, piece_ref, acc, cnt):
    i = pl.program_id(0)
    devices, rows, tokens = part_ref.shape
    stretch, width = h_ref.shape[0] // devices, h_ref.shape[1]
    g = jnp.zeros((rows, width), f32)
    count = jnp.zeros((8, rows), f32)
    ones = jnp.ones((8, tokens), bf16)
    for d in range(devices):
        part = part_ref[d]
        h = h_ref[pl.ds(d * stretch, stretch), :]
        if half:
            h = pick_quarters(h, at_ref[1], 0)
        g += jnp.dot(part, h, preferred_element_type=f32)
        count += lax.dot_general(
            ones, part, (((1,), (1,)), ((), ())), preferred_element_type=f32
        )

    @pl.when(i == 0)
    def _():
        acc[...] = g
        cnt[...] = count

    @pl.when(i > 0)
    def _():
        acc[...] += g
        cnt[...] += count

    @pl.when(i == pl.num_programs(0) - 1)
    def _():
        nexp, share, _ = piece_ref.shape
        line = jnp.concatenate([cnt[...], jnp.zeros((8, width - rows), f32)], axis=1)
        line = jnp.concatenate([line, small_ref[...]], axis=0)
        filled = rows + out_ref.shape[0] + 16
        parts = [acc[...].astype(bf16), out_ref[...], line.astype(bf16)]
        if nexp * share > filled:
            parts.append(jnp.zeros((nexp * share - filled, width), bf16))
        piece = jnp.concatenate(parts, axis=0)
        for e in range(nexp):
            piece_ref[at_ref[0] ^ e] = piece[e * share : (e + 1) * share]


def pack(part, h1, parity, half, out_rows, small):
    devices, rows, _ = part.shape
    nk, width = h1.shape
    nexp = lax.axis_size("exp")
    filled = rows + out_rows.shape[0] + 16
    share = -(-filled // (16 * nexp)) * 16
    steps = 4
    return pl.pallas_call(
        partial(pack_kernel, half),
        name="pack_half" if half else "pack_full",
        grid_spec=pltpu.PrefetchScalarGridSpec(
            num_scalar_prefetch=1,
            grid=(steps,),
            in_specs=[
                pl.BlockSpec(
                    (devices // steps, rows, nk // devices // (2 if half else 1)),
                    lambda i, _: (i, 0, 0),
                ),
                pl.BlockSpec((nk // steps, width), lambda i, _: (i, 0)),
                whole(out_rows),
                whole(small),
            ],
            out_specs=pl.BlockSpec((nexp, share, width), lambda i, _: (0, 0, 0)),
            scratch_shapes=[pltpu.VMEM((rows, width), f32), pltpu.VMEM((8, rows), f32)],
        ),
        out_shape=jax.ShapeDtypeStruct((nexp, share, width), bf16),
        compiler_params=pltpu.CompilerParams(vmem_limit_bytes=VMEM),
        cost_estimate=pl.CostEstimate(flops=1, bytes_accessed=1, transcendentals=0),
    )(jnp.stack([lax.axis_index("exp"), parity]), part, h1, out_rows, small)


def home_kernel(nseq, span, full_ref, half_ref, w_ref, x_ref, gain_ref, gm_ref, dx_ref, u_scr):
    pairs = full_ref.shape[0] // 2
    quarter = span // 4
    for n in range(nseq):
        here = pairs // nseq
        for j in range(here):
            p = n * here + j
            outer, inner = half_ref[2 * p], half_ref[2 * p + 1]
            mid = jnp.concatenate([outer[:, :quarter], inner, outer[:, quarter:]], axis=1)
            for role, unit in enumerate((full_ref[2 * p], mid, full_ref[2 * p + 1])):
                for c in range(3):
                    at = c * HEADS + 3 * j + role
                    u_scr[pl.ds(at * HEAD_DIM, HEAD_DIM), :] = unit[
                        c * HEAD_DIM : (c + 1) * HEAD_DIM
                    ]
        dh = jnp.dot(w_ref[...], u_scr[...], preferred_element_type=f32).T
        x = x_ref[n].astype(f32)
        x = x - jnp.mean(x, axis=-1, keepdims=True)
        inv = lax.rsqrt(jnp.mean(x * x, axis=-1, keepdims=True) + norm_eps)
        x = x * inv
        d = dh * gain_ref[...]
        dx_ref[n] = gm_ref[n] + inv * (
            d - jnp.mean(d, axis=-1, keepdims=True) - x * jnp.mean(d * x, axis=-1, keepdims=True)
        )


def home(full, half, w_qkv, x, gain, grad_middle):
    nseq, span, width = x.shape
    return pl.pallas_call(
        partial(home_kernel, nseq, span),
        name="home",
        out_shape=jax.ShapeDtypeStruct((nseq, span, width), f32),
        scratch_shapes=[pltpu.VMEM((3 * width, span), bf16)],
        compiler_params=pltpu.CompilerParams(vmem_limit_bytes=VMEM),
        cost_estimate=pl.CostEstimate(
            flops=1, bytes_accessed=1, transcendentals=0
        ),
    )(full, half, w_qkv, x, gain, grad_middle)


def build_kernel(nseq, nexp, devices, cut, at_ref, *refs):
    halves, fulls = refs[0], refs[1 : 1 + devices]
    w_ref, gain_ref, shift_ref, g_ref, out_ref, small_ref, half, full, acc, sem = refs[1 + devices :]
    me, z = at_ref[0], at_ref[1]
    c = pl.program_id(0)
    d = HEAD_DIM
    rows = 3 * d
    width = g_ref.shape[0]
    out_rows = width // devices

    @pl.when(c == 0)
    def _():
        share = full.shape[1] // nexp
        for j in range(devices):
            pltpu.make_async_copy(halves.at[j], half.at[j], sem).start()
            for e in range(nexp):
                pltpu.make_async_copy(
                    fulls[j].at[pl.ds(pl.multiple_of((z ^ e) * share, 16), share)],
                    full.at[j, pl.ds(e * share, share)],
                    sem,
                ).start()
        acc[...] = jnp.zeros_like(acc)
        pltpu.make_async_copy(half, half, sem).wait()
        pltpu.make_async_copy(full, full, sem).wait()

    def from_unit(u, at, lanes):
        p, role = u // 3, u % 3
        if role != 1:
            return full[me ^ (2 * p + role // 2), at, lanes].astype(f32)
        return half[2 * p, at, lanes].astype(f32) + half[2 * p + 1, at, lanes].astype(f32)

    def unit_rows(u):
        return from_unit(u, rows_of(c * d, d), slice(None))

    def unit_sums(u):
        line = rows + (cut if u % 3 == 1 else out_rows - cut)
        line = from_unit(u, pl.ds(line, 16), pl.ds(0, rows))[:1]
        return jnp.where(c == 0, line[:, :d], jnp.where(c == 1, line[:, d : 2 * d], line[:, 2 * d :]))

    for two in range(HEADS // 2):
        heads = (2 * two, 2 * two + 1)
        grads = [sum(unit_rows(n * HEADS + h) for n in range(nseq)) for h in heads]
        sums = [sum(unit_sums(n * HEADS + h) for n in range(nseq)) for h in heads]
        at = pl.ds(two * 2 * d, 2 * d)
        block = jnp.concatenate(grads, axis=0)
        total = jnp.concatenate(sums, axis=1)
        g_ref[:, at] = block.T
        w = w_ref[at, :]
        gained = w.astype(f32) * block
        acc[:8] += jnp.sum(gained.reshape(2 * d // 8, 8, width), axis=0)
        acc[8:] += jnp.dot(
            jnp.broadcast_to(total, (8, 2 * d)).astype(bf16), w, preferred_element_type=f32
        )

        @pl.when(c == 0)
        def _(at=at, total=total):
            small_ref[2:3, at] = total

        @pl.when(c == 2)
        def _(at=at, total=total):
            small_ref[3:4, at] = total

    @pl.when(c == 2)
    def _():
        gained = jnp.sum(acc[:8], axis=0, keepdims=True)
        shifted = acc[8:9]
        small_ref[0:1] = (gained - shift_ref[...] * shifted) / gain_ref[...]
        small_ref[1:2] = shifted
        small_ref[4:7] = half[0, pl.ds(rows + cut, 16), :].astype(f32)[8:11]
        small_ref[7:8] = jnp.zeros_like(shifted)
        for i in range(devices):
            out_ref[pl.ds(i * out_rows, cut), :] = half[i, pl.ds(rows, cut), :].astype(f32)
            out_ref[pl.ds(i * out_rows + cut, out_rows - cut), :] = full[
                me ^ i, pl.ds(rows, out_rows - cut), :
            ].astype(f32)


def build(halves, fulls, cut, w_rows, gain, shift, nseq):
    width = w_rows.shape[1]
    devices = len(fulls)
    nexp = lax.axis_size("exp")
    at = jnp.stack([lax.axis_index("seq"), lax.axis_index("exp")])
    away = pl.BlockSpec(memory_space=pl.ANY)
    return pl.pallas_call(
        partial(build_kernel, nseq, nexp, devices, cut),
        name="build",
        grid=(3,),
        in_specs=[pl.BlockSpec(memory_space=pltpu.SMEM)]
        + [away] * (1 + devices)
        + [pl.BlockSpec((width, width), lambda c: (c, 0)), whole(gain), whole(shift)],
        out_specs=[
            pl.BlockSpec((width, width), lambda c: (0, c)),
            pl.BlockSpec((width, width), lambda c: (0, 0)),
            pl.BlockSpec((8, width), lambda c: (0, 0)),
        ],
        out_shape=[
            jax.ShapeDtypeStruct((width, 3 * width), f32),
            jax.ShapeDtypeStruct((width, width), f32),
            jax.ShapeDtypeStruct((8, width), f32),
        ],
        scratch_shapes=[
            pltpu.VMEM(halves.shape, bf16),
            pltpu.VMEM((devices, *fulls[0].shape), bf16),
            pltpu.VMEM((16, width), f32),
            pltpu.SemaphoreType.DMA,
        ],
        compiler_params=pltpu.CompilerParams(vmem_limit_bytes=VMEM),
        cost_estimate=pl.CostEstimate(
            flops=0, bytes_accessed=18 * width * width, transcendentals=0
        ),
    )(at, halves, *fulls, w_rows, gain, shift)


def expert_sums_kernel(rows_ref, dy_ref, dz_ref, hid_ref, out_ref):
    contract = (((0,), (0,)), ((), ()))
    dz = dz_ref[...]
    share = dz.shape[1]
    dy = dy_ref[...]
    out_ref[0, :share] = lax.dot_general(
        dz, rows_ref[...], contract, preferred_element_type=f32
    ).astype(bf16)
    out_ref[0, share : 2 * share] = lax.dot_general(
        hid_ref[...], dy, contract, preferred_element_type=f32
    ).astype(bf16)
    ones = jnp.ones((16, dz.shape[0]), bf16)
    up = jnp.dot(ones, dz, preferred_element_type=f32).astype(bf16)
    fill = jnp.zeros((16, dy.shape[1] - share), bf16)
    out_ref[0, 2 * share : 2 * share + 16] = jnp.concatenate([up, fill], axis=1)
    out_ref[0, 2 * share + 16 :] = jnp.dot(ones, dy, preferred_element_type=f32).astype(bf16)


def expert_sums(rows, dy, dz, hidden):
    devices = lax.axis_size("seq")
    count, width = rows.shape
    ff = dz.shape[1]
    share = ff // devices
    if share % 128:
        contract = (((0,), (0,)), ((), ()))
        up = lax.dot_general(dz, rows, contract, preferred_element_type=f32)
        down = lax.dot_general(hidden, dy, contract, preferred_element_type=f32)
        up_bias = jnp.pad(
            jnp.sum(dz, axis=0, dtype=f32).reshape(devices, 1, share),
            ((0, 0), (0, 15), (0, width - share)),
        )
        down_bias = jnp.broadcast_to(jnp.sum(dy, axis=0, dtype=f32), (devices, 16, width))
        return jnp.concatenate(
            [up.reshape(devices, share, width), down.reshape(devices, share, width), up_bias, down_bias],
            axis=1,
        ).astype(bf16)
    total = 2 * share + 32
    return pl.pallas_call(
        expert_sums_kernel,
        name="expert_sums",
        grid=(devices,),
        in_specs=[
            pl.BlockSpec((count, width), lambda j: (0, 0)),
            pl.BlockSpec((count, width), lambda j: (0, 0)),
            pl.BlockSpec((count, share), lambda j: (0, j)),
            pl.BlockSpec((count, share), lambda j: (0, j)),
        ],
        out_specs=pl.BlockSpec((1, total, width), lambda j: (j, 0, 0)),
        out_shape=jax.ShapeDtypeStruct((devices, total, width), bf16),
        compiler_params=pltpu.CompilerParams(vmem_limit_bytes=VMEM),
        cost_estimate=pl.CostEstimate(
            flops=1, bytes_accessed=1, transcendentals=0
        ),
    )(rows, dy, dz, hidden)


def swap(x, axis, distance):
    return lax.ppermute(x, axis, [(i, i ^ distance) for i in range(lax.axis_size(axis))])


def gather_chips(x, beside=()):
    chips = lax.axis_size("seq") // 2
    if chips != 4:
        return [x] + [swap(x, "seq", 2 * d) for d in range(1, chips)], beside
    one, two = swap(x, "seq", 2), swap(x, "seq", 4)
    if beside:
        one, two, beside = lax.optimization_barrier((one, two, beside))
    axis = x.ndim - 2
    half = x.shape[axis] // 2
    low = swap(lax.slice_in_dim(one, 0, half, axis=axis), "seq", 4)
    high = swap(lax.slice_in_dim(two, half, 2 * half, axis=axis), "seq", 2)
    return [x, one, two, jnp.concatenate([low, high], axis=axis)], beside


def gather_seq(x, beside):
    blocks = []
    chips, beside = gather_chips(x, beside)
    for block in chips:
        blocks += [block, swap(block, "seq", 1)]
    return blocks, beside


def in_order(stack, axis):
    me = lax.axis_index(axis)
    return jnp.take(stack, me ^ lax.iota(jnp.int32, stack.shape[0]), axis=0)


def sum_exp(parts):
    total = parts[0].astype(f32)
    for d in range(1, parts.shape[0]):
        total = total + swap(parts[d], "exp", d).astype(f32)
    return total.astype(bf16)


def gather_exp(total):
    return jnp.concatenate([total] + [swap(total, "exp", d) for d in range(1, lax.axis_size("exp"))])


def layer_norm(values, gain, shift):
    centre = jnp.mean(values, axis=-1, keepdims=True)
    centered = values - centre
    spread = jnp.mean(centered * centered, axis=-1, keepdims=True)
    return centered * lax.rsqrt(spread + norm_eps) * gain + shift


def from_owners(got, span):
    quarter = span // 4
    both = got.reshape(got.shape[0] // 2, 2, *got.shape[1:])
    outer, inner = both[:, 0, ..., span:], both[:, 1, ..., span:]
    mid = jnp.concatenate([outer[..., :quarter], inner, outer[..., quarter:]], axis=-1)
    return jnp.stack([both[:, 0, ..., :span], mid, both[:, 1, ..., :span]], axis=1)


def exchange(x, axis):
    return lax.all_to_all(x, axis, split_axis=0, concat_axis=0, tiled=True)


def exchange_exp(x):
    nexp = lax.axis_size("exp")
    parts = x.reshape(nexp, x.shape[0] // nexp, x.shape[1])
    return jnp.concatenate([parts[0]] + [swap(parts[d], "exp", d) for d in range(1, nexp)])


def local(
    inputs,
    token_ids,
    hash_table,
    capacity,
    ln1_gain,
    ln1_bias,
    w_qkv,
    q_bias,
    v_bias,
    w_out,
    out_bias,
    ln2_gain,
    ln2_bias,
    up_weight,
    up_bias,
    down_weight,
    down_bias,
    out_grad,
):
    nseq, span, width = inputs.shape
    tokens = nseq * span
    cycle = lax.axis_size("seq")
    me = lax.axis_index("seq")
    parity = me % 2
    pair = me // 2
    pairs = cycle // 2
    nk = cycle * span
    assert nseq * HEADS == 3 * pairs
    up, down = up_weight[0], down_weight[0]
    ff = up.shape[1]
    share = ff // cycle
    row = lambda x: x.reshape(1, -1)

    mine = (3 * pair) // HEADS
    def of_sequence(blocks):
        return [lax.dynamic_index_in_dim(b, mine, 0, keepdims=False) for b in blocks]


    experts = capacity.shape[0]
    cap = 5 * tokens // (4 * experts)
    expert_of = jnp.take(hash_table, token_ids.reshape(tokens))
    onehot = (expert_of[:, None] == lax.iota(jnp.int32, experts)[None, :]).astype(jnp.int32)
    rank = jnp.sum(onehot * (jnp.cumsum(onehot, axis=0) - 1), axis=1)
    kept = rank < jnp.take(capacity, expert_of)
    near_expert = expert_of ^ lax.axis_index("exp")
    slot = jnp.where(kept, near_expert * cap + rank, experts * cap)
    slots = lax.iota(jnp.int32, experts * cap)
    place = (slots[:, None] == slot[None, :]).astype(bf16)
    pick = (slots[None, :] == slot[:, None]).astype(bf16)

    def to_experts(rows):
        sent = jnp.dot(place, rows, preferred_element_type=f32).astype(bf16)
        return exchange_exp(sent)

    grad_rows = out_grad.reshape(tokens, width)
    dy = to_experts(grad_rows)
    da = lax.dot_general(dy, down, (((1,), (1,)), ((), ())), preferred_element_type=f32)

    head_full = (3 * pair + 2 * parity) % HEADS
    head_half = (3 * pair + 1) % HEADS
    w_heads = w_qkv.reshape(width, 3, HEADS, HEAD_DIM)

    def of_head(x, axis):
        return jnp.stack(
            [
                lax.dynamic_index_in_dim(x, head_full, axis, keepdims=False),
                lax.dynamic_index_in_dim(x, head_half, axis, keepdims=False),
            ]
        )

    w_mine = of_head(w_heads, 2)
    qb = of_head(q_bias.reshape(HEADS, HEAD_DIM), 0)
    vb = of_head(v_bias.reshape(HEADS, HEAD_DIM), 0)
    bias = jnp.stack([qb, jnp.zeros_like(qb), vb], axis=1)
    wt = w_mine.transpose(0, 2, 3, 1).reshape(6 * HEAD_DIM, width)
    wn = w_mine[:, :, 1:].transpose(1, 2, 0, 3).reshape(width, 4 * HEAD_DIM)
    bn = row(bias[:, 1:].transpose(1, 0, 2))
    params = (row(ln1_gain), row(ln1_bias), wt, bias.reshape(-1, 1), wn, bn)
    places = me ^ lax.iota(jnp.int32, cycle)
    chips, _ = gather_chips(inputs)
    far, params, pick, place, places = lax.optimization_barrier(
        (chips[-1], params, pick, place, places)
    )
    blocks = []
    for block in chips[:-1] + [far]:
        blocks += [block, swap(block, "seq", 1)]
    h1, q, kt, vt, k, v = prep(of_sequence(blocks), places, parity, *params)

    full = [(0, i, (i * QT + QT + KC - 1) // KC) for i in range(nk // QT)]
    half = [(1, i, (2 * (i * QT + QT) + KC - 1) // KC) for i in range(nk // (2 * QT))]
    tiles = sorted(full + half, key=lambda t: t[2])
    attn, attn_low, linv, p = attn_fwd(q, k, vt, parity, tiles, span)

    got = from_owners(exchange(attn_low, "seq"), span).reshape(nseq, width, span)
    x_rows = inputs.reshape(tokens, width).astype(f32)
    middle = (
        x_rows
        + jnp.einsum("nht,hd->ntd", got, w_out, preferred_element_type=f32).reshape(tokens, width)
        + out_bias
    )
    h2 = layer_norm(middle, ln2_gain, ln2_bias).astype(bf16)

    h2, da, pick = lax.optimization_barrier((h2, da, pick))
    rows = lax.optimization_barrier(to_experts(h2))
    z = jnp.dot(rows, up, preferred_element_type=f32) + up_bias
    phi = 0.5 * (1.0 + lax.erf(z * (1.0 / math.sqrt(2.0))))
    hidden = (z * phi).astype(bf16)
    slope = phi + z * jnp.exp(-0.5 * z * z) * (1.0 / math.sqrt(2.0 * math.pi))
    dz = (da * slope).astype(bf16)
    dh2 = lax.dot_general(dz, up, (((1,), (1,)), ((), ())), preferred_element_type=f32)
    back = exchange_exp(dh2.astype(bf16))
    shares = expert_sums(rows, dy, dz, hidden)
    y = jnp.dot(hidden, down, preferred_element_type=f32) + down_bias[0]
    back, shares, y = lax.optimization_barrier((back, shares, y.astype(bf16)))

    grad_middle, branch, do_home, small2 = pull(
        back, pick, grad_rows, middle, row(ln2_gain), w_out, span
    )
    do = exchange(do_home, "seq")
    low_rows = got.transpose(0, 2, 1).reshape(tokens, width)
    grad_w_out = lax.dot_general(
        low_rows, branch, (((0,), (0,)), ((), ())), preferred_element_type=f32
    ).astype(bf16)
    small2 = jnp.pad(small2, ((0, 13), (0, 0))).astype(bf16)
    out_rows = width // cycle
    cut = -(-out_rows // 32) * 16
    do, grad_w_out, small2, shares = lax.optimization_barrier((do, grad_w_out, small2, shares))
    shares = lax.psum_scatter(
        shares.reshape(-1, width), "seq", scatter_dimension=0, tiled=True
    )
    w_out_part = jnp.concatenate(
        [
            grad_w_out.reshape(cycle, width // cycle, width),
            jnp.broadcast_to(small2[None], (cycle, 16, width)),
        ],
        axis=1,
    )
    w_out_part = jnp.sum(exchange(w_out_part, "seq"), axis=0, dtype=f32)
    small2 = w_out_part[out_rows : out_rows + 8]
    w_out_part = w_out_part[:out_rows].astype(bf16)

    slot_of = {t[:2]: j for j, t in enumerate(tiles)}
    dq_half, sums_mine, sums_other = attn_bwd(
        1, q, do, attn, linv, kt, v, p, parity, half, [slot_of[t[:2]] for t in half], span
    )
    sums = (sums_mine + swap(sums_other, "seq", 1).astype(f32)).astype(bf16)
    part_half = jnp.concatenate([dq_half, sums], axis=1)
    home_half = exchange(part_half, "seq")
    packed = pack(part_half, h1, parity, True, w_out_part[:cut], small2)
    both = jnp.concatenate([packed, y.reshape(experts, cap, width)], axis=1)
    both, late = lax.optimization_barrier((both, do))
    both = [both[0]] + [swap(both[d], "exp", d) for d in range(1, experts)]
    count = packed.shape[1]
    sum_half = sum(part[:count].astype(f32) for part in both).astype(bf16)
    y_back = jnp.concatenate([part[count:] for part in both])
    part_full = attn_bwd(
        0, q, late, attn, linv, kt, v, p, parity, full, [slot_of[t[:2]] for t in full], span
    )[0]
    part_full, home_half, sum_half = lax.optimization_barrier((part_full, home_half, sum_half))

    home_full = exchange(part_full, "seq")
    sum_full = sum_exp(pack(part_full, h1, parity, False, w_out_part[cut:], jnp.zeros_like(small2)))
    halves = lax.all_gather(sum_half, ("seq", "exp")).reshape(cycle, -1, width)
    sum_full, home_full = lax.optimization_barrier((sum_full, home_full))
    input_grad = home(
        home_full,
        home_half,
        w_qkv,
        inputs,
        row(ln1_gain),
        grad_middle.reshape(nseq, span, width),
    )
    output = middle + jnp.dot(pick, y_back, preferred_element_type=f32)
    output = output.astype(bf16).reshape(nseq, span, width)
    shares = shares.astype(f32)
    down_share = lax.dynamic_slice_in_dim(
        shares[2 * share + 16], me * (width // cycle), width // cycle, 0
    )
    expert_grads = (
        shares[:share].T[None],
        shares[2 * share : 2 * share + 1, :share],
        shares[share : 2 * share][None],
        down_share[None],
    )
    column, input_grad = lax.optimization_barrier((gather_exp(sum_full), input_grad))
    fulls, (output, expert_grads) = gather_seq(column, (output, expert_grads))
    grad_w_qkv, grad_w_out, small = build(
        halves, fulls, cut, w_qkv.T, row(ln1_gain), row(ln1_bias), nseq
    )
    return (
        output,
        input_grad,
        small[0],
        small[1],
        grad_w_qkv,
        small[2],
        small[3],
        grad_w_out,
        small[4],
        small[5],
        small[6],
        *expert_grads,
    )


def solution(mesh):
    in_specs = (
        P("exp", "seq", None),
        P("exp", "seq"),
        P(),
        P(),
        P(),
        P(),
        P(),
        P(),
        P(),
        P(),
        P(),
        P(),
        P(),
        P("exp", None, None),
        P("exp", None),
        P("exp", None, None),
        P("exp", None),
        P("exp", "seq", None),
    )
    out_specs = (
        P("exp", "seq", None),
        P("exp", "seq", None),
        P(),
        P(),
        P(),
        P(),
        P(),
        P(),
        P(),
        P(),
        P(),
        P("exp", None, "seq"),
        P("exp", "seq"),
        P("exp", "seq", None),
        P("exp", "seq"),
    )
    return jax.shard_map(local, mesh=mesh, in_specs=in_specs, out_specs=out_specs, check_vma=False)
```

```python
from functools import partial
import math

import jax
import jax.numpy as jnp
from jax import lax
from jax.experimental import pallas as pl
from jax.experimental.pallas import tpu as pltpu
from jax.sharding import PartitionSpec as P

HEADS = 12
HEAD_DIM = 64
f32 = jnp.float32
bf16 = jnp.bfloat16

norm_eps = 1e-05
logit_scale = 0.125
masked_score = -1e30
LOG2E = math.log2(math.e)

QT = 512
KC = 1024
SUB = 256
SUBF = 512
VMEM = 56 * 2**20


def rows_of(start, size):
    return pl.ds(pl.multiple_of(start, size), size)


def load_tile(ref, kind, t, span):
    nf, nh = QT // span, 2 * QT // span

    def full():
        return jnp.concatenate([ref[t * nf + j, :, :span] for j in range(nf)], axis=-1)

    def half(t):
        return jnp.concatenate([ref[t * nh + j, :, span:] for j in range(nh)], axis=-1)

    if isinstance(kind, int):
        return half(t) if kind else full()
    return jnp.where(kind == 0, full(), half(jnp.minimum(t, ref.shape[0] // nh - 1)))


def tile_places(kind, t, parity, span):
    col = lax.broadcasted_iota(jnp.int32, (1, QT), 1)
    at = t * QT + col
    block = lax.div(at, span // 2)
    j = at - block * (span // 2)
    quarter = span // 4
    outer = jnp.where(j >= quarter, j + 2 * quarter, j)
    half = block * span + jnp.where(parity == 0, outer, j + quarter)
    return jnp.where(kind == 0, at, half)


def loop(low, high, do):
    def step(c, _):
        do(c)
        return 0

    lax.fori_loop(low, high, step, 0)


def fwd_kernel(
    span,
    n_ref,
    kind_ref,
    tile_ref,
    par_ref,
    q_ref,
    k_ref,
    vt_ref,
    o_ref,
    low_ref,
    linv_ref,
    p_hbm,
    s0,
    s1,
    p0,
    p1,
    m0,
    m1,
    acc_scr,
    l_scr,
    sem0,
    sem1,
):
    i = pl.program_id(0)
    last = pl.num_programs(0) - 1
    before = jnp.maximum(i - 1, 0)
    n1 = n_ref[i]
    n2 = n_ref[before]
    unit1 = kind_ref[i]
    unit2 = kind_ref[before]

    def work(c1, c2, masked, now, old, q, place):
        s_now, m_now = now
        s_old, p_old, m_old = old
        if c1 is not None:
            m = m_now[...]
        if c2 is not None:
            top = jnp.max(m_old[...], axis=0, keepdims=True) * (logit_scale * LOG2E)
            l = l_scr[...]
            o = acc_scr[...]
        for j in range(KC // SUBF):
            if c1 is not None:
                off = c1 * KC + j * SUBF
                s = jnp.dot(k_ref[rows_of(off, SUBF), :], q, preferred_element_type=f32)
                if masked:
                    key = lax.broadcasted_iota(jnp.int32, (SUBF, QT), 0)
                    s = jnp.where(key <= place - off, s, masked_score)
                s_now[rows_of(off, SUBF), :] = s
                m = jnp.maximum(m, jnp.max(s.reshape(SUBF // 8, 8, QT), axis=0))
            if c2 is not None:
                off = c2 * KC + j * SUBF
                s = s_old[rows_of(off, SUBF), :]
                p = jnp.exp2(s * (logit_scale * LOG2E) - top)
                l = l + jnp.sum(p.reshape(SUBF // 8, 8, QT), axis=0)
                low = p.astype(bf16)
                p_old[rows_of(off, SUBF), :] = low
                o = o + jnp.dot(
                    vt_ref[unit2, :, rows_of(off, SUBF)], low, preferred_element_type=f32
                )
        if c1 is not None:
            m_now[...] = m
        if c2 is not None:
            l_scr[...] = l
            acc_scr[...] = o

    def send(c, p_scr, sem):
        part = rows_of(c * KC, KC)
        pltpu.make_async_copy(p_scr.at[part], p_hbm.at[before, part], sem).start()

    def drain(count, p_scr, sem):
        def wait(c):
            part = pl.ds(0, KC)
            pltpu.make_async_copy(p_scr.at[part], p_hbm.at[0, part], sem).wait()

        loop(0, count, wait)

    @pl.when(i >= 1)
    def _():
        l_scr[...] = jnp.zeros_like(l_scr)
        acc_scr[...] = jnp.zeros_like(acc_scr)

    slots = ((s0, p0, m0, sem0), (s1, p1, m1, sem1))
    for turn in (0, 1):
        s_now, p_now, m_now, sem_now = slots[turn]
        s_old, p_old, m_old, sem_old = slots[1 - turn]

        @pl.when(lax.rem(i, 2) == turn)
        def _(s_now=s_now, p_now=p_now, m_now=m_now, sem_now=sem_now, s_old=s_old, p_old=p_old, m_old=m_old, sem_old=sem_old, turn=turn):
            q = load_tile(q_ref, unit1, tile_ref[i], span)
            none = jnp.zeros_like(q)
            q = jnp.concatenate(
                [jnp.where(unit1 == 0, q, none), jnp.where(unit1 == 0, none, q)], axis=0
            )
            place = tile_places(unit1, tile_ref[i], par_ref[0], span)
            m_now[...] = jnp.full((8, QT), -jnp.inf, f32)

            @pl.when(i >= 3)
            def _():
                drain(n_ref[jnp.maximum(i - 3, 0)], p_old, sem_old)

            def go(c1, c2, masked=False):
                work(c1, c2, masked, (s_now, m_now), (s_old, p_old, m_old), q, place)

            if turn == 0:

                @pl.when(i == 0)
                def _():
                    loop(0, n1, lambda c: go(c, None, True))

            @pl.when(jnp.logical_and(i > 0, i < last))
            def _():
                go(n1 - 1, n2 - 1, True)
                send(n2 - 1, p_old, sem_old)
                both = jnp.minimum(n1, n2) - 1

                def step(c):
                    go(c, c)
                    send(c, p_old, sem_old)

                loop(0, both, step)
                loop(both, n1 - 1, lambda c: go(c, None))

            @pl.when(i == last)
            def _():
                def step(c):
                    go(None, c)
                    send(c, p_old, sem_old)

                loop(0, n2, step)
                drain(n_ref[jnp.maximum(i - 2, 0)], p_now, sem_now)
                drain(n2, p_old, sem_old)

    @pl.when(i > 0)
    def _():
        linv = 1.0 / jnp.sum(l_scr[...], axis=0, keepdims=True)
        o = acc_scr[...] * linv
        t = tile_ref[before]
        nf, nh = QT // span, 2 * QT // span
        for count, width, start, unit in ((nf, span, 0, 0), (nh, span // 2, span, 1)):

            @pl.when(unit2 == unit)
            def _(count=count, width=width, start=start):
                for j in range(count):
                    here = slice(j * width, (j + 1) * width)
                    there = pl.ds(start, width)
                    o_ref[t * count + j, :, there] = o[:, here]
                    low_ref[t * count + j, :, there] = o[:, here].astype(bf16)
                    linv_ref[t * count + j, :, there] = linv[:, here]


def table(values):
    return jnp.array(values, jnp.int32)


def pair_units(tiles):
    return sum(t[2] for t in tiles) * KC * QT


def whole(x):
    zeros = (0,) * len(x.shape)
    return pl.BlockSpec(x.shape, lambda *_: zeros)


def attn_fwd(q, k, vt, parity, tiles, span):
    nk = k.shape[0]
    steps = len(tiles)
    listed = tiles + [(tiles[-1][0], tiles[-1][1], 0)]
    linv = jax.ShapeDtypeStruct((q.shape[0], 1, q.shape[2]), f32)
    o = jax.ShapeDtypeStruct(q.shape, f32)
    work = pair_units(tiles)
    return pl.pallas_call(
        partial(fwd_kernel, span),
        name="attn_fwd",
        grid_spec=pltpu.PrefetchScalarGridSpec(
            num_scalar_prefetch=4,
            grid=(steps + 1,),
            in_specs=[whole(q), whole(k), whole(vt)],
            out_specs=[whole(q), whole(q), whole(linv), pl.BlockSpec(memory_space=pl.ANY)],
            scratch_shapes=[
                pltpu.VMEM((nk, QT), f32),
                pltpu.VMEM((nk, QT), f32),
                pltpu.VMEM((nk, QT), bf16),
                pltpu.VMEM((nk, QT), bf16),
                pltpu.VMEM((8, QT), f32),
                pltpu.VMEM((8, QT), f32),
                pltpu.VMEM((HEAD_DIM, QT), f32),
                pltpu.VMEM((8, QT), f32),
                pltpu.SemaphoreType.DMA,
                pltpu.SemaphoreType.DMA,
            ],
        ),
        out_shape=[
            o,
            jax.ShapeDtypeStruct(q.shape, bf16),
            linv,
            jax.ShapeDtypeStruct((steps, nk, QT), bf16),
        ],
        compiler_params=pltpu.CompilerParams(vmem_limit_bytes=VMEM),
        cost_estimate=pl.CostEstimate(
            flops=work * 1024, bytes_accessed=work * 2, transcendentals=work
        ),
    )(
        table([t[2] for t in listed]),
        table([t[0] for t in listed]),
        table([t[1] for t in listed]),
        parity.reshape(1),
        q,
        k,
        vt,
    )


def bwd_kernel(
    unit,
    span,
    qt,
    n_ref,
    tile_ref,
    slot_ref,
    turn_ref,
    par_ref,
    q_ref,
    do_ref,
    o_ref,
    linv_ref,
    kt_ref,
    v_ref,
    p_hbm,
    *refs,
):
    outs = refs[:-10]
    p_scr, dp0, dp1, q_scr, do_scr, de_scr, dq_scr, dk_scr, dv_scr, sem = refs[-10:]
    dps = (dp0, dp1)
    i = pl.program_id(0)
    last = pl.num_programs(0) - 1
    a = lax.rem(i, 2)
    b = 1 - a
    before = jnp.maximum(i - 1, 0)
    n1 = n_ref[i]
    n2 = n_ref[before]
    turn1 = turn_ref[i]
    turn2 = turn_ref[before]
    devices = kt_ref.shape[2] // span
    cuts = qt // QT
    width = span // 2 if unit else span

    def tile(ref):
        count = qt // width
        return jnp.concatenate([ref[tile_ref[i] * count + j] for j in range(count)], axis=-1)

    def fetch(t, slot):
        def start(c):
            part = rows_of(c * KC, KC)
            for s in range(cuts):
                there = p_scr.at[slot, part, pl.ds(s * QT, QT)]
                pltpu.make_async_copy(
                    p_hbm.at[slot_ref[t * cuts + s], part], there, sem.at[slot]
                ).start()

        loop(0, n_ref[t], start)

    def work(c1, dp_now, c2, slot, dp_old):
        if c1 is not None:
            do_now = do_scr[a]
        if c2 is not None:
            query = q_scr[slot]
            dot = do_scr[slot, unit * HEAD_DIM : (unit + 1) * HEAD_DIM, :]
            delta = de_scr[slot]
            dq = dq_scr[...]
        for j in range(KC // SUB):
            here = pl.ds(j * SUB, SUB)
            if c1 is not None:
                dp_now[here, :] = jnp.dot(
                    v_ref[rows_of(c1 * KC + j * SUB, SUB), :],
                    do_now,
                    preferred_element_type=f32,
                )
            if c2 is not None:
                keys = rows_of(c2 * KC + j * SUB, SUB)
                p = p_scr[slot, keys, :]
                ds = (p.astype(f32) * (dp_old[here, :] - delta)).astype(bf16)
                dv_scr[:, keys] += lax.dot_general(
                    dot, p, (((1,), (1,)), ((), ())), preferred_element_type=f32
                )
                dk_scr[:, keys] += lax.dot_general(
                    query, ds, (((1,), (1,)), ((), ())), preferred_element_type=f32
                )
                dq = dq + jnp.dot(kt_ref[0, :, keys], ds, preferred_element_type=f32)
        if c2 is not None:
            dq_scr[...] = dq

    def by_turn(turn, do):
        for t in (0, 1):

            @pl.when(lax.rem(turn, 2) == t)
            def _(t=t):
                do(dps[t], dps[1 - t])

    def load():
        scaled = tile(do_ref).astype(f32) * tile(linv_ref)
        de_scr[a] = jnp.sum(scaled * tile(o_ref), axis=0, keepdims=True)
        do_scr[a, unit * HEAD_DIM : (unit + 1) * HEAD_DIM, :] = scaled.astype(bf16)
        q_scr[a] = tile(q_ref)

    @pl.when(i == 0)
    def _():
        do_scr[...] = jnp.zeros_like(do_scr)
        dk_scr[...] = jnp.zeros_like(dk_scr)
        dv_scr[...] = jnp.zeros_like(dv_scr)
        dq_scr[...] = jnp.zeros_like(dq_scr)
        fetch(0, 0)
        load()
        work(0, dps[0], None, None, None)

    @pl.when(jnp.logical_and(i > 0, i < last))
    def _():
        load()

        def step(now, other):
            work(0, now, n2 - 1, b, other)

        by_turn(turn1, step)

    @pl.when(i == last)
    def _():
        by_turn(n2 - 1 + turn2, lambda now, other: work(None, None, n2 - 1, b, now))

    @pl.when(i > 0)
    def _():
        dq = (dq_scr[...] * logit_scale).astype(bf16)
        t = tile_ref[before]
        count = qt // width
        for j in range(count):
            outs[0][t * count + j, :HEAD_DIM, :width] = dq[:, j * width : (j + 1) * width]
        dq_scr[...] = jnp.zeros_like(dq_scr)

    @pl.when(i < last)
    def _():
        def wait(c):
            part = pl.ds(0, KC)
            pltpu.make_async_copy(p_scr.at[a, part], p_scr.at[a, part], sem.at[a]).wait()

        loop(0, n1, wait)

        @pl.when(i + 1 < last)
        def _():
            fetch(i + 1, b)

        def step(c):
            def both(now, other):
                work(c + 1, other, c, a, now)

            by_turn(c + turn1, both)

        loop(0, n1 - 1, step)

    @pl.when(i == last)
    def _():
        quarter = span // 4
        for d in range(devices):
            keys = pl.ds(d * span, span)
            dk = dk_scr[:, keys] * logit_scale
            dv = dv_scr[:, keys]
            if not unit:
                outs[0][d, HEAD_DIM : 2 * HEAD_DIM, :span] = dk.astype(bf16)
                outs[0][d, 2 * HEAD_DIM :, :span] = dv.astype(bf16)
            else:
                both = jnp.concatenate([dk, dv], axis=0)
                outer = jnp.concatenate([both[:, :quarter], both[:, 3 * quarter :]], axis=1)
                inner = both[:, quarter : 3 * quarter]
                even = par_ref[0] == 0
                outs[1][d] = jnp.where(even, outer, inner)
                outs[2][d] = jnp.where(even, inner, outer).astype(bf16)


def attn_bwd(unit, q, do, o, linv, kt, v, p, parity, tiles, slots, span):
    nk = kt.shape[2]
    steps = len(tiles)
    qt = KC if unit == 0 else QT
    width = span // 2 if unit else span

    def columns(x):
        return pl.BlockSpec((*x.shape[:2], width), lambda *_: (0, 0, 2 if unit else 0))

    listed = tiles + [(unit, tiles[-1][1], 0)]
    turns = [0]
    for t in tiles:
        turns.append((turns[-1] + t[2]) % 2)
    devices = nk // span
    if unit:
        outs = [
            jax.ShapeDtypeStruct((devices, HEAD_DIM, span // 2), bf16),
            jax.ShapeDtypeStruct((devices, 2 * HEAD_DIM, span // 2), f32),
            jax.ShapeDtypeStruct((devices, 2 * HEAD_DIM, span // 2), bf16),
        ]
    else:
        outs = [jax.ShapeDtypeStruct((devices, 3 * HEAD_DIM, span), bf16)]
    work = pair_units(tiles) * (qt // QT)
    return pl.pallas_call(
        partial(bwd_kernel, unit, span, qt),
        name="attn_bwd_half" if unit else "attn_bwd_full",
        grid_spec=pltpu.PrefetchScalarGridSpec(
            num_scalar_prefetch=5,
            grid=(steps + 1,),
            in_specs=[
                columns(q),
                columns(do),
                columns(o),
                columns(linv),
                pl.BlockSpec((1, HEAD_DIM, nk), lambda *_: (unit, 0, 0)),
                whole(v),
                pl.BlockSpec(memory_space=pl.ANY),
            ],
            out_specs=[whole(x) for x in outs],
            scratch_shapes=[
                pltpu.VMEM((2, nk, qt), bf16),
                pltpu.VMEM((KC, qt), f32),
                pltpu.VMEM((KC, qt), f32),
                pltpu.VMEM((2, HEAD_DIM, qt), bf16),
                pltpu.VMEM((2, 2 * HEAD_DIM, qt), bf16),
                pltpu.VMEM((2, 1, qt), f32),
                pltpu.VMEM((HEAD_DIM, qt), f32),
                pltpu.VMEM((HEAD_DIM, nk), f32),
                pltpu.VMEM((HEAD_DIM, nk), f32),
                pltpu.SemaphoreType.DMA((2,)),
            ],
        ),
        out_shape=outs,
        compiler_params=pltpu.CompilerParams(vmem_limit_bytes=VMEM),
        cost_estimate=pl.CostEstimate(
            flops=work * 2048, bytes_accessed=work * 2, transcendentals=0
        ),
    )(
        table([t[2] for t in listed]),
        table([t[1] for t in listed]),
        table(slots),
        table(turns),
        parity.reshape(1),
        q,
        do,
        o,
        linv,
        kt,
        v,
        p,
    )


def pick_quarters(x, parity, axis):
    q = x.shape[axis] // 4

    def cut(low, high):
        return x[low * q : high * q] if axis == 0 else x[:, low * q : high * q]

    outer = jnp.concatenate([cut(0, 1), cut(3, 4)], axis=axis)
    return jnp.where(parity == 0, outer, cut(1, 3))


def prep_kernel(count, pos_ref, par_ref, *refs):
    blocks = refs[:count]
    gain_ref, shift_ref, wt_ref, bt_ref, wn_ref, bn_ref = refs[count : count + 6]
    h_ref, q_ref, kt_ref, vt_ref, k_ref, v_ref, x_scr, sem = refs[count + 6 :]
    i = pl.program_id(0)
    for j in range(count):

        @pl.when(i == max(j - 1, 0))
        def _(j=j):
            pltpu.make_async_copy(blocks[j], x_scr.at[j % 2], sem.at[j % 2]).start()

    slot = lax.rem(i, 2)
    pltpu.make_async_copy(x_scr.at[slot], x_scr.at[slot], sem.at[slot]).wait()
    _, span, width = x_scr.shape
    d = HEAD_DIM
    cuts = 2
    sub = span // cuts
    for r in range(cuts):
        here = pl.ds(r * sub, sub)
        x = x_scr[slot, here, :].astype(f32)
        x = x - jnp.mean(x, axis=-1, keepdims=True)
        spread = jnp.mean(x * x, axis=-1, keepdims=True)
        h = (x * lax.rsqrt(spread + norm_eps) * gain_ref[...] + shift_ref[...]).astype(bf16)
        h_ref[here, :] = h
        over = lax.dot_general(
            wt_ref[...], h, (((1,), (1,)), ((), ())), preferred_element_type=f32
        )
        over = (over + bt_ref[...]).astype(bf16)
        q_ref[0, :, here] = over[:d]
        half = over[3 * d : 4 * d]
        low, high = half[:, : sub // 2], half[:, sub // 2 :]
        outer, inner = (low, high) if r == 0 else (high, low)
        q_ref[0, :, pl.ds(span + r * sub // 2, sub // 2)] = jnp.where(
            par_ref[0] == 0, outer, inner
        )
        for unit in (0, 1):
            kt_ref[unit, :, here] = over[(3 * unit + 1) * d : (3 * unit + 2) * d]
            vt_ref[unit, :, here] = over[(3 * unit + 2) * d : (3 * unit + 3) * d]
        flat = jnp.dot(h, wn_ref[...], preferred_element_type=f32) + bn_ref[...]
        flat = flat.astype(bf16)
        k_ref[here, :] = flat[:, : 2 * d]
        v_ref[here, :] = flat[:, 2 * d :]


def prep(blocks, pos, parity, gain, shift, wt, bt, wn, bn):
    count = len(blocks)
    span, width = blocks[0].shape
    devices = lax.axis_size("seq")
    nk = devices * span
    d = HEAD_DIM
    shapes = [
        ((nk, width), (span, width), lambda i, s, _: (s[i], 0)),
        ((devices, d, 3 * span // 2), (1, d, 3 * span // 2), lambda i, s, _: (s[i], 0, 0)),
        ((2, d, nk), (2, d, span), lambda i, s, _: (0, 0, s[i])),
        ((2, d, nk), (2, d, span), lambda i, s, _: (0, 0, s[i])),
        ((nk, 2 * d), (span, 2 * d), lambda i, s, _: (s[i], 0)),
        ((nk, 2 * d), (span, 2 * d), lambda i, s, _: (s[i], 0)),
    ]
    params = (gain, shift, wt, bt, wn, bn)
    return pl.pallas_call(
        partial(prep_kernel, count),
        name="prep",
        grid_spec=pltpu.PrefetchScalarGridSpec(
            num_scalar_prefetch=2,
            grid=(count,),
            in_specs=[pl.BlockSpec(memory_space=pl.ANY)] * count + [whole(x) for x in params],
            out_specs=[pl.BlockSpec(block, index) for _, block, index in shapes],
            scratch_shapes=[pltpu.VMEM((2, span, width), bf16), pltpu.SemaphoreType.DMA((2,))],
        ),
        out_shape=[jax.ShapeDtypeStruct(shape, bf16) for shape, _, _ in shapes],
        compiler_params=pltpu.CompilerParams(vmem_limit_bytes=VMEM),
        cost_estimate=pl.CostEstimate(
            flops=1, bytes_accessed=1, transcendentals=0
        ),
    )(pos, parity.reshape(1), *blocks, *params)


def pull_kernel(
    back_ref, pick_ref, grad_ref, mid_ref, gain_ref, w_ref, gm_ref, br_ref, do_ref, small_ref
):
    tokens = grad_ref.shape[0]
    gain = gain_ref[...]
    totals = [0.0, 0.0, 0.0]
    cut = tokens // 4
    for r in range(4):
        here = pl.ds(r * cut, cut)
        dh = jnp.dot(pick_ref[here, :], back_ref[...], preferred_element_type=f32)
        x = mid_ref[here, :]
        x = x - jnp.mean(x, axis=-1, keepdims=True)
        inv = lax.rsqrt(jnp.mean(x * x, axis=-1, keepdims=True) + norm_eps)
        x = x * inv
        d = dh * gain
        dx = inv * (
            d - jnp.mean(d, axis=-1, keepdims=True) - x * jnp.mean(d * x, axis=-1, keepdims=True)
        )
        gm = grad_ref[here, :].astype(f32) + dx
        branch = gm.astype(bf16)
        gm_ref[here, :] = gm
        br_ref[here, :] = branch
        for at, part in enumerate((branch.astype(f32), dh * x, dh)):
            totals[at] = totals[at] + jnp.sum(part, axis=0, keepdims=True)
    for at in range(3):
        small_ref[at : at + 1] = totals[at]
    do = lax.dot_general(
        w_ref[...], br_ref[...], (((1,), (1,)), ((), ())), preferred_element_type=f32
    ).astype(bf16)
    span = do_ref.shape[2] * 2 // 3
    for u in range(do.shape[1] // span * HEADS):
        n, head = u // HEADS, u % HEADS
        part = do[head * HEAD_DIM : (head + 1) * HEAD_DIM, n * span : (n + 1) * span]
        p, role = u // 3, u % 3
        if role != 1:
            do_ref[2 * p + role // 2, :, :span] = part
        else:
            q = span // 4
            outer = jnp.concatenate([part[:, :q], part[:, 3 * q :]], axis=1)
            do_ref[2 * p, :, span:] = outer
            do_ref[2 * p + 1, :, span:] = part[:, q : 3 * q]


def pull(back, pick, grad, mid, gain, w_out, span):
    tokens, width = grad.shape
    return pl.pallas_call(
        pull_kernel,
        name="pull",
        out_shape=[
            jax.ShapeDtypeStruct((tokens, width), f32),
            jax.ShapeDtypeStruct((tokens, width), bf16),
            jax.ShapeDtypeStruct((lax.axis_size("seq"), HEAD_DIM, 3 * span // 2), bf16),
            jax.ShapeDtypeStruct((3, width), f32),
        ],
        compiler_params=pltpu.CompilerParams(vmem_limit_bytes=VMEM),
        cost_estimate=pl.CostEstimate(
            flops=4 * tokens * width * width, bytes_accessed=tokens * width * 16, transcendentals=0
        ),
    )(back, pick, grad, mid, gain, w_out)


def pack_kernel(half, at_ref, part_ref, h_ref, out_ref, small_ref, piece_ref, acc, cnt):
    i = pl.program_id(0)
    devices, rows, tokens = part_ref.shape
    stretch, width = h_ref.shape[0] // devices, h_ref.shape[1]
    g = jnp.zeros((rows, width), f32)
    count = jnp.zeros((8, rows), f32)
    ones = jnp.ones((8, tokens), bf16)
    for d in range(devices):
        part = part_ref[d]
        h = h_ref[pl.ds(d * stretch, stretch), :]
        if half:
            h = pick_quarters(h, at_ref[1], 0)
        g += jnp.dot(part, h, preferred_element_type=f32)
        count += lax.dot_general(
            ones, part, (((1,), (1,)), ((), ())), preferred_element_type=f32
        )

    @pl.when(i == 0)
    def _():
        acc[...] = g
        cnt[...] = count

    @pl.when(i > 0)
    def _():
        acc[...] += g
        cnt[...] += count

    @pl.when(i == pl.num_programs(0) - 1)
    def _():
        nexp, share, _ = piece_ref.shape
        line = jnp.concatenate([cnt[...], jnp.zeros((8, width - rows), f32)], axis=1)
        line = jnp.concatenate([line, small_ref[...]], axis=0)
        filled = rows + out_ref.shape[0] + 16
        parts = [acc[...].astype(bf16), out_ref[...], line.astype(bf16)]
        if nexp * share > filled:
            parts.append(jnp.zeros((nexp * share - filled, width), bf16))
        piece = jnp.concatenate(parts, axis=0)
        for e in range(nexp):
            piece_ref[at_ref[0] ^ e] = piece[e * share : (e + 1) * share]


def pack(part, h1, parity, half, out_rows, small):
    devices, rows, _ = part.shape
    nk, width = h1.shape
    nexp = lax.axis_size("exp")
    filled = rows + out_rows.shape[0] + 16
    share = -(-filled // (16 * nexp)) * 16
    steps = 4
    return pl.pallas_call(
        partial(pack_kernel, half),
        name="pack_half" if half else "pack_full",
        grid_spec=pltpu.PrefetchScalarGridSpec(
            num_scalar_prefetch=1,
            grid=(steps,),
            in_specs=[
                pl.BlockSpec(
                    (devices // steps, rows, nk // devices // (2 if half else 1)),
                    lambda i, _: (i, 0, 0),
                ),
                pl.BlockSpec((nk // steps, width), lambda i, _: (i, 0)),
                whole(out_rows),
                whole(small),
            ],
            out_specs=pl.BlockSpec((nexp, share, width), lambda i, _: (0, 0, 0)),
            scratch_shapes=[pltpu.VMEM((rows, width), f32), pltpu.VMEM((8, rows), f32)],
        ),
        out_shape=jax.ShapeDtypeStruct((nexp, share, width), bf16),
        compiler_params=pltpu.CompilerParams(vmem_limit_bytes=VMEM),
        cost_estimate=pl.CostEstimate(flops=1, bytes_accessed=1, transcendentals=0),
    )(jnp.stack([lax.axis_index("exp"), parity]), part, h1, out_rows, small)


def home_kernel(nseq, span, full_ref, half_ref, w_ref, x_ref, gain_ref, gm_ref, dx_ref, u_scr):
    pairs = full_ref.shape[0] // 2
    quarter = span // 4
    for n in range(nseq):
        here = pairs // nseq
        for j in range(here):
            p = n * here + j
            outer, inner = half_ref[2 * p], half_ref[2 * p + 1]
            mid = jnp.concatenate([outer[:, :quarter], inner, outer[:, quarter:]], axis=1)
            for role, unit in enumerate((full_ref[2 * p], mid, full_ref[2 * p + 1])):
                for c in range(3):
                    at = c * HEADS + 3 * j + role
                    u_scr[pl.ds(at * HEAD_DIM, HEAD_DIM), :] = unit[
                        c * HEAD_DIM : (c + 1) * HEAD_DIM
                    ]
        dh = jnp.dot(w_ref[...], u_scr[...], preferred_element_type=f32).T
        x = x_ref[n].astype(f32)
        x = x - jnp.mean(x, axis=-1, keepdims=True)
        inv = lax.rsqrt(jnp.mean(x * x, axis=-1, keepdims=True) + norm_eps)
        x = x * inv
        d = dh * gain_ref[...]
        dx_ref[n] = gm_ref[n] + inv * (
            d - jnp.mean(d, axis=-1, keepdims=True) - x * jnp.mean(d * x, axis=-1, keepdims=True)
        )


def home(full, half, w_qkv, x, gain, grad_middle):
    nseq, span, width = x.shape
    return pl.pallas_call(
        partial(home_kernel, nseq, span),
        name="home",
        out_shape=jax.ShapeDtypeStruct((nseq, span, width), f32),
        scratch_shapes=[pltpu.VMEM((3 * width, span), bf16)],
        compiler_params=pltpu.CompilerParams(vmem_limit_bytes=VMEM),
        cost_estimate=pl.CostEstimate(
            flops=1, bytes_accessed=1, transcendentals=0
        ),
    )(full, half, w_qkv, x, gain, grad_middle)


def build_kernel(nseq, nexp, devices, cut, at_ref, *refs):
    halves, fulls = refs[0], refs[1 : 1 + devices]
    w_ref, gain_ref, shift_ref, g_ref, out_ref, small_ref, half, full, acc, sem = refs[1 + devices :]
    me, z = at_ref[0], at_ref[1]
    c = pl.program_id(0)
    d = HEAD_DIM
    rows = 3 * d
    width = g_ref.shape[0]
    out_rows = width // devices

    @pl.when(c == 0)
    def _():
        for j in range(devices):
            for e in range(nexp):
                for block, got in ((halves.at[j], half), (fulls[j], full)):
                    share = got.shape[1] // nexp
                    pltpu.make_async_copy(
                        block.at[pl.ds(pl.multiple_of((z ^ e) * share, 16), share)],
                        got.at[j, pl.ds(e * share, share)],
                        sem,
                    ).start()
        acc[...] = jnp.zeros_like(acc)
        pltpu.make_async_copy(half, half, sem).wait()
        pltpu.make_async_copy(full, full, sem).wait()

    def from_unit(u, at, lanes):
        p, role = u // 3, u % 3
        if role != 1:
            return full[me ^ (2 * p + role // 2), at, lanes].astype(f32)
        return half[2 * p, at, lanes].astype(f32) + half[2 * p + 1, at, lanes].astype(f32)

    def unit_rows(u):
        return from_unit(u, rows_of(c * d, d), slice(None))

    def unit_sums(u):
        line = rows + (cut if u % 3 == 1 else out_rows - cut)
        line = from_unit(u, pl.ds(line, 16), pl.ds(0, rows))[:1]
        return jnp.where(c == 0, line[:, :d], jnp.where(c == 1, line[:, d : 2 * d], line[:, 2 * d :]))

    for two in range(HEADS // 2):
        heads = (2 * two, 2 * two + 1)
        grads = [sum(unit_rows(n * HEADS + h) for n in range(nseq)) for h in heads]
        sums = [sum(unit_sums(n * HEADS + h) for n in range(nseq)) for h in heads]
        at = pl.ds(two * 2 * d, 2 * d)
        block = jnp.concatenate(grads, axis=0)
        total = jnp.concatenate(sums, axis=1)
        g_ref[:, at] = block.T
        w = w_ref[at, :]
        gained = w.astype(f32) * block
        acc[:8] += jnp.sum(gained.reshape(2 * d // 8, 8, width), axis=0)
        acc[8:16] += jnp.dot(
            jnp.broadcast_to(total, (8, 2 * d)).astype(bf16), w, preferred_element_type=f32
        )

        acc[pl.ds(16 + 8 * c, 1), at] = total
    @pl.when(c == 2)
    def _():
        gained = jnp.sum(acc[:8], axis=0, keepdims=True)
        shifted = acc[8:9]
        small_ref[0:1] = (gained - shift_ref[...] * shifted) / gain_ref[...]
        small_ref[1:2] = shifted
        small_ref[2:3] = acc[16:17]
        small_ref[3:4] = acc[32:33]
        small_ref[4:7] = half[0, pl.ds(rows + cut, 16), :].astype(f32)[8:11]
        small_ref[7:8] = jnp.zeros_like(shifted)
        for i in range(devices):
            out_ref[pl.ds(i * out_rows, cut), :] = half[i, pl.ds(rows, cut), :].astype(f32)
            out_ref[pl.ds(i * out_rows + cut, out_rows - cut), :] = full[
                me ^ i, pl.ds(rows, out_rows - cut), :
            ].astype(f32)


def build(halves, fulls, cut, w_rows, gain, shift, nseq):
    width = w_rows.shape[1]
    devices = len(fulls)
    nexp = lax.axis_size("exp")
    at = jnp.stack([lax.axis_index("seq"), lax.axis_index("exp")])
    away = pl.BlockSpec(memory_space=pl.ANY)
    return pl.pallas_call(
        partial(build_kernel, nseq, nexp, devices, cut),
        name="build",
        grid=(3,),
        in_specs=[pl.BlockSpec(memory_space=pltpu.SMEM)]
        + [away] * (1 + devices)
        + [pl.BlockSpec((width, width), lambda c: (c, 0)), whole(gain), whole(shift)],
        out_specs=[
            pl.BlockSpec((width, width), lambda c: (0, c)),
            pl.BlockSpec((width, width), lambda c: (0, 0)),
            pl.BlockSpec((8, width), lambda c: (0, 0)),
        ],
        out_shape=[
            jax.ShapeDtypeStruct((width, 3 * width), f32),
            jax.ShapeDtypeStruct((width, width), f32),
            jax.ShapeDtypeStruct((8, width), f32),
        ],
        scratch_shapes=[
            pltpu.VMEM(halves.shape, bf16),
            pltpu.VMEM((devices, *fulls[0].shape), bf16),
            pltpu.VMEM((40, width), f32),
            pltpu.SemaphoreType.DMA,
        ],
        compiler_params=pltpu.CompilerParams(vmem_limit_bytes=VMEM),
        cost_estimate=pl.CostEstimate(
            flops=0, bytes_accessed=18 * width * width, transcendentals=0
        ),
    )(at, halves, *fulls, w_rows, gain, shift)


def expert_sums_kernel(rows_ref, dy_ref, dz_ref, hid_ref, out_ref):
    contract = (((0,), (0,)), ((), ()))
    dz = dz_ref[...]
    share = dz.shape[1]
    dy = dy_ref[...]
    out_ref[0, :share] = lax.dot_general(
        dz, rows_ref[...], contract, preferred_element_type=f32
    ).astype(bf16)
    out_ref[0, share : 2 * share] = lax.dot_general(
        hid_ref[...], dy, contract, preferred_element_type=f32
    ).astype(bf16)
    ones = jnp.ones((16, dz.shape[0]), bf16)
    up = jnp.dot(ones, dz, preferred_element_type=f32).astype(bf16)
    fill = jnp.zeros((16, dy.shape[1] - share), bf16)
    out_ref[0, 2 * share : 2 * share + 16] = jnp.concatenate([up, fill], axis=1)
    out_ref[0, 2 * share + 16 :] = jnp.dot(ones, dy, preferred_element_type=f32).astype(bf16)


def expert_sums(rows, dy, dz, hidden):
    devices = lax.axis_size("seq")
    count, width = rows.shape
    ff = dz.shape[1]
    share = ff // devices
    if share % 128:
        contract = (((0,), (0,)), ((), ()))
        up = lax.dot_general(dz, rows, contract, preferred_element_type=f32)
        down = lax.dot_general(hidden, dy, contract, preferred_element_type=f32)
        up_bias = jnp.pad(
            jnp.sum(dz, axis=0, dtype=f32).reshape(devices, 1, share),
            ((0, 0), (0, 15), (0, width - share)),
        )
        down_bias = jnp.broadcast_to(jnp.sum(dy, axis=0, dtype=f32), (devices, 16, width))
        return jnp.concatenate(
            [up.reshape(devices, share, width), down.reshape(devices, share, width), up_bias, down_bias],
            axis=1,
        ).astype(bf16)
    total = 2 * share + 32
    return pl.pallas_call(
        expert_sums_kernel,
        name="expert_sums",
        grid=(devices,),
        in_specs=[
            pl.BlockSpec((count, width), lambda j: (0, 0)),
            pl.BlockSpec((count, width), lambda j: (0, 0)),
            pl.BlockSpec((count, share), lambda j: (0, j)),
            pl.BlockSpec((count, share), lambda j: (0, j)),
        ],
        out_specs=pl.BlockSpec((1, total, width), lambda j: (j, 0, 0)),
        out_shape=jax.ShapeDtypeStruct((devices, total, width), bf16),
        compiler_params=pltpu.CompilerParams(vmem_limit_bytes=VMEM),
        cost_estimate=pl.CostEstimate(
            flops=1, bytes_accessed=1, transcendentals=0
        ),
    )(rows, dy, dz, hidden)


def swap(x, axis, distance):
    return lax.ppermute(x, axis, [(i, i ^ distance) for i in range(lax.axis_size(axis))])


def gather_chips(x, beside=()):
    chips = lax.axis_size("seq") // 2
    if chips != 4:
        return [x] + [swap(x, "seq", 2 * d) for d in range(1, chips)], beside
    one, two = swap(x, "seq", 2), swap(x, "seq", 4)
    if beside:
        one, two, beside = lax.optimization_barrier((one, two, beside))
    axis = x.ndim - 2
    half = x.shape[axis] // 2
    low = swap(lax.slice_in_dim(one, 0, half, axis=axis), "seq", 4)
    high = swap(lax.slice_in_dim(two, half, 2 * half, axis=axis), "seq", 2)
    return [x, one, two, jnp.concatenate([low, high], axis=axis)], beside


def gather_seq(x, beside):
    blocks = []
    chips, beside = gather_chips(x, beside)
    for block in chips:
        blocks += [block, swap(block, "seq", 1)]
    return blocks, beside


def in_order(stack, axis):
    me = lax.axis_index(axis)
    return jnp.take(stack, me ^ lax.iota(jnp.int32, stack.shape[0]), axis=0)


def sum_exp(parts):
    total = parts[0].astype(f32)
    for d in range(1, parts.shape[0]):
        total = total + swap(parts[d], "exp", d).astype(f32)
    return total.astype(bf16)


def gather_exp(total):
    return jnp.concatenate([total] + [swap(total, "exp", d) for d in range(1, lax.axis_size("exp"))])


def layer_norm(values, gain, shift):
    centre = jnp.mean(values, axis=-1, keepdims=True)
    centered = values - centre
    spread = jnp.mean(centered * centered, axis=-1, keepdims=True)
    return centered * lax.rsqrt(spread + norm_eps) * gain + shift


def from_owners(got, span):
    quarter = span // 4
    both = got.reshape(got.shape[0] // 2, 2, *got.shape[1:])
    outer, inner = both[:, 0, ..., span:], both[:, 1, ..., span:]
    mid = jnp.concatenate([outer[..., :quarter], inner, outer[..., quarter:]], axis=-1)
    return jnp.stack([both[:, 0, ..., :span], mid, both[:, 1, ..., :span]], axis=1)


def exchange(x, axis):
    return lax.all_to_all(x, axis, split_axis=0, concat_axis=0, tiled=True)


def exchange_exp(x):
    nexp = lax.axis_size("exp")
    parts = x.reshape(nexp, x.shape[0] // nexp, x.shape[1])
    return jnp.concatenate([parts[0]] + [swap(parts[d], "exp", d) for d in range(1, nexp)])


def local(
    inputs,
    token_ids,
    hash_table,
    capacity,
    ln1_gain,
    ln1_bias,
    w_qkv,
    q_bias,
    v_bias,
    w_out,
    out_bias,
    ln2_gain,
    ln2_bias,
    up_weight,
    up_bias,
    down_weight,
    down_bias,
    out_grad,
):
    nseq, span, width = inputs.shape
    tokens = nseq * span
    cycle = lax.axis_size("seq")
    me = lax.axis_index("seq")
    parity = me % 2
    pair = me // 2
    pairs = cycle // 2
    nk = cycle * span
    assert nseq * HEADS == 3 * pairs
    up, down = up_weight[0], down_weight[0]
    ff = up.shape[1]
    share = ff // cycle
    row = lambda x: x.reshape(1, -1)

    mine = (3 * pair) // HEADS
    def of_sequence(blocks):
        return [lax.dynamic_index_in_dim(b, mine, 0, keepdims=False) for b in blocks]


    experts = capacity.shape[0]
    cap = 5 * tokens // (4 * experts)
    expert_of = jnp.take(hash_table, token_ids.reshape(tokens))
    onehot = (expert_of[:, None] == lax.iota(jnp.int32, experts)[None, :]).astype(jnp.int32)
    rank = jnp.sum(onehot * (jnp.cumsum(onehot, axis=0) - 1), axis=1)
    kept = rank < jnp.take(capacity, expert_of)
    near_expert = expert_of ^ lax.axis_index("exp")
    slot = jnp.where(kept, near_expert * cap + rank, experts * cap)
    slots = lax.iota(jnp.int32, experts * cap)
    place = (slots[:, None] == slot[None, :]).astype(bf16)
    pick = (slots[None, :] == slot[:, None]).astype(bf16)

    def to_experts(rows):
        sent = jnp.dot(place, rows, preferred_element_type=f32).astype(bf16)
        return exchange_exp(sent)

    grad_rows = out_grad.reshape(tokens, width)
    dy = to_experts(grad_rows)
    da = lax.dot_general(dy, down, (((1,), (1,)), ((), ())), preferred_element_type=f32)

    head_full = (3 * pair + 2 * parity) % HEADS
    head_half = (3 * pair + 1) % HEADS
    w_heads = w_qkv.reshape(width, 3, HEADS, HEAD_DIM)

    def of_head(x, axis):
        return jnp.stack(
            [
                lax.dynamic_index_in_dim(x, head_full, axis, keepdims=False),
                lax.dynamic_index_in_dim(x, head_half, axis, keepdims=False),
            ]
        )

    w_mine = of_head(w_heads, 2)
    qb = of_head(q_bias.reshape(HEADS, HEAD_DIM), 0)
    vb = of_head(v_bias.reshape(HEADS, HEAD_DIM), 0)
    bias = jnp.stack([qb, jnp.zeros_like(qb), vb], axis=1)
    wt = w_mine.transpose(0, 2, 3, 1).reshape(6 * HEAD_DIM, width)
    wn = w_mine[:, :, 1:].transpose(1, 2, 0, 3).reshape(width, 4 * HEAD_DIM)
    bn = row(bias[:, 1:].transpose(1, 0, 2))
    params = (row(ln1_gain), row(ln1_bias), wt, bias.reshape(-1, 1), wn, bn)
    places = me ^ lax.iota(jnp.int32, cycle)
    chips, _ = gather_chips(inputs)
    far, params, pick, place, places = lax.optimization_barrier(
        (chips[-1], params, pick, place, places)
    )
    blocks = []
    for block in chips[:-1] + [far]:
        blocks += [block, swap(block, "seq", 1)]
    h1, q, kt, vt, k, v = prep(of_sequence(blocks), places, parity, *params)

    full = [(0, i, (i * QT + QT + KC - 1) // KC) for i in range(nk // QT)]
    half = [(1, i, (2 * (i * QT + QT) + KC - 1) // KC) for i in range(nk // (2 * QT))]
    tiles = sorted(full + half, key=lambda t: t[2])
    wide = [(0, i, i + 1) for i in range(nk // KC)]
    attn, attn_low, linv, p = attn_fwd(q, k, vt, parity, tiles, span)

    got = from_owners(exchange(attn_low, "seq"), span).reshape(nseq, width, span)
    x_rows = inputs.reshape(tokens, width).astype(f32)
    middle = (
        x_rows
        + jnp.einsum("nht,hd->ntd", got, w_out, preferred_element_type=f32).reshape(tokens, width)
        + out_bias
    )
    h2 = layer_norm(middle, ln2_gain, ln2_bias).astype(bf16)

    h2, da, pick = lax.optimization_barrier((h2, da, pick))
    rows = lax.optimization_barrier(to_experts(h2))
    z = jnp.dot(rows, up, preferred_element_type=f32) + up_bias
    phi = 0.5 * (1.0 + lax.erf(z * (1.0 / math.sqrt(2.0))))
    hidden = (z * phi).astype(bf16)
    slope = phi + z * jnp.exp(-0.5 * z * z) * (1.0 / math.sqrt(2.0 * math.pi))
    dz = (da * slope).astype(bf16)
    dh2 = lax.dot_general(dz, up, (((1,), (1,)), ((), ())), preferred_element_type=f32)
    back = exchange_exp(dh2.astype(bf16))
    shares = expert_sums(rows, dy, dz, hidden)
    y = jnp.dot(hidden, down, preferred_element_type=f32) + down_bias[0]
    back, shares, y = lax.optimization_barrier((back, shares, y.astype(bf16)))

    grad_middle, branch, do_home, small2 = pull(
        back, pick, grad_rows, middle, row(ln2_gain), w_out, span
    )
    do = exchange(do_home, "seq")
    low_rows = got.transpose(0, 2, 1).reshape(tokens, width)
    grad_w_out = lax.dot_general(
        low_rows, branch, (((0,), (0,)), ((), ())), preferred_element_type=f32
    ).astype(bf16)
    small2 = jnp.pad(small2, ((0, 13), (0, 0))).astype(bf16)
    out_rows = width // cycle
    cut = -(-out_rows // 32) * 16
    do, grad_w_out, small2, shares = lax.optimization_barrier((do, grad_w_out, small2, shares))
    shares = lax.psum_scatter(
        shares.reshape(-1, width), "seq", scatter_dimension=0, tiled=True
    )
    w_out_part = jnp.concatenate(
        [
            grad_w_out.reshape(cycle, width // cycle, width),
            jnp.broadcast_to(small2[None], (cycle, 16, width)),
        ],
        axis=1,
    )
    w_out_part = jnp.sum(exchange(w_out_part, "seq"), axis=0, dtype=f32)
    small2 = w_out_part[out_rows : out_rows + 8]
    w_out_part = w_out_part[:out_rows].astype(bf16)

    slot_of = {t[:2]: j for j, t in enumerate(tiles)}
    dq_half, sums_mine, sums_other = attn_bwd(
        1, q, do, attn, linv, kt, v, p, parity, half, [slot_of[t[:2]] for t in half], span
    )
    sums = (sums_mine + swap(sums_other, "seq", 1).astype(f32)).astype(bf16)
    part_half = jnp.concatenate([dq_half, sums], axis=1)
    home_half = exchange(part_half, "seq")
    packed = pack(part_half, h1, parity, True, w_out_part[:cut], small2)
    both = jnp.concatenate([packed, y.reshape(experts, cap, width)], axis=1)
    both, late = lax.optimization_barrier((both, do))
    both = [both[0]] + [swap(both[d], "exp", d) for d in range(1, experts)]
    count = packed.shape[1]
    sum_half = sum(part[:count].astype(f32) for part in both).astype(bf16)
    y_back = jnp.concatenate([part[count:] for part in both])
    part_full = attn_bwd(
        0, q, late, attn, linv, kt, v, p, parity, wide, [slot_of[t[:2]] for t in full], span
    )[0]
    part_full, home_half, sum_half = lax.optimization_barrier((part_full, home_half, sum_half))

    packed = pack(part_full, h1, parity, False, w_out_part[cut:], jnp.zeros_like(small2))
    column_half, packed, part_full = lax.optimization_barrier(
        (gather_exp(sum_half), packed, part_full)
    )
    halves = lax.all_gather(column_half, "seq")
    home_full = exchange(part_full, "seq")
    sum_full = sum_exp(packed)
    input_grad = home(
        home_full,
        home_half,
        w_qkv,
        inputs,
        row(ln1_gain),
        grad_middle.reshape(nseq, span, width),
    )
    output = middle + jnp.dot(pick, y_back, preferred_element_type=f32)
    output = output.astype(bf16).reshape(nseq, span, width)
    shares = shares.astype(f32)
    down_share = lax.dynamic_slice_in_dim(
        shares[2 * share + 16], me * (width // cycle), width // cycle, 0
    )
    expert_grads = (
        shares[:share].T[None],
        shares[2 * share : 2 * share + 1, :share],
        shares[share : 2 * share][None],
        down_share[None],
    )
    fulls, (output, expert_grads, input_grad) = gather_seq(
        gather_exp(sum_full), (output, expert_grads, input_grad)
    )
    grad_w_qkv, grad_w_out, small = build(
        halves, fulls, cut, w_qkv.T, row(ln1_gain), row(ln1_bias), nseq
    )
    return (
        output,
        input_grad,
        small[0],
        small[1],
        grad_w_qkv,
        small[2],
        small[3],
        grad_w_out,
        small[4],
        small[5],
        small[6],
        *expert_grads,
    )


def solution(mesh):
    in_specs = (
        P("exp", "seq", None),
        P("exp", "seq"),
        P(),
        P(),
        P(),
        P(),
        P(),
        P(),
        P(),
        P(),
        P(),
        P(),
        P(),
        P("exp", None, None),
        P("exp", None),
        P("exp", None, None),
        P("exp", None),
        P("exp", "seq", None),
    )
    out_specs = (
        P("exp", "seq", None),
        P("exp", "seq", None),
        P(),
        P(),
        P(),
        P(),
        P(),
        P(),
        P(),
        P(),
        P(),
        P("exp", None, "seq"),
        P("exp", "seq"),
        P("exp", "seq", None),
        P("exp", "seq"),
    )
    return jax.shard_map(local, mesh=mesh, in_specs=in_specs, out_specs=out_specs, check_vma=False)
```

```python
from functools import partial
import math

import jax
import jax.numpy as jnp
from jax import lax
from jax.experimental import pallas as pl
from jax.experimental.pallas import tpu as pltpu
from jax.sharding import PartitionSpec as P

HEADS = 12
HEAD_DIM = 64
f32 = jnp.float32
bf16 = jnp.bfloat16

norm_eps = 1e-05
logit_scale = 0.125
masked_score = -1e30
LOG2E = math.log2(math.e)

QT = 512
KC = 1024
SUB = 256
SUBF = 512
VMEM = 56 * 2**20


def rows_of(start, size):
    return pl.ds(pl.multiple_of(start, size), size)


def load_tile(ref, kind, t, span):
    nf, nh = QT // span, 2 * QT // span

    def full():
        return jnp.concatenate([ref[t * nf + j, :, :span] for j in range(nf)], axis=-1)

    def half(t):
        return jnp.concatenate([ref[t * nh + j, :, span:] for j in range(nh)], axis=-1)

    if isinstance(kind, int):
        return half(t) if kind else full()
    return jnp.where(kind == 0, full(), half(jnp.minimum(t, ref.shape[0] // nh - 1)))


def tile_places(kind, t, parity, span):
    col = lax.broadcasted_iota(jnp.int32, (1, QT), 1)
    at = t * QT + col
    block = lax.div(at, span // 2)
    j = at - block * (span // 2)
    quarter = span // 4
    outer = jnp.where(j >= quarter, j + 2 * quarter, j)
    half = block * span + jnp.where(parity == 0, outer, j + quarter)
    return jnp.where(kind == 0, at, half)


def loop(low, high, do):
    def step(c, _):
        do(c)
        return 0

    lax.fori_loop(low, high, step, 0)


def fwd_kernel(
    span,
    n_ref,
    kind_ref,
    tile_ref,
    par_ref,
    q_ref,
    k_ref,
    vt_ref,
    o_ref,
    low_ref,
    linv_ref,
    p_hbm,
    s0,
    s1,
    p0,
    p1,
    m0,
    m1,
    acc_scr,
    l_scr,
    sem0,
    sem1,
):
    i = pl.program_id(0)
    last = pl.num_programs(0) - 1
    before = jnp.maximum(i - 1, 0)
    n1 = n_ref[i]
    n2 = n_ref[before]
    unit1 = kind_ref[i]
    unit2 = kind_ref[before]

    def work(c1, c2, masked, now, old, q, place):
        s_now, m_now = now
        s_old, p_old, m_old = old
        if c1 is not None:
            m = m_now[...]
        if c2 is not None:
            top = jnp.max(m_old[...], axis=0, keepdims=True) * (logit_scale * LOG2E)
            l = l_scr[...]
            o = acc_scr[...]
        for j in range(KC // SUBF):
            if c1 is not None:
                off = c1 * KC + j * SUBF
                s = jnp.dot(k_ref[rows_of(off, SUBF), :], q, preferred_element_type=f32)
                if masked:
                    key = lax.broadcasted_iota(jnp.int32, (SUBF, QT), 0)
                    s = jnp.where(key <= place - off, s, masked_score)
                s_now[rows_of(off, SUBF), :] = s
                m = jnp.maximum(m, jnp.max(s.reshape(SUBF // 8, 8, QT), axis=0))
            if c2 is not None:
                off = c2 * KC + j * SUBF
                s = s_old[rows_of(off, SUBF), :]
                p = jnp.exp2(s * (logit_scale * LOG2E) - top)
                l = l + jnp.sum(p.reshape(SUBF // 8, 8, QT), axis=0)
                low = p.astype(bf16)
                p_old[rows_of(off, SUBF), :] = low
                o = o + jnp.dot(
                    vt_ref[unit2, :, rows_of(off, SUBF)], low, preferred_element_type=f32
                )
        if c1 is not None:
            m_now[...] = m
        if c2 is not None:
            l_scr[...] = l
            acc_scr[...] = o

    def send(c, p_scr, sem):
        part = rows_of(c * KC, KC)
        pltpu.make_async_copy(p_scr.at[part], p_hbm.at[before, part], sem).start()

    def drain(count, p_scr, sem):
        def wait(c):
            part = pl.ds(0, KC)
            pltpu.make_async_copy(p_scr.at[part], p_hbm.at[0, part], sem).wait()

        loop(0, count, wait)

    @pl.when(i >= 1)
    def _():
        l_scr[...] = jnp.zeros_like(l_scr)
        acc_scr[...] = jnp.zeros_like(acc_scr)

    slots = ((s0, p0, m0, sem0), (s1, p1, m1, sem1))
    for turn in (0, 1):
        s_now, p_now, m_now, sem_now = slots[turn]
        s_old, p_old, m_old, sem_old = slots[1 - turn]

        @pl.when(lax.rem(i, 2) == turn)
        def _(s_now=s_now, p_now=p_now, m_now=m_now, sem_now=sem_now, s_old=s_old, p_old=p_old, m_old=m_old, sem_old=sem_old, turn=turn):
            q = load_tile(q_ref, unit1, tile_ref[i], span)
            none = jnp.zeros_like(q)
            q = jnp.concatenate(
                [jnp.where(unit1 == 0, q, none), jnp.where(unit1 == 0, none, q)], axis=0
            )
            place = tile_places(unit1, tile_ref[i], par_ref[0], span)
            m_now[...] = jnp.full((8, QT), -jnp.inf, f32)

            @pl.when(i >= 3)
            def _():
                drain(n_ref[jnp.maximum(i - 3, 0)], p_old, sem_old)

            def go(c1, c2, masked=False):
                work(c1, c2, masked, (s_now, m_now), (s_old, p_old, m_old), q, place)

            if turn == 0:

                @pl.when(i == 0)
                def _():
                    loop(0, n1, lambda c: go(c, None, True))

            @pl.when(jnp.logical_and(i > 0, i < last))
            def _():
                go(n1 - 1, n2 - 1, True)
                send(n2 - 1, p_old, sem_old)
                both = jnp.minimum(n1, n2) - 1

                def step(c):
                    go(c, c)
                    send(c, p_old, sem_old)

                loop(0, both, step)
                loop(both, n1 - 1, lambda c: go(c, None))

            @pl.when(i == last)
            def _():
                def step(c):
                    go(None, c)
                    send(c, p_old, sem_old)

                loop(0, n2, step)
                drain(n_ref[jnp.maximum(i - 2, 0)], p_now, sem_now)
                drain(n2, p_old, sem_old)

    @pl.when(i > 0)
    def _():
        linv = 1.0 / jnp.sum(l_scr[...], axis=0, keepdims=True)
        o = acc_scr[...] * linv
        t = tile_ref[before]
        nf, nh = QT // span, 2 * QT // span
        for count, width, start, unit in ((nf, span, 0, 0), (nh, span // 2, span, 1)):

            @pl.when(unit2 == unit)
            def _(count=count, width=width, start=start):
                for j in range(count):
                    here = slice(j * width, (j + 1) * width)
                    there = pl.ds(start, width)
                    o_ref[t * count + j, :, there] = o[:, here]
                    low_ref[t * count + j, :, there] = o[:, here].astype(bf16)
                    linv_ref[t * count + j, :, there] = linv[:, here]


def table(values):
    return jnp.array(values, jnp.int32)


def pair_units(tiles):
    return sum(t[2] for t in tiles) * KC * QT


def whole(x):
    zeros = (0,) * len(x.shape)
    return pl.BlockSpec(x.shape, lambda *_: zeros)


def attn_fwd(q, k, vt, parity, tiles, span):
    nk = k.shape[0]
    steps = len(tiles)
    listed = tiles + [(tiles[-1][0], tiles[-1][1], 0)]
    linv = jax.ShapeDtypeStruct((q.shape[0], 1, q.shape[2]), f32)
    o = jax.ShapeDtypeStruct(q.shape, f32)
    work = pair_units(tiles)
    return pl.pallas_call(
        partial(fwd_kernel, span),
        name="attn_fwd",
        grid_spec=pltpu.PrefetchScalarGridSpec(
            num_scalar_prefetch=4,
            grid=(steps + 1,),
            in_specs=[whole(q), whole(k), whole(vt)],
            out_specs=[whole(q), whole(q), whole(linv), pl.BlockSpec(memory_space=pl.ANY)],
            scratch_shapes=[
                pltpu.VMEM((nk, QT), f32),
                pltpu.VMEM((nk, QT), f32),
                pltpu.VMEM((nk, QT), bf16),
                pltpu.VMEM((nk, QT), bf16),
                pltpu.VMEM((8, QT), f32),
                pltpu.VMEM((8, QT), f32),
                pltpu.VMEM((HEAD_DIM, QT), f32),
                pltpu.VMEM((8, QT), f32),
                pltpu.SemaphoreType.DMA,
                pltpu.SemaphoreType.DMA,
            ],
        ),
        out_shape=[
            o,
            jax.ShapeDtypeStruct(q.shape, bf16),
            linv,
            jax.ShapeDtypeStruct((steps, nk, QT), bf16),
        ],
        compiler_params=pltpu.CompilerParams(vmem_limit_bytes=VMEM),
        cost_estimate=pl.CostEstimate(
            flops=work * 1024, bytes_accessed=work * 2, transcendentals=work
        ),
    )(
        table([t[2] for t in listed]),
        table([t[0] for t in listed]),
        table([t[1] for t in listed]),
        parity.reshape(1),
        q,
        k,
        vt,
    )


def bwd_kernel(
    unit,
    span,
    qt,
    n_ref,
    tile_ref,
    slot_ref,
    turn_ref,
    par_ref,
    q_ref,
    do_ref,
    o_ref,
    linv_ref,
    kt_ref,
    v_ref,
    p_hbm,
    *refs,
):
    outs = refs[:-10]
    p_scr, dp0, dp1, q_scr, do_scr, de_scr, dq_scr, dk_scr, dv_scr, sem = refs[-10:]
    dps = (dp0, dp1)
    i = pl.program_id(0)
    last = pl.num_programs(0) - 1
    a = lax.rem(i, 2)
    b = 1 - a
    before = jnp.maximum(i - 1, 0)
    n1 = n_ref[i]
    n2 = n_ref[before]
    turn1 = turn_ref[i]
    turn2 = turn_ref[before]
    devices = kt_ref.shape[2] // span
    cuts = qt // QT
    width = span // 2 if unit else span

    def tile(ref):
        count = qt // width
        return jnp.concatenate([ref[tile_ref[i] * count + j] for j in range(count)], axis=-1)

    def fetch(t, slot):
        def start(c):
            part = rows_of(c * KC, KC)
            for s in range(cuts):
                there = p_scr.at[slot, part, pl.ds(s * QT, QT)]
                pltpu.make_async_copy(
                    p_hbm.at[slot_ref[t * cuts + s], part], there, sem.at[slot]
                ).start()

        loop(0, n_ref[t], start)

    def work(c1, dp_now, c2, slot, dp_old):
        if c1 is not None:
            do_now = do_scr[a]
        if c2 is not None:
            query = q_scr[slot]
            dot = do_scr[slot, unit * HEAD_DIM : (unit + 1) * HEAD_DIM, :]
            delta = de_scr[slot]
            dq = dq_scr[...]
        for j in range(KC // SUB):
            here = pl.ds(j * SUB, SUB)
            if c1 is not None:
                dp_now[here, :] = jnp.dot(
                    v_ref[rows_of(c1 * KC + j * SUB, SUB), :],
                    do_now,
                    preferred_element_type=f32,
                )
            if c2 is not None:
                keys = rows_of(c2 * KC + j * SUB, SUB)
                p = p_scr[slot, keys, :]
                ds = (p.astype(f32) * (dp_old[here, :] - delta)).astype(bf16)
                dv_scr[:, keys] += lax.dot_general(
                    dot, p, (((1,), (1,)), ((), ())), preferred_element_type=f32
                )
                dk_scr[:, keys] += lax.dot_general(
                    query, ds, (((1,), (1,)), ((), ())), preferred_element_type=f32
                )
                dq = dq + jnp.dot(kt_ref[0, :, keys], ds, preferred_element_type=f32)
        if c2 is not None:
            dq_scr[...] = dq

    def by_turn(turn, do):
        for t in (0, 1):

            @pl.when(lax.rem(turn, 2) == t)
            def _(t=t):
                do(dps[t], dps[1 - t])

    def load():
        scaled = tile(do_ref).astype(f32) * tile(linv_ref)
        de_scr[a] = jnp.sum(scaled * tile(o_ref), axis=0, keepdims=True)
        do_scr[a, unit * HEAD_DIM : (unit + 1) * HEAD_DIM, :] = scaled.astype(bf16)
        q_scr[a] = tile(q_ref)

    @pl.when(i == 0)
    def _():
        do_scr[...] = jnp.zeros_like(do_scr)
        dk_scr[...] = jnp.zeros_like(dk_scr)
        dv_scr[...] = jnp.zeros_like(dv_scr)
        dq_scr[...] = jnp.zeros_like(dq_scr)
        fetch(0, 0)
        load()
        work(0, dps[0], None, None, None)

    @pl.when(jnp.logical_and(i > 0, i < last))
    def _():
        load()

        def step(now, other):
            work(0, now, n2 - 1, b, other)

        by_turn(turn1, step)

    @pl.when(i == last)
    def _():
        by_turn(n2 - 1 + turn2, lambda now, other: work(None, None, n2 - 1, b, now))

    @pl.when(i > 0)
    def _():
        dq = (dq_scr[...] * logit_scale).astype(bf16)
        t = tile_ref[before]
        count = qt // width
        for j in range(count):
            outs[0][t * count + j, :HEAD_DIM, :width] = dq[:, j * width : (j + 1) * width]
        dq_scr[...] = jnp.zeros_like(dq_scr)

    @pl.when(i < last)
    def _():
        def wait(c):
            part = pl.ds(0, KC)
            pltpu.make_async_copy(p_scr.at[a, part], p_scr.at[a, part], sem.at[a]).wait()

        loop(0, n1, wait)

        @pl.when(i + 1 < last)
        def _():
            fetch(i + 1, b)

        def step(c):
            def both(now, other):
                work(c + 1, other, c, a, now)

            by_turn(c + turn1, both)

        loop(0, n1 - 1, step)

    @pl.when(i == last)
    def _():
        quarter = span // 4
        for d in range(devices):
            keys = pl.ds(d * span, span)
            dk = dk_scr[:, keys] * logit_scale
            dv = dv_scr[:, keys]
            if not unit:
                outs[0][d, HEAD_DIM : 2 * HEAD_DIM, :span] = dk.astype(bf16)
                outs[0][d, 2 * HEAD_DIM :, :span] = dv.astype(bf16)
            else:
                both = jnp.concatenate([dk, dv], axis=0)
                outer = jnp.concatenate([both[:, :quarter], both[:, 3 * quarter :]], axis=1)
                inner = both[:, quarter : 3 * quarter]
                even = par_ref[0] == 0
                outs[1][d] = jnp.where(even, outer, inner)
                outs[2][d] = jnp.where(even, inner, outer).astype(bf16)


def attn_bwd(unit, q, do, o, linv, kt, v, p, parity, tiles, slots, span):
    nk = kt.shape[2]
    steps = len(tiles)
    qt = KC if unit == 0 else QT
    width = span // 2 if unit else span

    def columns(x):
        return pl.BlockSpec((*x.shape[:2], width), lambda *_: (0, 0, 2 if unit else 0))

    listed = tiles + [(unit, tiles[-1][1], 0)]
    turns = [0]
    for t in tiles:
        turns.append((turns[-1] + t[2]) % 2)
    devices = nk // span
    if unit:
        outs = [
            jax.ShapeDtypeStruct((devices, HEAD_DIM, span // 2), bf16),
            jax.ShapeDtypeStruct((devices, 2 * HEAD_DIM, span // 2), f32),
            jax.ShapeDtypeStruct((devices, 2 * HEAD_DIM, span // 2), bf16),
        ]
    else:
        outs = [jax.ShapeDtypeStruct((devices, 3 * HEAD_DIM, span), bf16)]
    work = pair_units(tiles) * (qt // QT)
    return pl.pallas_call(
        partial(bwd_kernel, unit, span, qt),
        name="attn_bwd_half" if unit else "attn_bwd_full",
        grid_spec=pltpu.PrefetchScalarGridSpec(
            num_scalar_prefetch=5,
            grid=(steps + 1,),
            in_specs=[
                columns(q),
                columns(do),
                columns(o),
                columns(linv),
                pl.BlockSpec((1, HEAD_DIM, nk), lambda *_: (unit, 0, 0)),
                whole(v),
                pl.BlockSpec(memory_space=pl.ANY),
            ],
            out_specs=[whole(x) for x in outs],
            scratch_shapes=[
                pltpu.VMEM((2, nk, qt), bf16),
                pltpu.VMEM((KC, qt), f32),
                pltpu.VMEM((KC, qt), f32),
                pltpu.VMEM((2, HEAD_DIM, qt), bf16),
                pltpu.VMEM((2, 2 * HEAD_DIM, qt), bf16),
                pltpu.VMEM((2, 1, qt), f32),
                pltpu.VMEM((HEAD_DIM, qt), f32),
                pltpu.VMEM((HEAD_DIM, nk), f32),
                pltpu.VMEM((HEAD_DIM, nk), f32),
                pltpu.SemaphoreType.DMA((2,)),
            ],
        ),
        out_shape=outs,
        compiler_params=pltpu.CompilerParams(vmem_limit_bytes=VMEM),
        cost_estimate=pl.CostEstimate(
            flops=work * 2048, bytes_accessed=work * 2, transcendentals=0
        ),
    )(
        table([t[2] for t in listed]),
        table([t[1] for t in listed]),
        table(slots),
        table(turns),
        parity.reshape(1),
        q,
        do,
        o,
        linv,
        kt,
        v,
        p,
    )


def pick_quarters(x, parity, axis):
    q = x.shape[axis] // 4

    def cut(low, high):
        return x[low * q : high * q] if axis == 0 else x[:, low * q : high * q]

    outer = jnp.concatenate([cut(0, 1), cut(3, 4)], axis=axis)
    return jnp.where(parity == 0, outer, cut(1, 3))


def prep_kernel(count, pos_ref, par_ref, *refs):
    blocks = refs[:count]
    gain_ref, shift_ref, wt_ref, bt_ref, wn_ref, bn_ref = refs[count : count + 6]
    h_ref, q_ref, kt_ref, vt_ref, k_ref, v_ref, x_scr, sem = refs[count + 6 :]
    i = pl.program_id(0)
    for j in range(count):

        @pl.when(i == max(j - 1, 0))
        def _(j=j):
            pltpu.make_async_copy(blocks[j], x_scr.at[j % 2], sem.at[j % 2]).start()

    slot = lax.rem(i, 2)
    pltpu.make_async_copy(x_scr.at[slot], x_scr.at[slot], sem.at[slot]).wait()
    _, span, width = x_scr.shape
    d = HEAD_DIM
    cuts = 2
    sub = span // cuts
    for r in range(cuts):
        here = pl.ds(r * sub, sub)
        x = x_scr[slot, here, :].astype(f32)
        x = x - jnp.mean(x, axis=-1, keepdims=True)
        spread = jnp.mean(x * x, axis=-1, keepdims=True)
        h = (x * lax.rsqrt(spread + norm_eps) * gain_ref[...] + shift_ref[...]).astype(bf16)
        h_ref[here, :] = h
        over = lax.dot_general(
            wt_ref[...], h, (((1,), (1,)), ((), ())), preferred_element_type=f32
        )
        over = (over + bt_ref[...]).astype(bf16)
        q_ref[0, :, here] = over[:d]
        half = over[3 * d : 4 * d]
        low, high = half[:, : sub // 2], half[:, sub // 2 :]
        outer, inner = (low, high) if r == 0 else (high, low)
        q_ref[0, :, pl.ds(span + r * sub // 2, sub // 2)] = jnp.where(
            par_ref[0] == 0, outer, inner
        )
        for unit in (0, 1):
            kt_ref[unit, :, here] = over[(3 * unit + 1) * d : (3 * unit + 2) * d]
            vt_ref[unit, :, here] = over[(3 * unit + 2) * d : (3 * unit + 3) * d]
        flat = jnp.dot(h, wn_ref[...], preferred_element_type=f32) + bn_ref[...]
        flat = flat.astype(bf16)
        k_ref[here, :] = flat[:, : 2 * d]
        v_ref[here, :] = flat[:, 2 * d :]


def prep(blocks, pos, parity, gain, shift, wt, bt, wn, bn):
    count = len(blocks)
    span, width = blocks[0].shape
    devices = lax.axis_size("seq")
    nk = devices * span
    d = HEAD_DIM
    shapes = [
        ((nk, width), (span, width), lambda i, s, _: (s[i], 0)),
        ((devices, d, 3 * span // 2), (1, d, 3 * span // 2), lambda i, s, _: (s[i], 0, 0)),
        ((2, d, nk), (2, d, span), lambda i, s, _: (0, 0, s[i])),
        ((2, d, nk), (2, d, span), lambda i, s, _: (0, 0, s[i])),
        ((nk, 2 * d), (span, 2 * d), lambda i, s, _: (s[i], 0)),
        ((nk, 2 * d), (span, 2 * d), lambda i, s, _: (s[i], 0)),
    ]
    params = (gain, shift, wt, bt, wn, bn)
    return pl.pallas_call(
        partial(prep_kernel, count),
        name="prep",
        grid_spec=pltpu.PrefetchScalarGridSpec(
            num_scalar_prefetch=2,
            grid=(count,),
            in_specs=[pl.BlockSpec(memory_space=pl.ANY)] * count + [whole(x) for x in params],
            out_specs=[pl.BlockSpec(block, index) for _, block, index in shapes],
            scratch_shapes=[pltpu.VMEM((2, span, width), bf16), pltpu.SemaphoreType.DMA((2,))],
        ),
        out_shape=[jax.ShapeDtypeStruct(shape, bf16) for shape, _, _ in shapes],
        compiler_params=pltpu.CompilerParams(vmem_limit_bytes=VMEM),
        cost_estimate=pl.CostEstimate(
            flops=1, bytes_accessed=1, transcendentals=0
        ),
    )(pos, parity.reshape(1), *blocks, *params)


def pull_kernel(
    back_ref, pick_ref, grad_ref, mid_ref, gain_ref, w_ref, gm_ref, br_ref, do_ref, small_ref
):
    tokens = grad_ref.shape[0]
    gain = gain_ref[...]
    totals = [0.0, 0.0, 0.0]
    cut = tokens // 4
    for r in range(4):
        here = pl.ds(r * cut, cut)
        dh = jnp.dot(pick_ref[here, :], back_ref[...], preferred_element_type=f32)
        x = mid_ref[here, :]
        x = x - jnp.mean(x, axis=-1, keepdims=True)
        inv = lax.rsqrt(jnp.mean(x * x, axis=-1, keepdims=True) + norm_eps)
        x = x * inv
        d = dh * gain
        dx = inv * (
            d - jnp.mean(d, axis=-1, keepdims=True) - x * jnp.mean(d * x, axis=-1, keepdims=True)
        )
        gm = grad_ref[here, :].astype(f32) + dx
        branch = gm.astype(bf16)
        gm_ref[here, :] = gm
        br_ref[here, :] = branch
        for at, part in enumerate((branch.astype(f32), dh * x, dh)):
            totals[at] = totals[at] + jnp.sum(part, axis=0, keepdims=True)
    for at in range(3):
        small_ref[at : at + 1] = totals[at]
    do = lax.dot_general(
        w_ref[...], br_ref[...], (((1,), (1,)), ((), ())), preferred_element_type=f32
    ).astype(bf16)
    span = do_ref.shape[2] * 2 // 3
    for u in range(do.shape[1] // span * HEADS):
        n, head = u // HEADS, u % HEADS
        part = do[head * HEAD_DIM : (head + 1) * HEAD_DIM, n * span : (n + 1) * span]
        p, role = u // 3, u % 3
        if role != 1:
            do_ref[2 * p + role // 2, :, :span] = part
        else:
            q = span // 4
            outer = jnp.concatenate([part[:, :q], part[:, 3 * q :]], axis=1)
            do_ref[2 * p, :, span:] = outer
            do_ref[2 * p + 1, :, span:] = part[:, q : 3 * q]


def pull(back, pick, grad, mid, gain, w_out, span):
    tokens, width = grad.shape
    return pl.pallas_call(
        pull_kernel,
        name="pull",
        out_shape=[
            jax.ShapeDtypeStruct((tokens, width), f32),
            jax.ShapeDtypeStruct((tokens, width), bf16),
            jax.ShapeDtypeStruct((lax.axis_size("seq"), HEAD_DIM, 3 * span // 2), bf16),
            jax.ShapeDtypeStruct((3, width), f32),
        ],
        compiler_params=pltpu.CompilerParams(vmem_limit_bytes=VMEM),
        cost_estimate=pl.CostEstimate(
            flops=4 * tokens * width * width, bytes_accessed=tokens * width * 16, transcendentals=0
        ),
    )(back, pick, grad, mid, gain, w_out)


def pack_kernel(half, at_ref, part_ref, h_ref, out_ref, small_ref, piece_ref, acc, cnt):
    i = pl.program_id(0)
    devices, rows, tokens = part_ref.shape
    stretch, width = h_ref.shape[0] // devices, h_ref.shape[1]
    g = jnp.zeros((rows, width), f32)
    count = jnp.zeros((8, rows), f32)
    ones = jnp.ones((8, tokens), bf16)
    for d in range(devices):
        part = part_ref[d]
        h = h_ref[pl.ds(d * stretch, stretch), :]
        if half:
            h = pick_quarters(h, at_ref[1], 0)
        g += jnp.dot(part, h, preferred_element_type=f32)
        count += lax.dot_general(
            ones, part, (((1,), (1,)), ((), ())), preferred_element_type=f32
        )

    @pl.when(i == 0)
    def _():
        acc[...] = g
        cnt[...] = count

    @pl.when(i > 0)
    def _():
        acc[...] += g
        cnt[...] += count

    @pl.when(i == pl.num_programs(0) - 1)
    def _():
        nexp, share, _ = piece_ref.shape
        line = jnp.concatenate([cnt[...], jnp.zeros((8, width - rows), f32)], axis=1)
        line = jnp.concatenate([line, small_ref[...]], axis=0)
        filled = rows + out_ref.shape[0] + 16
        parts = [acc[...].astype(bf16), out_ref[...], line.astype(bf16)]
        if nexp * share > filled:
            parts.append(jnp.zeros((nexp * share - filled, width), bf16))
        piece = jnp.concatenate(parts, axis=0)
        for e in range(nexp):
            piece_ref[at_ref[0] ^ e] = piece[e * share : (e + 1) * share]


def pack(part, h1, parity, half, out_rows, small):
    devices, rows, _ = part.shape
    nk, width = h1.shape
    nexp = lax.axis_size("exp")
    filled = rows + out_rows.shape[0] + 16
    share = -(-filled // (16 * nexp)) * 16
    steps = 4
    return pl.pallas_call(
        partial(pack_kernel, half),
        name="pack_half" if half else "pack_full",
        grid_spec=pltpu.PrefetchScalarGridSpec(
            num_scalar_prefetch=1,
            grid=(steps,),
            in_specs=[
                pl.BlockSpec(
                    (devices // steps, rows, nk // devices // (2 if half else 1)),
                    lambda i, _: (i, 0, 0),
                ),
                pl.BlockSpec((nk // steps, width), lambda i, _: (i, 0)),
                whole(out_rows),
                whole(small),
            ],
            out_specs=pl.BlockSpec((nexp, share, width), lambda i, _: (0, 0, 0)),
            scratch_shapes=[pltpu.VMEM((rows, width), f32), pltpu.VMEM((8, rows), f32)],
        ),
        out_shape=jax.ShapeDtypeStruct((nexp, share, width), bf16),
        compiler_params=pltpu.CompilerParams(vmem_limit_bytes=VMEM),
        cost_estimate=pl.CostEstimate(flops=1, bytes_accessed=1, transcendentals=0),
    )(jnp.stack([lax.axis_index("exp"), parity]), part, h1, out_rows, small)


def home_kernel(nseq, span, full_ref, half_ref, w_ref, x_ref, gain_ref, gm_ref, dx_ref, u_scr):
    pairs = full_ref.shape[0] // 2
    quarter = span // 4
    for n in range(nseq):
        here = pairs // nseq
        for j in range(here):
            p = n * here + j
            outer, inner = half_ref[2 * p], half_ref[2 * p + 1]
            mid = jnp.concatenate([outer[:, :quarter], inner, outer[:, quarter:]], axis=1)
            for role, unit in enumerate((full_ref[2 * p], mid, full_ref[2 * p + 1])):
                for c in range(3):
                    at = c * HEADS + 3 * j + role
                    u_scr[pl.ds(at * HEAD_DIM, HEAD_DIM), :] = unit[
                        c * HEAD_DIM : (c + 1) * HEAD_DIM
                    ]
        dh = jnp.dot(w_ref[...], u_scr[...], preferred_element_type=f32).T
        x = x_ref[n].astype(f32)
        x = x - jnp.mean(x, axis=-1, keepdims=True)
        inv = lax.rsqrt(jnp.mean(x * x, axis=-1, keepdims=True) + norm_eps)
        x = x * inv
        d = dh * gain_ref[...]
        dx_ref[n] = gm_ref[n] + inv * (
            d - jnp.mean(d, axis=-1, keepdims=True) - x * jnp.mean(d * x, axis=-1, keepdims=True)
        )


def home(full, half, w_qkv, x, gain, grad_middle):
    nseq, span, width = x.shape
    return pl.pallas_call(
        partial(home_kernel, nseq, span),
        name="home",
        out_shape=jax.ShapeDtypeStruct((nseq, span, width), f32),
        scratch_shapes=[pltpu.VMEM((3 * width, span), bf16)],
        compiler_params=pltpu.CompilerParams(vmem_limit_bytes=VMEM),
        cost_estimate=pl.CostEstimate(
            flops=1, bytes_accessed=1, transcendentals=0
        ),
    )(full, half, w_qkv, x, gain, grad_middle)


def part_kernel(got_ref, up_ref, down_ref, line_ref):
    share = up_ref.shape[1]
    up_ref[...] = got_ref[:share].T.astype(f32)
    down_ref[...] = got_ref[share : 2 * share].astype(f32)
    line_ref[...] = got_ref[2 * share :].astype(f32)


def part_shares(got, share):
    width = got.shape[1]
    return pl.pallas_call(
        part_kernel,
        name="part_shares",
        out_shape=[
            jax.ShapeDtypeStruct((width, share), f32),
            jax.ShapeDtypeStruct((share, width), f32),
            jax.ShapeDtypeStruct((got.shape[0] - 2 * share, width), f32),
        ],
        compiler_params=pltpu.CompilerParams(vmem_limit_bytes=VMEM),
        cost_estimate=pl.CostEstimate(flops=1, bytes_accessed=1, transcendentals=0),
    )(got)


def build_kernel(nseq, nexp, devices, cut, at_ref, *refs):
    halves, fulls = refs[0], refs[1 : 1 + devices]
    w_ref, gain_ref, shift_ref, g_ref, out_ref, small_ref, half, full, acc, sem = refs[1 + devices :]
    me, z = at_ref[0], at_ref[1]
    c = pl.program_id(0)
    d = HEAD_DIM
    rows = 3 * d
    width = g_ref.shape[0]
    out_rows = width // devices

    @pl.when(c == 0)
    def _():
        for j in range(devices):
            for e in range(nexp):
                for block, got in ((halves.at[j], half), (fulls[j], full)):
                    share = got.shape[1] // nexp
                    pltpu.make_async_copy(
                        block.at[pl.ds(pl.multiple_of((z ^ e) * share, 16), share)],
                        got.at[j, pl.ds(e * share, share)],
                        sem,
                    ).start()
        acc[...] = jnp.zeros_like(acc)
        pltpu.make_async_copy(half, half, sem).wait()
        pltpu.make_async_copy(full, full, sem).wait()

    def from_unit(u, at, lanes):
        p, role = u // 3, u % 3
        if role != 1:
            return full[me ^ (2 * p + role // 2), at, lanes].astype(f32)
        return half[2 * p, at, lanes].astype(f32) + half[2 * p + 1, at, lanes].astype(f32)

    def unit_rows(u):
        return from_unit(u, rows_of(c * d, d), slice(None))

    def unit_sums(u):
        line = rows + (cut if u % 3 == 1 else out_rows - cut)
        line = from_unit(u, pl.ds(line, 16), pl.ds(0, rows))[:1]
        return jnp.where(c == 0, line[:, :d], jnp.where(c == 1, line[:, d : 2 * d], line[:, 2 * d :]))

    for two in range(HEADS // 2):
        heads = (2 * two, 2 * two + 1)
        grads = [sum(unit_rows(n * HEADS + h) for n in range(nseq)) for h in heads]
        sums = [sum(unit_sums(n * HEADS + h) for n in range(nseq)) for h in heads]
        at = pl.ds(two * 2 * d, 2 * d)
        block = jnp.concatenate(grads, axis=0)
        total = jnp.concatenate(sums, axis=1)
        g_ref[:, at] = block.T
        w = w_ref[at, :]
        gained = w.astype(f32) * block
        acc[:8] += jnp.sum(gained.reshape(2 * d // 8, 8, width), axis=0)
        acc[8:16] += jnp.dot(
            jnp.broadcast_to(total, (8, 2 * d)).astype(bf16), w, preferred_element_type=f32
        )

        acc[pl.ds(16 + 8 * c, 1), at] = total
    @pl.when(c == 2)
    def _():
        gained = jnp.sum(acc[:8], axis=0, keepdims=True)
        shifted = acc[8:9]
        small_ref[0:1] = (gained - shift_ref[...] * shifted) / gain_ref[...]
        small_ref[1:2] = shifted
        small_ref[2:3] = acc[16:17]
        small_ref[3:4] = acc[32:33]
        small_ref[4:7] = half[0, pl.ds(rows + cut, 16), :].astype(f32)[8:11]
        small_ref[7:8] = jnp.zeros_like(shifted)
        for i in range(devices):
            out_ref[pl.ds(i * out_rows, cut), :] = half[i, pl.ds(rows, cut), :].astype(f32)
            out_ref[pl.ds(i * out_rows + cut, out_rows - cut), :] = full[
                me ^ i, pl.ds(rows, out_rows - cut), :
            ].astype(f32)


def build(halves, fulls, cut, w_rows, gain, shift, nseq):
    width = w_rows.shape[1]
    devices = len(fulls)
    nexp = lax.axis_size("exp")
    at = jnp.stack([lax.axis_index("seq"), lax.axis_index("exp")])
    away = pl.BlockSpec(memory_space=pl.ANY)
    return pl.pallas_call(
        partial(build_kernel, nseq, nexp, devices, cut),
        name="build",
        grid=(3,),
        in_specs=[pl.BlockSpec(memory_space=pltpu.SMEM)]
        + [away] * (1 + devices)
        + [pl.BlockSpec((width, width), lambda c: (c, 0)), whole(gain), whole(shift)],
        out_specs=[
            pl.BlockSpec((width, width), lambda c: (0, c)),
            pl.BlockSpec((width, width), lambda c: (0, 0)),
            pl.BlockSpec((8, width), lambda c: (0, 0)),
        ],
        out_shape=[
            jax.ShapeDtypeStruct((width, 3 * width), f32),
            jax.ShapeDtypeStruct((width, width), f32),
            jax.ShapeDtypeStruct((8, width), f32),
        ],
        scratch_shapes=[
            pltpu.VMEM(halves.shape, bf16),
            pltpu.VMEM((devices, *fulls[0].shape), bf16),
            pltpu.VMEM((40, width), f32),
            pltpu.SemaphoreType.DMA,
        ],
        compiler_params=pltpu.CompilerParams(vmem_limit_bytes=VMEM),
        cost_estimate=pl.CostEstimate(
            flops=0, bytes_accessed=18 * width * width, transcendentals=0
        ),
    )(at, halves, *fulls, w_rows, gain, shift)


def expert_sums_kernel(rows_ref, dy_ref, dz_ref, hid_ref, out_ref):
    contract = (((0,), (0,)), ((), ()))
    dz = dz_ref[...]
    share = dz.shape[1]
    dy = dy_ref[...]
    out_ref[0, :share] = lax.dot_general(
        dz, rows_ref[...], contract, preferred_element_type=f32
    ).astype(bf16)
    out_ref[0, share : 2 * share] = lax.dot_general(
        hid_ref[...], dy, contract, preferred_element_type=f32
    ).astype(bf16)
    ones = jnp.ones((16, dz.shape[0]), bf16)
    up = jnp.dot(ones, dz, preferred_element_type=f32).astype(bf16)
    fill = jnp.zeros((16, dy.shape[1] - share), bf16)
    out_ref[0, 2 * share : 2 * share + 16] = jnp.concatenate([up, fill], axis=1)
    out_ref[0, 2 * share + 16 :] = jnp.dot(ones, dy, preferred_element_type=f32).astype(bf16)


def expert_sums(rows, dy, dz, hidden):
    devices = lax.axis_size("seq")
    count, width = rows.shape
    ff = dz.shape[1]
    share = ff // devices
    if share % 128:
        contract = (((0,), (0,)), ((), ()))
        up = lax.dot_general(dz, rows, contract, preferred_element_type=f32)
        down = lax.dot_general(hidden, dy, contract, preferred_element_type=f32)
        up_bias = jnp.pad(
            jnp.sum(dz, axis=0, dtype=f32).reshape(devices, 1, share),
            ((0, 0), (0, 15), (0, width - share)),
        )
        down_bias = jnp.broadcast_to(jnp.sum(dy, axis=0, dtype=f32), (devices, 16, width))
        return jnp.concatenate(
            [up.reshape(devices, share, width), down.reshape(devices, share, width), up_bias, down_bias],
            axis=1,
        ).astype(bf16)
    total = 2 * share + 32
    return pl.pallas_call(
        expert_sums_kernel,
        name="expert_sums",
        grid=(devices,),
        in_specs=[
            pl.BlockSpec((count, width), lambda j: (0, 0)),
            pl.BlockSpec((count, width), lambda j: (0, 0)),
            pl.BlockSpec((count, share), lambda j: (0, j)),
            pl.BlockSpec((count, share), lambda j: (0, j)),
        ],
        out_specs=pl.BlockSpec((1, total, width), lambda j: (j, 0, 0)),
        out_shape=jax.ShapeDtypeStruct((devices, total, width), bf16),
        compiler_params=pltpu.CompilerParams(vmem_limit_bytes=VMEM),
        cost_estimate=pl.CostEstimate(
            flops=1, bytes_accessed=1, transcendentals=0
        ),
    )(rows, dy, dz, hidden)


def swap(x, axis, distance):
    return lax.ppermute(x, axis, [(i, i ^ distance) for i in range(lax.axis_size(axis))])


def gather_chips(x, beside=None):
    chips = lax.axis_size("seq") // 2
    if chips != 4:
        return [x] + [swap(x, "seq", 2 * d) for d in range(1, chips)], beside
    one, two = swap(x, "seq", 2), swap(x, "seq", 4)
    if beside is not None:
        one, two, beside = lax.optimization_barrier((one, two, beside))
    axis = x.ndim - 2
    half = x.shape[axis] // 2
    low = swap(lax.slice_in_dim(one, 0, half, axis=axis), "seq", 4)
    high = swap(lax.slice_in_dim(two, half, 2 * half, axis=axis), "seq", 2)
    return [x, one, two, jnp.concatenate([low, high], axis=axis)], beside


def gather_seq(x, beside):
    blocks = []
    chips, beside = gather_chips(x, beside)
    for block in chips:
        blocks += [block, swap(block, "seq", 1)]
    return blocks, beside


def in_order(stack, axis):
    me = lax.axis_index(axis)
    return jnp.take(stack, me ^ lax.iota(jnp.int32, stack.shape[0]), axis=0)


def sum_exp(parts):
    total = parts[0].astype(f32)
    for d in range(1, parts.shape[0]):
        total = total + swap(parts[d], "exp", d).astype(f32)
    return total.astype(bf16)


def gather_exp(total):
    return jnp.concatenate([total] + [swap(total, "exp", d) for d in range(1, lax.axis_size("exp"))])


def layer_norm(values, gain, shift):
    centre = jnp.mean(values, axis=-1, keepdims=True)
    centered = values - centre
    spread = jnp.mean(centered * centered, axis=-1, keepdims=True)
    return centered * lax.rsqrt(spread + norm_eps) * gain + shift


def from_owners(got, span):
    quarter = span // 4
    both = got.reshape(got.shape[0] // 2, 2, *got.shape[1:])
    outer, inner = both[:, 0, ..., span:], both[:, 1, ..., span:]
    mid = jnp.concatenate([outer[..., :quarter], inner, outer[..., quarter:]], axis=-1)
    return jnp.stack([both[:, 0, ..., :span], mid, both[:, 1, ..., :span]], axis=1)


def exchange(x, axis):
    return lax.all_to_all(x, axis, split_axis=0, concat_axis=0, tiled=True)


def exchange_exp(x):
    nexp = lax.axis_size("exp")
    parts = x.reshape(nexp, x.shape[0] // nexp, x.shape[1])
    return jnp.concatenate([parts[0]] + [swap(parts[d], "exp", d) for d in range(1, nexp)])


def local(
    inputs,
    token_ids,
    hash_table,
    capacity,
    ln1_gain,
    ln1_bias,
    w_qkv,
    q_bias,
    v_bias,
    w_out,
    out_bias,
    ln2_gain,
    ln2_bias,
    up_weight,
    up_bias,
    down_weight,
    down_bias,
    out_grad,
):
    nseq, span, width = inputs.shape
    tokens = nseq * span
    cycle = lax.axis_size("seq")
    me = lax.axis_index("seq")
    parity = me % 2
    pair = me // 2
    pairs = cycle // 2
    nk = cycle * span
    assert nseq * HEADS == 3 * pairs
    up, down = up_weight[0], down_weight[0]
    ff = up.shape[1]
    share = ff // cycle
    row = lambda x: x.reshape(1, -1)

    mine = (3 * pair) // HEADS
    def of_sequence(blocks):
        return [lax.dynamic_index_in_dim(b, mine, 0, keepdims=False) for b in blocks]


    experts = capacity.shape[0]
    cap = 5 * tokens // (4 * experts)
    expert_of = jnp.take(hash_table, token_ids.reshape(tokens))
    onehot = (expert_of[:, None] == lax.iota(jnp.int32, experts)[None, :]).astype(jnp.int32)
    rank = jnp.sum(onehot * (jnp.cumsum(onehot, axis=0) - 1), axis=1)
    kept = rank < jnp.take(capacity, expert_of)
    near_expert = expert_of ^ lax.axis_index("exp")
    slot = jnp.where(kept, near_expert * cap + rank, experts * cap)
    slots = lax.iota(jnp.int32, experts * cap)
    place = (slots[:, None] == slot[None, :]).astype(bf16)
    pick = (slots[None, :] == slot[:, None]).astype(bf16)

    def to_experts(rows):
        sent = jnp.dot(place, rows, preferred_element_type=f32).astype(bf16)
        return exchange_exp(sent)

    grad_rows = out_grad.reshape(tokens, width)
    dy = to_experts(grad_rows)
    da = lax.dot_general(dy, down, (((1,), (1,)), ((), ())), preferred_element_type=f32)

    head_full = (3 * pair + 2 * parity) % HEADS
    head_half = (3 * pair + 1) % HEADS
    w_heads = w_qkv.reshape(width, 3, HEADS, HEAD_DIM)

    def of_head(x, axis):
        return jnp.stack(
            [
                lax.dynamic_index_in_dim(x, head_full, axis, keepdims=False),
                lax.dynamic_index_in_dim(x, head_half, axis, keepdims=False),
            ]
        )

    w_mine = of_head(w_heads, 2)
    qb = of_head(q_bias.reshape(HEADS, HEAD_DIM), 0)
    vb = of_head(v_bias.reshape(HEADS, HEAD_DIM), 0)
    bias = jnp.stack([qb, jnp.zeros_like(qb), vb], axis=1)
    wt = w_mine.transpose(0, 2, 3, 1).reshape(6 * HEAD_DIM, width)
    wn = w_mine[:, :, 1:].transpose(1, 2, 0, 3).reshape(width, 4 * HEAD_DIM)
    bn = row(bias[:, 1:].transpose(1, 0, 2))
    params = (row(ln1_gain), row(ln1_bias), wt, bias.reshape(-1, 1), wn, bn)
    places = me ^ lax.iota(jnp.int32, cycle)
    chips, _ = gather_chips(inputs)
    far, params, pick, place, places = lax.optimization_barrier(
        (chips[-1], params, pick, place, places)
    )
    blocks = []
    for block in chips[:-1] + [far]:
        blocks += [block, swap(block, "seq", 1)]
    h1, q, kt, vt, k, v = prep(of_sequence(blocks), places, parity, *params)

    full = [(0, i, (i * QT + QT + KC - 1) // KC) for i in range(nk // QT)]
    half = [(1, i, (2 * (i * QT + QT) + KC - 1) // KC) for i in range(nk // (2 * QT))]
    tiles = sorted(full + half, key=lambda t: t[2])
    wide = [(0, i, i + 1) for i in range(nk // KC)]
    attn, attn_low, linv, p = attn_fwd(q, k, vt, parity, tiles, span)

    got = from_owners(exchange(attn_low, "seq"), span).reshape(nseq, width, span)
    x_rows = inputs.reshape(tokens, width).astype(f32)
    middle = (
        x_rows
        + jnp.einsum("nht,hd->ntd", got, w_out, preferred_element_type=f32).reshape(tokens, width)
        + out_bias
    )
    h2 = layer_norm(middle, ln2_gain, ln2_bias).astype(bf16)

    h2, da, pick = lax.optimization_barrier((h2, da, pick))
    rows = lax.optimization_barrier(to_experts(h2))
    z = jnp.dot(rows, up, preferred_element_type=f32) + up_bias
    phi = 0.5 * (1.0 + lax.erf(z * (1.0 / math.sqrt(2.0))))
    hidden = (z * phi).astype(bf16)
    slope = phi + z * jnp.exp(-0.5 * z * z) * (1.0 / math.sqrt(2.0 * math.pi))
    dz = (da * slope).astype(bf16)
    dh2 = lax.dot_general(dz, up, (((1,), (1,)), ((), ())), preferred_element_type=f32)
    back = exchange_exp(dh2.astype(bf16))
    shares = expert_sums(rows, dy, dz, hidden)
    y = jnp.dot(hidden, down, preferred_element_type=f32) + down_bias[0]
    back, shares, y = lax.optimization_barrier((back, shares, y.astype(bf16)))

    grad_middle, branch, do_home, small2 = pull(
        back, pick, grad_rows, middle, row(ln2_gain), w_out, span
    )
    do = exchange(do_home, "seq")
    low_rows = got.transpose(0, 2, 1).reshape(tokens, width)
    grad_w_out = lax.dot_general(
        low_rows, branch, (((0,), (0,)), ((), ())), preferred_element_type=f32
    ).astype(bf16)
    small2 = jnp.pad(small2, ((0, 13), (0, 0))).astype(bf16)
    out_rows = width // cycle
    cut = -(-out_rows // 32) * 16
    do, grad_w_out, small2, shares = lax.optimization_barrier((do, grad_w_out, small2, shares))
    shares = lax.psum_scatter(
        shares.reshape(-1, width), "seq", scatter_dimension=0, tiled=True
    )
    w_out_part = jnp.concatenate(
        [
            grad_w_out.reshape(cycle, width // cycle, width),
            jnp.broadcast_to(small2[None], (cycle, 16, width)),
        ],
        axis=1,
    )
    w_out_part = jnp.sum(exchange(w_out_part, "seq"), axis=0, dtype=f32)
    small2 = w_out_part[out_rows : out_rows + 8]
    w_out_part = w_out_part[:out_rows].astype(bf16)

    slot_of = {t[:2]: j for j, t in enumerate(tiles)}
    dq_half, sums_mine, sums_other = attn_bwd(
        1, q, do, attn, linv, kt, v, p, parity, half, [slot_of[t[:2]] for t in half], span
    )
    sums = (sums_mine + swap(sums_other, "seq", 1).astype(f32)).astype(bf16)
    part_half = jnp.concatenate([dq_half, sums], axis=1)
    home_half = exchange(part_half, "seq")
    packed = pack(part_half, h1, parity, True, w_out_part[:cut], small2)
    both = jnp.concatenate([packed, y.reshape(experts, cap, width)], axis=1)
    both, late = lax.optimization_barrier((both, do))
    both = [both[0]] + [swap(both[d], "exp", d) for d in range(1, experts)]
    count = packed.shape[1]
    sum_half = sum(part[:count].astype(f32) for part in both).astype(bf16)
    y_back = jnp.concatenate([part[count:] for part in both])
    part_full = attn_bwd(
        0, q, late, attn, linv, kt, v, p, parity, wide, [slot_of[t[:2]] for t in full], span
    )[0]
    part_full, home_half, sum_half = lax.optimization_barrier((part_full, home_half, sum_half))

    packed = pack(part_full, h1, parity, False, w_out_part[cut:], jnp.zeros_like(small2))
    column_half, packed, part_full = lax.optimization_barrier(
        (gather_exp(sum_half), packed, part_full)
    )
    halves = lax.all_gather(column_half, "seq")
    home_full = exchange(part_full, "seq")
    sum_full = sum_exp(packed)
    input_grad = home(
        home_full,
        home_half,
        w_qkv,
        inputs,
        row(ln1_gain),
        grad_middle.reshape(nseq, span, width),
    )
    output = middle + jnp.dot(pick, y_back, preferred_element_type=f32)
    output = output.astype(bf16).reshape(nseq, span, width)
    up_grad, down_grad, lines = part_shares(shares, share)
    down_share = lax.dynamic_slice_in_dim(lines[16], me * (width // cycle), width // cycle, 0)
    expert_grads = (up_grad[None], lines[:1, :share], down_grad[None], down_share[None])
    column, output, expert_grads = lax.optimization_barrier(
        (gather_exp(sum_full), output, expert_grads)
    )
    fulls, input_grad = gather_seq(column, input_grad)
    grad_w_qkv, grad_w_out, small = build(
        halves, fulls, cut, w_qkv.T, row(ln1_gain), row(ln1_bias), nseq
    )
    return (
        output,
        input_grad,
        small[0],
        small[1],
        grad_w_qkv,
        small[2],
        small[3],
        grad_w_out,
        small[4],
        small[5],
        small[6],
        *expert_grads,
    )


def solution(mesh):
    in_specs = (
        P("exp", "seq", None),
        P("exp", "seq"),
        P(),
        P(),
        P(),
        P(),
        P(),
        P(),
        P(),
        P(),
        P(),
        P(),
        P(),
        P("exp", None, None),
        P("exp", None),
        P("exp", None, None),
        P("exp", None),
        P("exp", "seq", None),
    )
    out_specs = (
        P("exp", "seq", None),
        P("exp", "seq", None),
        P(),
        P(),
        P(),
        P(),
        P(),
        P(),
        P(),
        P(),
        P(),
        P("exp", None, "seq"),
        P("exp", "seq"),
        P("exp", "seq", None),
        P("exp", "seq"),
    )
    return jax.shard_map(local, mesh=mesh, in_specs=in_specs, out_specs=out_specs, check_vma=False)
```

```python
from functools import partial
import math

import jax
import jax.numpy as jnp
from jax import lax
from jax.experimental import pallas as pl
from jax.experimental.pallas import tpu as pltpu
from jax.sharding import PartitionSpec as P

HEADS = 12
HEAD_DIM = 64
f32 = jnp.float32
bf16 = jnp.bfloat16

norm_eps = 1e-05
logit_scale = 0.125
masked_score = -1e30
LOG2E = math.log2(math.e)

QT = 512
KC = 1024
SUB = 256
SUBF = 512
VMEM = 56 * 2**20


def rows_of(start, size):
    return pl.ds(pl.multiple_of(start, size), size)


def load_tile(ref, kind, t, span):
    nf, nh = QT // span, 2 * QT // span

    def full():
        return jnp.concatenate([ref[t * nf + j, :, :span] for j in range(nf)], axis=-1)

    def half(t):
        return jnp.concatenate([ref[t * nh + j, :, span:] for j in range(nh)], axis=-1)

    if isinstance(kind, int):
        return half(t) if kind else full()
    return jnp.where(kind == 0, full(), half(jnp.minimum(t, ref.shape[0] // nh - 1)))


def tile_places(kind, t, parity, span):
    col = lax.broadcasted_iota(jnp.int32, (1, QT), 1)
    at = t * QT + col
    block = lax.div(at, span // 2)
    j = at - block * (span // 2)
    quarter = span // 4
    outer = jnp.where(j >= quarter, j + 2 * quarter, j)
    half = block * span + jnp.where(parity == 0, outer, j + quarter)
    return jnp.where(kind == 0, at, half)


def loop(low, high, do):
    def step(c, _):
        do(c)
        return 0

    lax.fori_loop(low, high, step, 0)


def fwd_kernel(
    span,
    n_ref,
    kind_ref,
    tile_ref,
    par_ref,
    q_ref,
    k_ref,
    vt_ref,
    o_ref,
    low_ref,
    linv_ref,
    p_hbm,
    s0,
    s1,
    p0,
    p1,
    m0,
    m1,
    acc_scr,
    l_scr,
    sem0,
    sem1,
):
    i = pl.program_id(0)
    last = pl.num_programs(0) - 1
    before = jnp.maximum(i - 1, 0)
    n1 = n_ref[i]
    n2 = n_ref[before]
    unit1 = kind_ref[i]
    unit2 = kind_ref[before]

    def work(c1, c2, masked, now, old, q, place):
        s_now, m_now = now
        s_old, p_old, m_old = old
        if c1 is not None:
            m = m_now[...]
        if c2 is not None:
            top = jnp.max(m_old[...], axis=0, keepdims=True) * (logit_scale * LOG2E)
            l = l_scr[...]
            o = acc_scr[...]
        for j in range(KC // SUBF):
            if c1 is not None:
                off = c1 * KC + j * SUBF
                s = jnp.dot(k_ref[rows_of(off, SUBF), :], q, preferred_element_type=f32)
                if masked:
                    key = lax.broadcasted_iota(jnp.int32, (SUBF, QT), 0)
                    s = jnp.where(key <= place - off, s, masked_score)
                s_now[rows_of(off, SUBF), :] = s
                m = jnp.maximum(m, jnp.max(s.reshape(SUBF // 8, 8, QT), axis=0))
            if c2 is not None:
                off = c2 * KC + j * SUBF
                s = s_old[rows_of(off, SUBF), :]
                p = jnp.exp2(s * (logit_scale * LOG2E) - top)
                l = l + jnp.sum(p.reshape(SUBF // 8, 8, QT), axis=0)
                low = p.astype(bf16)
                p_old[rows_of(off, SUBF), :] = low
                o = o + jnp.dot(
                    vt_ref[unit2, :, rows_of(off, SUBF)], low, preferred_element_type=f32
                )
        if c1 is not None:
            m_now[...] = m
        if c2 is not None:
            l_scr[...] = l
            acc_scr[...] = o

    def send(c, p_scr, sem):
        part = rows_of(c * KC, KC)
        pltpu.make_async_copy(p_scr.at[part], p_hbm.at[before, part], sem).start()

    def drain(count, p_scr, sem):
        def wait(c):
            part = pl.ds(0, KC)
            pltpu.make_async_copy(p_scr.at[part], p_hbm.at[0, part], sem).wait()

        loop(0, count, wait)

    @pl.when(i >= 1)
    def _():
        l_scr[...] = jnp.zeros_like(l_scr)
        acc_scr[...] = jnp.zeros_like(acc_scr)

    slots = ((s0, p0, m0, sem0), (s1, p1, m1, sem1))
    for turn in (0, 1):
        s_now, p_now, m_now, sem_now = slots[turn]
        s_old, p_old, m_old, sem_old = slots[1 - turn]

        @pl.when(lax.rem(i, 2) == turn)
        def _(s_now=s_now, p_now=p_now, m_now=m_now, sem_now=sem_now, s_old=s_old, p_old=p_old, m_old=m_old, sem_old=sem_old, turn=turn):
            q = load_tile(q_ref, unit1, tile_ref[i], span)
            none = jnp.zeros_like(q)
            q = jnp.concatenate(
                [jnp.where(unit1 == 0, q, none), jnp.where(unit1 == 0, none, q)], axis=0
            )
            place = tile_places(unit1, tile_ref[i], par_ref[0], span)
            m_now[...] = jnp.full((8, QT), -jnp.inf, f32)

            @pl.when(i >= 3)
            def _():
                drain(n_ref[jnp.maximum(i - 3, 0)], p_old, sem_old)

            def go(c1, c2, masked=False):
                work(c1, c2, masked, (s_now, m_now), (s_old, p_old, m_old), q, place)

            if turn == 0:

                @pl.when(i == 0)
                def _():
                    loop(0, n1, lambda c: go(c, None, True))

            @pl.when(jnp.logical_and(i > 0, i < last))
            def _():
                go(n1 - 1, n2 - 1, True)
                send(n2 - 1, p_old, sem_old)
                both = jnp.minimum(n1, n2) - 1

                def step(c):
                    go(c, c)
                    send(c, p_old, sem_old)

                loop(0, both, step)
                loop(both, n1 - 1, lambda c: go(c, None))

            @pl.when(i == last)
            def _():
                def step(c):
                    go(None, c)
                    send(c, p_old, sem_old)

                loop(0, n2, step)
                drain(n_ref[jnp.maximum(i - 2, 0)], p_now, sem_now)
                drain(n2, p_old, sem_old)

    @pl.when(i > 0)
    def _():
        linv = 1.0 / jnp.sum(l_scr[...], axis=0, keepdims=True)
        o = acc_scr[...] * linv
        t = tile_ref[before]
        nf, nh = QT // span, 2 * QT // span
        for count, width, start, unit in ((nf, span, 0, 0), (nh, span // 2, span, 1)):

            @pl.when(unit2 == unit)
            def _(count=count, width=width, start=start):
                for j in range(count):
                    here = slice(j * width, (j + 1) * width)
                    there = pl.ds(start, width)
                    o_ref[t * count + j, :, there] = o[:, here]
                    low_ref[t * count + j, :, there] = o[:, here].astype(bf16)
                    linv_ref[t * count + j, :, there] = linv[:, here]


def table(values):
    return jnp.array(values, jnp.int32)


def pair_units(tiles):
    return sum(t[2] for t in tiles) * KC * QT


def whole(x):
    zeros = (0,) * len(x.shape)
    return pl.BlockSpec(x.shape, lambda *_: zeros)


def attn_fwd(q, k, vt, parity, tiles, span):
    nk = k.shape[0]
    steps = len(tiles)
    listed = tiles + [(tiles[-1][0], tiles[-1][1], 0)]
    linv = jax.ShapeDtypeStruct((q.shape[0], 1, q.shape[2]), f32)
    o = jax.ShapeDtypeStruct(q.shape, f32)
    work = pair_units(tiles)
    return pl.pallas_call(
        partial(fwd_kernel, span),
        name="attn_fwd",
        grid_spec=pltpu.PrefetchScalarGridSpec(
            num_scalar_prefetch=4,
            grid=(steps + 1,),
            in_specs=[whole(q), whole(k), whole(vt)],
            out_specs=[whole(q), whole(q), whole(linv), pl.BlockSpec(memory_space=pl.ANY)],
            scratch_shapes=[
                pltpu.VMEM((nk, QT), f32),
                pltpu.VMEM((nk, QT), f32),
                pltpu.VMEM((nk, QT), bf16),
                pltpu.VMEM((nk, QT), bf16),
                pltpu.VMEM((8, QT), f32),
                pltpu.VMEM((8, QT), f32),
                pltpu.VMEM((HEAD_DIM, QT), f32),
                pltpu.VMEM((8, QT), f32),
                pltpu.SemaphoreType.DMA,
                pltpu.SemaphoreType.DMA,
            ],
        ),
        out_shape=[
            o,
            jax.ShapeDtypeStruct(q.shape, bf16),
            linv,
            jax.ShapeDtypeStruct((steps, nk, QT), bf16),
        ],
        compiler_params=pltpu.CompilerParams(vmem_limit_bytes=VMEM),
        cost_estimate=pl.CostEstimate(
            flops=work * 1024, bytes_accessed=work * 2, transcendentals=work
        ),
    )(
        table([t[2] for t in listed]),
        table([t[0] for t in listed]),
        table([t[1] for t in listed]),
        parity.reshape(1),
        q,
        k,
        vt,
    )


def bwd_kernel(
    unit,
    span,
    qt,
    n_ref,
    tile_ref,
    slot_ref,
    turn_ref,
    par_ref,
    q_ref,
    do_ref,
    o_ref,
    linv_ref,
    kt_ref,
    v_ref,
    p_hbm,
    *refs,
):
    outs = refs[:-10]
    p_scr, dp0, dp1, q_scr, do_scr, de_scr, dq_scr, dk_scr, dv_scr, sem = refs[-10:]
    dps = (dp0, dp1)
    i = pl.program_id(0)
    last = pl.num_programs(0) - 1
    a = lax.rem(i, 2)
    b = 1 - a
    before = jnp.maximum(i - 1, 0)
    n1 = n_ref[i]
    n2 = n_ref[before]
    turn1 = turn_ref[i]
    turn2 = turn_ref[before]
    devices = kt_ref.shape[2] // span
    cuts = qt // QT
    width = span // 2 if unit else span

    def tile(ref):
        count = qt // width
        return jnp.concatenate([ref[tile_ref[i] * count + j] for j in range(count)], axis=-1)

    def fetch(t, slot):
        def start(c):
            part = rows_of(c * KC, KC)
            for s in range(cuts):
                there = p_scr.at[slot, part, pl.ds(s * QT, QT)]
                pltpu.make_async_copy(
                    p_hbm.at[slot_ref[t * cuts + s], part], there, sem.at[slot]
                ).start()

        loop(0, n_ref[t], start)

    def work(c1, dp_now, c2, slot, dp_old):
        if c1 is not None:
            do_now = do_scr[a]
        if c2 is not None:
            query = q_scr[slot]
            dot = do_scr[slot, unit * HEAD_DIM : (unit + 1) * HEAD_DIM, :]
            delta = de_scr[slot]
            dq = dq_scr[...]
        for j in range(KC // SUB):
            here = pl.ds(j * SUB, SUB)
            if c1 is not None:
                dp_now[here, :] = jnp.dot(
                    v_ref[rows_of(c1 * KC + j * SUB, SUB), :],
                    do_now,
                    preferred_element_type=f32,
                )
            if c2 is not None:
                keys = rows_of(c2 * KC + j * SUB, SUB)
                p = p_scr[slot, keys, :]
                ds = (p.astype(f32) * (dp_old[here, :] - delta)).astype(bf16)
                dv_scr[:, keys] += lax.dot_general(
                    dot, p, (((1,), (1,)), ((), ())), preferred_element_type=f32
                )
                dk_scr[:, keys] += lax.dot_general(
                    query, ds, (((1,), (1,)), ((), ())), preferred_element_type=f32
                )
                dq = dq + jnp.dot(kt_ref[0, :, keys], ds, preferred_element_type=f32)
        if c2 is not None:
            dq_scr[...] = dq

    def by_turn(turn, do):
        for t in (0, 1):

            @pl.when(lax.rem(turn, 2) == t)
            def _(t=t):
                do(dps[t], dps[1 - t])

    def load():
        scaled = tile(do_ref).astype(f32) * tile(linv_ref)
        de_scr[a] = jnp.sum(scaled * tile(o_ref), axis=0, keepdims=True)
        do_scr[a, unit * HEAD_DIM : (unit + 1) * HEAD_DIM, :] = scaled.astype(bf16)
        q_scr[a] = tile(q_ref)

    @pl.when(i == 0)
    def _():
        do_scr[...] = jnp.zeros_like(do_scr)
        dk_scr[...] = jnp.zeros_like(dk_scr)
        dv_scr[...] = jnp.zeros_like(dv_scr)
        dq_scr[...] = jnp.zeros_like(dq_scr)
        fetch(0, 0)
        load()
        work(0, dps[0], None, None, None)

    @pl.when(jnp.logical_and(i > 0, i < last))
    def _():
        load()

        def step(now, other):
            work(0, now, n2 - 1, b, other)

        by_turn(turn1, step)

    @pl.when(i == last)
    def _():
        by_turn(n2 - 1 + turn2, lambda now, other: work(None, None, n2 - 1, b, now))

    @pl.when(i > 0)
    def _():
        dq = (dq_scr[...] * logit_scale).astype(bf16)
        t = tile_ref[before]
        count = qt // width
        for j in range(count):
            outs[0][t * count + j, :HEAD_DIM, :width] = dq[:, j * width : (j + 1) * width]
        dq_scr[...] = jnp.zeros_like(dq_scr)

    @pl.when(i < last)
    def _():
        def wait(c):
            part = pl.ds(0, KC)
            pltpu.make_async_copy(p_scr.at[a, part], p_scr.at[a, part], sem.at[a]).wait()

        loop(0, n1, wait)

        @pl.when(i + 1 < last)
        def _():
            fetch(i + 1, b)

        def step(c):
            def both(now, other):
                work(c + 1, other, c, a, now)

            by_turn(c + turn1, both)

        loop(0, n1 - 1, step)

    @pl.when(i == last)
    def _():
        quarter = span // 4
        for d in range(devices):
            keys = pl.ds(d * span, span)
            dk = dk_scr[:, keys] * logit_scale
            dv = dv_scr[:, keys]
            if not unit:
                outs[0][d, HEAD_DIM : 2 * HEAD_DIM, :span] = dk.astype(bf16)
                outs[0][d, 2 * HEAD_DIM :, :span] = dv.astype(bf16)
            else:
                both = jnp.concatenate([dk, dv], axis=0)
                outer = jnp.concatenate([both[:, :quarter], both[:, 3 * quarter :]], axis=1)
                inner = both[:, quarter : 3 * quarter]
                even = par_ref[0] == 0
                outs[1][d] = jnp.where(even, outer, inner)
                outs[2][d] = jnp.where(even, inner, outer).astype(bf16)


def attn_bwd(unit, q, do, o, linv, kt, v, p, parity, tiles, slots, span):
    nk = kt.shape[2]
    steps = len(tiles)
    qt = KC if unit == 0 else QT
    width = span // 2 if unit else span

    def columns(x):
        return pl.BlockSpec((*x.shape[:2], width), lambda *_: (0, 0, 2 if unit else 0))

    listed = tiles + [(unit, tiles[-1][1], 0)]
    turns = [0]
    for t in tiles:
        turns.append((turns[-1] + t[2]) % 2)
    devices = nk // span
    if unit:
        outs = [
            jax.ShapeDtypeStruct((devices, HEAD_DIM, span // 2), bf16),
            jax.ShapeDtypeStruct((devices, 2 * HEAD_DIM, span // 2), f32),
            jax.ShapeDtypeStruct((devices, 2 * HEAD_DIM, span // 2), bf16),
        ]
    else:
        outs = [jax.ShapeDtypeStruct((devices, 3 * HEAD_DIM, span), bf16)]
    work = pair_units(tiles) * (qt // QT)
    return pl.pallas_call(
        partial(bwd_kernel, unit, span, qt),
        name="attn_bwd_half" if unit else "attn_bwd_full",
        grid_spec=pltpu.PrefetchScalarGridSpec(
            num_scalar_prefetch=5,
            grid=(steps + 1,),
            in_specs=[
                columns(q),
                columns(do),
                columns(o),
                columns(linv),
                pl.BlockSpec((1, HEAD_DIM, nk), lambda *_: (unit, 0, 0)),
                whole(v),
                pl.BlockSpec(memory_space=pl.ANY),
            ],
            out_specs=[whole(x) for x in outs],
            scratch_shapes=[
                pltpu.VMEM((2, nk, qt), bf16),
                pltpu.VMEM((KC, qt), f32),
                pltpu.VMEM((KC, qt), f32),
                pltpu.VMEM((2, HEAD_DIM, qt), bf16),
                pltpu.VMEM((2, 2 * HEAD_DIM, qt), bf16),
                pltpu.VMEM((2, 1, qt), f32),
                pltpu.VMEM((HEAD_DIM, qt), f32),
                pltpu.VMEM((HEAD_DIM, nk), f32),
                pltpu.VMEM((HEAD_DIM, nk), f32),
                pltpu.SemaphoreType.DMA((2,)),
            ],
        ),
        out_shape=outs,
        compiler_params=pltpu.CompilerParams(vmem_limit_bytes=VMEM),
        cost_estimate=pl.CostEstimate(
            flops=work * 2048, bytes_accessed=work * 2, transcendentals=0
        ),
    )(
        table([t[2] for t in listed]),
        table([t[1] for t in listed]),
        table(slots),
        table(turns),
        parity.reshape(1),
        q,
        do,
        o,
        linv,
        kt,
        v,
        p,
    )


def pick_quarters(x, parity, axis):
    q = x.shape[axis] // 4

    def cut(low, high):
        return x[low * q : high * q] if axis == 0 else x[:, low * q : high * q]

    outer = jnp.concatenate([cut(0, 1), cut(3, 4)], axis=axis)
    return jnp.where(parity == 0, outer, cut(1, 3))


def prep_kernel(count, pos_ref, par_ref, *refs):
    blocks = refs[:count]
    gain_ref, shift_ref, wt_ref, bt_ref, wn_ref, bn_ref = refs[count : count + 6]
    h_ref, q_ref, kt_ref, vt_ref, k_ref, v_ref, x_scr, sem = refs[count + 6 :]
    i = pl.program_id(0)
    for j in range(count):

        @pl.when(i == max(j - 1, 0))
        def _(j=j):
            pltpu.make_async_copy(blocks[j], x_scr.at[j % 2], sem.at[j % 2]).start()

    slot = lax.rem(i, 2)
    pltpu.make_async_copy(x_scr.at[slot], x_scr.at[slot], sem.at[slot]).wait()
    _, span, width = x_scr.shape
    d = HEAD_DIM
    cuts = 2
    sub = span // cuts
    for r in range(cuts):
        here = pl.ds(r * sub, sub)
        x = x_scr[slot, here, :].astype(f32)
        x = x - jnp.mean(x, axis=-1, keepdims=True)
        spread = jnp.mean(x * x, axis=-1, keepdims=True)
        h = (x * lax.rsqrt(spread + norm_eps) * gain_ref[...] + shift_ref[...]).astype(bf16)
        h_ref[here, :] = h
        over = lax.dot_general(
            wt_ref[...], h, (((1,), (1,)), ((), ())), preferred_element_type=f32
        )
        over = (over + bt_ref[...]).astype(bf16)
        q_ref[0, :, here] = over[:d]
        half = over[3 * d : 4 * d]
        low, high = half[:, : sub // 2], half[:, sub // 2 :]
        outer, inner = (low, high) if r == 0 else (high, low)
        q_ref[0, :, pl.ds(span + r * sub // 2, sub // 2)] = jnp.where(
            par_ref[0] == 0, outer, inner
        )
        for unit in (0, 1):
            kt_ref[unit, :, here] = over[(3 * unit + 1) * d : (3 * unit + 2) * d]
            vt_ref[unit, :, here] = over[(3 * unit + 2) * d : (3 * unit + 3) * d]
        flat = jnp.dot(h, wn_ref[...], preferred_element_type=f32) + bn_ref[...]
        flat = flat.astype(bf16)
        k_ref[here, :] = flat[:, : 2 * d]
        v_ref[here, :] = flat[:, 2 * d :]


def prep(blocks, pos, parity, gain, shift, wt, bt, wn, bn):
    count = len(blocks)
    span, width = blocks[0].shape
    devices = lax.axis_size("seq")
    nk = devices * span
    d = HEAD_DIM
    shapes = [
        ((nk, width), (span, width), lambda i, s, _: (s[i], 0)),
        ((devices, d, 3 * span // 2), (1, d, 3 * span // 2), lambda i, s, _: (s[i], 0, 0)),
        ((2, d, nk), (2, d, span), lambda i, s, _: (0, 0, s[i])),
        ((2, d, nk), (2, d, span), lambda i, s, _: (0, 0, s[i])),
        ((nk, 2 * d), (span, 2 * d), lambda i, s, _: (s[i], 0)),
        ((nk, 2 * d), (span, 2 * d), lambda i, s, _: (s[i], 0)),
    ]
    params = (gain, shift, wt, bt, wn, bn)
    return pl.pallas_call(
        partial(prep_kernel, count),
        name="prep",
        grid_spec=pltpu.PrefetchScalarGridSpec(
            num_scalar_prefetch=2,
            grid=(count,),
            in_specs=[pl.BlockSpec(memory_space=pl.ANY)] * count + [whole(x) for x in params],
            out_specs=[pl.BlockSpec(block, index) for _, block, index in shapes],
            scratch_shapes=[pltpu.VMEM((2, span, width), bf16), pltpu.SemaphoreType.DMA((2,))],
        ),
        out_shape=[jax.ShapeDtypeStruct(shape, bf16) for shape, _, _ in shapes],
        compiler_params=pltpu.CompilerParams(vmem_limit_bytes=VMEM),
        cost_estimate=pl.CostEstimate(
            flops=1, bytes_accessed=1, transcendentals=0
        ),
    )(pos, parity.reshape(1), *blocks, *params)


def pull_kernel(
    back_ref, pick_ref, grad_ref, mid_ref, gain_ref, w_ref, gm_ref, br_ref, do_ref, small_ref
):
    tokens = grad_ref.shape[0]
    gain = gain_ref[...]
    totals = [0.0, 0.0, 0.0]
    cut = tokens // 4
    for r in range(4):
        here = pl.ds(r * cut, cut)
        dh = jnp.dot(pick_ref[here, :], back_ref[...], preferred_element_type=f32)
        x = mid_ref[here, :]
        x = x - jnp.mean(x, axis=-1, keepdims=True)
        inv = lax.rsqrt(jnp.mean(x * x, axis=-1, keepdims=True) + norm_eps)
        x = x * inv
        d = dh * gain
        dx = inv * (
            d - jnp.mean(d, axis=-1, keepdims=True) - x * jnp.mean(d * x, axis=-1, keepdims=True)
        )
        gm = grad_ref[here, :].astype(f32) + dx
        branch = gm.astype(bf16)
        gm_ref[here, :] = gm
        br_ref[here, :] = branch
        for at, part in enumerate((branch.astype(f32), dh * x, dh)):
            totals[at] = totals[at] + jnp.sum(part, axis=0, keepdims=True)
    for at in range(3):
        small_ref[at : at + 1] = totals[at]
    do = lax.dot_general(
        w_ref[...], br_ref[...], (((1,), (1,)), ((), ())), preferred_element_type=f32
    ).astype(bf16)
    span = do_ref.shape[2] * 2 // 3
    for u in range(do.shape[1] // span * HEADS):
        n, head = u // HEADS, u % HEADS
        part = do[head * HEAD_DIM : (head + 1) * HEAD_DIM, n * span : (n + 1) * span]
        p, role = u // 3, u % 3
        if role != 1:
            do_ref[2 * p + role // 2, :, :span] = part
        else:
            q = span // 4
            outer = jnp.concatenate([part[:, :q], part[:, 3 * q :]], axis=1)
            do_ref[2 * p, :, span:] = outer
            do_ref[2 * p + 1, :, span:] = part[:, q : 3 * q]


def pull(back, pick, grad, mid, gain, w_out, span):
    tokens, width = grad.shape
    return pl.pallas_call(
        pull_kernel,
        name="pull",
        out_shape=[
            jax.ShapeDtypeStruct((tokens, width), f32),
            jax.ShapeDtypeStruct((tokens, width), bf16),
            jax.ShapeDtypeStruct((lax.axis_size("seq"), HEAD_DIM, 3 * span // 2), bf16),
            jax.ShapeDtypeStruct((3, width), f32),
        ],
        compiler_params=pltpu.CompilerParams(vmem_limit_bytes=VMEM),
        cost_estimate=pl.CostEstimate(
            flops=4 * tokens * width * width, bytes_accessed=tokens * width * 16, transcendentals=0
        ),
    )(back, pick, grad, mid, gain, w_out)


def pack_kernel(half, at_ref, part_ref, h_ref, out_ref, small_ref, piece_ref, acc, cnt):
    i = pl.program_id(0)
    devices, rows, tokens = part_ref.shape
    stretch, width = h_ref.shape[0] // devices, h_ref.shape[1]
    g = jnp.zeros((rows, width), f32)
    count = jnp.zeros((8, rows), f32)
    ones = jnp.ones((8, tokens), bf16)
    for d in range(devices):
        part = part_ref[d]
        h = h_ref[pl.ds(d * stretch, stretch), :]
        if half:
            h = pick_quarters(h, at_ref[1], 0)
        g += jnp.dot(part, h, preferred_element_type=f32)
        count += lax.dot_general(
            ones, part, (((1,), (1,)), ((), ())), preferred_element_type=f32
        )

    @pl.when(i == 0)
    def _():
        acc[...] = g
        cnt[...] = count

    @pl.when(i > 0)
    def _():
        acc[...] += g
        cnt[...] += count

    @pl.when(i == pl.num_programs(0) - 1)
    def _():
        nexp, share, _ = piece_ref.shape
        line = jnp.concatenate([cnt[...], jnp.zeros((8, width - rows), f32)], axis=1)
        line = jnp.concatenate([line, small_ref[...]], axis=0)
        filled = rows + out_ref.shape[0] + 16
        parts = [acc[...].astype(bf16), out_ref[...], line.astype(bf16)]
        if nexp * share > filled:
            parts.append(jnp.zeros((nexp * share - filled, width), bf16))
        piece = jnp.concatenate(parts, axis=0)
        for e in range(nexp):
            piece_ref[at_ref[0] ^ e] = piece[e * share : (e + 1) * share]


def pack(part, h1, parity, half, out_rows, small):
    devices, rows, _ = part.shape
    nk, width = h1.shape
    nexp = lax.axis_size("exp")
    filled = rows + out_rows.shape[0] + 16
    share = -(-filled // (16 * nexp)) * 16
    steps = 4
    return pl.pallas_call(
        partial(pack_kernel, half),
        name="pack_half" if half else "pack_full",
        grid_spec=pltpu.PrefetchScalarGridSpec(
            num_scalar_prefetch=1,
            grid=(steps,),
            in_specs=[
                pl.BlockSpec(
                    (devices // steps, rows, nk // devices // (2 if half else 1)),
                    lambda i, _: (i, 0, 0),
                ),
                pl.BlockSpec((nk // steps, width), lambda i, _: (i, 0)),
                whole(out_rows),
                whole(small),
            ],
            out_specs=pl.BlockSpec((nexp, share, width), lambda i, _: (0, 0, 0)),
            scratch_shapes=[pltpu.VMEM((rows, width), f32), pltpu.VMEM((8, rows), f32)],
        ),
        out_shape=jax.ShapeDtypeStruct((nexp, share, width), bf16),
        compiler_params=pltpu.CompilerParams(vmem_limit_bytes=VMEM),
        cost_estimate=pl.CostEstimate(flops=1, bytes_accessed=1, transcendentals=0),
    )(jnp.stack([lax.axis_index("exp"), parity]), part, h1, out_rows, small)


def home_kernel(nseq, span, full_ref, half_ref, w_ref, x_ref, gain_ref, gm_ref, dx_ref, u_scr):
    pairs = full_ref.shape[0] // 2
    quarter = span // 4
    for n in range(nseq):
        here = pairs // nseq
        for j in range(here):
            p = n * here + j
            outer, inner = half_ref[2 * p], half_ref[2 * p + 1]
            mid = jnp.concatenate([outer[:, :quarter], inner, outer[:, quarter:]], axis=1)
            for role, unit in enumerate((full_ref[2 * p], mid, full_ref[2 * p + 1])):
                for c in range(3):
                    at = c * HEADS + 3 * j + role
                    u_scr[pl.ds(at * HEAD_DIM, HEAD_DIM), :] = unit[
                        c * HEAD_DIM : (c + 1) * HEAD_DIM
                    ]
        dh = jnp.dot(w_ref[...], u_scr[...], preferred_element_type=f32).T
        x = x_ref[n].astype(f32)
        x = x - jnp.mean(x, axis=-1, keepdims=True)
        inv = lax.rsqrt(jnp.mean(x * x, axis=-1, keepdims=True) + norm_eps)
        x = x * inv
        d = dh * gain_ref[...]
        dx_ref[n] = gm_ref[n] + inv * (
            d - jnp.mean(d, axis=-1, keepdims=True) - x * jnp.mean(d * x, axis=-1, keepdims=True)
        )


def home(full, half, w_qkv, x, gain, grad_middle):
    nseq, span, width = x.shape
    return pl.pallas_call(
        partial(home_kernel, nseq, span),
        name="home",
        out_shape=jax.ShapeDtypeStruct((nseq, span, width), f32),
        scratch_shapes=[pltpu.VMEM((3 * width, span), bf16)],
        compiler_params=pltpu.CompilerParams(vmem_limit_bytes=VMEM),
        cost_estimate=pl.CostEstimate(
            flops=1, bytes_accessed=1, transcendentals=0
        ),
    )(full, half, w_qkv, x, gain, grad_middle)


def part_kernel(got_ref, up_ref, down_ref, line_ref):
    share = up_ref.shape[1]
    up_ref[...] = got_ref[:share].T.astype(f32)
    down_ref[...] = got_ref[share : 2 * share].astype(f32)
    line_ref[...] = got_ref[2 * share :].astype(f32)


def part_shares(got, share):
    width = got.shape[1]
    return pl.pallas_call(
        part_kernel,
        name="part_shares",
        out_shape=[
            jax.ShapeDtypeStruct((width, share), f32),
            jax.ShapeDtypeStruct((share, width), f32),
            jax.ShapeDtypeStruct((got.shape[0] - 2 * share, width), f32),
        ],
        compiler_params=pltpu.CompilerParams(vmem_limit_bytes=VMEM),
        cost_estimate=pl.CostEstimate(flops=1, bytes_accessed=1, transcendentals=0),
    )(got)


def build_kernel(nseq, nexp, devices, cut, at_ref, *refs):
    halves, fulls = refs[0], refs[1 : 1 + devices]
    w_ref, gain_ref, shift_ref, g_ref, out_ref, small_ref, half, full, acc, sem = refs[1 + devices :]
    me, z = at_ref[0], at_ref[1]
    c = pl.program_id(0)
    d = HEAD_DIM
    rows = 3 * d
    width = g_ref.shape[0]
    out_rows = width // devices

    @pl.when(c == 0)
    def _():
        for j in range(devices):
            for e in range(nexp):
                for block, got in ((halves.at[j], half), (fulls[j], full)):
                    share = got.shape[1] // nexp
                    pltpu.make_async_copy(
                        block.at[pl.ds(pl.multiple_of((z ^ e) * share, 16), share)],
                        got.at[j, pl.ds(e * share, share)],
                        sem,
                    ).start()
        acc[...] = jnp.zeros_like(acc)
        pltpu.make_async_copy(half, half, sem).wait()
        pltpu.make_async_copy(full, full, sem).wait()

    def from_unit(u, at, lanes):
        p, role = u // 3, u % 3
        if role != 1:
            return full[me ^ (2 * p + role // 2), at, lanes].astype(f32)
        return half[2 * p, at, lanes].astype(f32) + half[2 * p + 1, at, lanes].astype(f32)

    def unit_rows(u):
        return from_unit(u, rows_of(c * d, d), slice(None))

    def unit_sums(u):
        line = rows + (cut if u % 3 == 1 else out_rows - cut)
        line = from_unit(u, pl.ds(line, 16), pl.ds(0, rows))[:1]
        return jnp.where(c == 0, line[:, :d], jnp.where(c == 1, line[:, d : 2 * d], line[:, 2 * d :]))

    for two in range(HEADS // 2):
        heads = (2 * two, 2 * two + 1)
        grads = [sum(unit_rows(n * HEADS + h) for n in range(nseq)) for h in heads]
        sums = [sum(unit_sums(n * HEADS + h) for n in range(nseq)) for h in heads]
        at = pl.ds(two * 2 * d, 2 * d)
        block = jnp.concatenate(grads, axis=0)
        total = jnp.concatenate(sums, axis=1)
        g_ref[:, at] = block.T
        w = w_ref[at, :]
        gained = w.astype(f32) * block
        acc[:8] += jnp.sum(gained.reshape(2 * d // 8, 8, width), axis=0)
        acc[8:16] += jnp.dot(
            jnp.broadcast_to(total, (8, 2 * d)).astype(bf16), w, preferred_element_type=f32
        )

        acc[pl.ds(16 + 8 * c, 1), at] = total
    @pl.when(c == 2)
    def _():
        gained = jnp.sum(acc[:8], axis=0, keepdims=True)
        shifted = acc[8:9]
        small_ref[0:1] = (gained - shift_ref[...] * shifted) / gain_ref[...]
        small_ref[1:2] = shifted
        small_ref[2:3] = acc[16:17]
        small_ref[3:4] = acc[32:33]
        small_ref[4:7] = half[0, pl.ds(rows + cut, 16), :].astype(f32)[8:11]
        small_ref[7:8] = jnp.zeros_like(shifted)
        for i in range(devices):
            out_ref[pl.ds(i * out_rows, cut), :] = half[i, pl.ds(rows, cut), :].astype(f32)
            out_ref[pl.ds(i * out_rows + cut, out_rows - cut), :] = full[
                me ^ i, pl.ds(rows, out_rows - cut), :
            ].astype(f32)


def build(halves, fulls, cut, w_rows, gain, shift, nseq):
    width = w_rows.shape[1]
    devices = len(fulls)
    nexp = lax.axis_size("exp")
    at = jnp.stack([lax.axis_index("seq"), lax.axis_index("exp")])
    away = pl.BlockSpec(memory_space=pl.ANY)
    return pl.pallas_call(
        partial(build_kernel, nseq, nexp, devices, cut),
        name="build",
        grid=(3,),
        in_specs=[pl.BlockSpec(memory_space=pltpu.SMEM)]
        + [away] * (1 + devices)
        + [pl.BlockSpec((width, width), lambda c: (c, 0)), whole(gain), whole(shift)],
        out_specs=[
            pl.BlockSpec((width, width), lambda c: (0, c)),
            pl.BlockSpec((width, width), lambda c: (0, 0)),
            pl.BlockSpec((8, width), lambda c: (0, 0)),
        ],
        out_shape=[
            jax.ShapeDtypeStruct((width, 3 * width), f32),
            jax.ShapeDtypeStruct((width, width), f32),
            jax.ShapeDtypeStruct((8, width), f32),
        ],
        scratch_shapes=[
            pltpu.VMEM(halves.shape, bf16),
            pltpu.VMEM((devices, *fulls[0].shape), bf16),
            pltpu.VMEM((40, width), f32),
            pltpu.SemaphoreType.DMA,
        ],
        compiler_params=pltpu.CompilerParams(vmem_limit_bytes=VMEM),
        cost_estimate=pl.CostEstimate(
            flops=0, bytes_accessed=18 * width * width, transcendentals=0
        ),
    )(at, halves, *fulls, w_rows, gain, shift)


def expert_sums_kernel(rows_ref, dy_ref, dz_ref, hid_ref, out_ref):
    contract = (((0,), (0,)), ((), ()))
    dz = dz_ref[...]
    share = dz.shape[1]
    dy = dy_ref[...]
    out_ref[0, :share] = lax.dot_general(
        dz, rows_ref[...], contract, preferred_element_type=f32
    ).astype(bf16)
    out_ref[0, share : 2 * share] = lax.dot_general(
        hid_ref[...], dy, contract, preferred_element_type=f32
    ).astype(bf16)
    ones = jnp.ones((16, dz.shape[0]), bf16)
    up = jnp.dot(ones, dz, preferred_element_type=f32).astype(bf16)
    fill = jnp.zeros((16, dy.shape[1] - share), bf16)
    out_ref[0, 2 * share : 2 * share + 16] = jnp.concatenate([up, fill], axis=1)
    out_ref[0, 2 * share + 16 :] = jnp.dot(ones, dy, preferred_element_type=f32).astype(bf16)


def expert_sums(rows, dy, dz, hidden):
    devices = lax.axis_size("seq")
    count, width = rows.shape
    ff = dz.shape[1]
    share = ff // devices
    if share % 128:
        contract = (((0,), (0,)), ((), ()))
        up = lax.dot_general(dz, rows, contract, preferred_element_type=f32)
        down = lax.dot_general(hidden, dy, contract, preferred_element_type=f32)
        up_bias = jnp.pad(
            jnp.sum(dz, axis=0, dtype=f32).reshape(devices, 1, share),
            ((0, 0), (0, 15), (0, width - share)),
        )
        down_bias = jnp.broadcast_to(jnp.sum(dy, axis=0, dtype=f32), (devices, 16, width))
        return jnp.concatenate(
            [up.reshape(devices, share, width), down.reshape(devices, share, width), up_bias, down_bias],
            axis=1,
        ).astype(bf16)
    total = 2 * share + 32
    return pl.pallas_call(
        expert_sums_kernel,
        name="expert_sums",
        grid=(devices,),
        in_specs=[
            pl.BlockSpec((count, width), lambda j: (0, 0)),
            pl.BlockSpec((count, width), lambda j: (0, 0)),
            pl.BlockSpec((count, share), lambda j: (0, j)),
            pl.BlockSpec((count, share), lambda j: (0, j)),
        ],
        out_specs=pl.BlockSpec((1, total, width), lambda j: (j, 0, 0)),
        out_shape=jax.ShapeDtypeStruct((devices, total, width), bf16),
        compiler_params=pltpu.CompilerParams(vmem_limit_bytes=VMEM),
        cost_estimate=pl.CostEstimate(
            flops=1, bytes_accessed=1, transcendentals=0
        ),
    )(rows, dy, dz, hidden)


def swap(x, axis, distance):
    return lax.ppermute(x, axis, [(i, i ^ distance) for i in range(lax.axis_size(axis))])


def gather_chips(x, beside=None):
    chips = lax.axis_size("seq") // 2
    if chips != 4:
        return [x] + [swap(x, "seq", 2 * d) for d in range(1, chips)], beside
    one, two = swap(x, "seq", 2), swap(x, "seq", 4)
    if beside is not None:
        one, two, beside = lax.optimization_barrier((one, two, beside))
    axis = x.ndim - 2
    half = x.shape[axis] // 2
    low = swap(lax.slice_in_dim(one, 0, half, axis=axis), "seq", 4)
    high = swap(lax.slice_in_dim(two, half, 2 * half, axis=axis), "seq", 2)
    return [x, one, two, jnp.concatenate([low, high], axis=axis)], beside


def gather_seq(x, beside):
    blocks = []
    chips, beside = gather_chips(x, beside)
    for block in chips:
        blocks += [block, swap(block, "seq", 1)]
    return blocks, beside


def in_order(stack, axis):
    me = lax.axis_index(axis)
    return jnp.take(stack, me ^ lax.iota(jnp.int32, stack.shape[0]), axis=0)


def sum_exp(parts):
    total = parts[0].astype(f32)
    for d in range(1, parts.shape[0]):
        total = total + swap(parts[d], "exp", d).astype(f32)
    return total.astype(bf16)


def gather_exp(total):
    return jnp.concatenate([total] + [swap(total, "exp", d) for d in range(1, lax.axis_size("exp"))])


def layer_norm(values, gain, shift):
    centre = jnp.mean(values, axis=-1, keepdims=True)
    centered = values - centre
    spread = jnp.mean(centered * centered, axis=-1, keepdims=True)
    return centered * lax.rsqrt(spread + norm_eps) * gain + shift


def from_owners(got, span):
    quarter = span // 4
    both = got.reshape(got.shape[0] // 2, 2, *got.shape[1:])
    outer, inner = both[:, 0, ..., span:], both[:, 1, ..., span:]
    mid = jnp.concatenate([outer[..., :quarter], inner, outer[..., quarter:]], axis=-1)
    return jnp.stack([both[:, 0, ..., :span], mid, both[:, 1, ..., :span]], axis=1)


def exchange(x, axis):
    return lax.all_to_all(x, axis, split_axis=0, concat_axis=0, tiled=True)


def exchange_exp(x):
    nexp = lax.axis_size("exp")
    parts = x.reshape(nexp, x.shape[0] // nexp, x.shape[1])
    return jnp.concatenate([parts[0]] + [swap(parts[d], "exp", d) for d in range(1, nexp)])


def local(
    inputs,
    token_ids,
    hash_table,
    capacity,
    ln1_gain,
    ln1_bias,
    w_qkv,
    q_bias,
    v_bias,
    w_out,
    out_bias,
    ln2_gain,
    ln2_bias,
    up_weight,
    up_bias,
    down_weight,
    down_bias,
    out_grad,
):
    nseq, span, width = inputs.shape
    tokens = nseq * span
    cycle = lax.axis_size("seq")
    me = lax.axis_index("seq")
    parity = me % 2
    pair = me // 2
    pairs = cycle // 2
    nk = cycle * span
    assert nseq * HEADS == 3 * pairs
    up, down = up_weight[0], down_weight[0]
    ff = up.shape[1]
    share = ff // cycle
    row = lambda x: x.reshape(1, -1)

    mine = (3 * pair) // HEADS
    def of_sequence(blocks):
        return [lax.dynamic_index_in_dim(b, mine, 0, keepdims=False) for b in blocks]


    experts = capacity.shape[0]
    cap = 5 * tokens // (4 * experts)
    expert_of = jnp.take(hash_table, token_ids.reshape(tokens))
    onehot = (expert_of[:, None] == lax.iota(jnp.int32, experts)[None, :]).astype(jnp.int32)
    rank = jnp.sum(onehot * (jnp.cumsum(onehot, axis=0) - 1), axis=1)
    kept = rank < jnp.take(capacity, expert_of)
    near_expert = expert_of ^ lax.axis_index("exp")
    slot = jnp.where(kept, near_expert * cap + rank, experts * cap)
    slots = lax.iota(jnp.int32, experts * cap)
    place = (slots[:, None] == slot[None, :]).astype(bf16)
    pick = (slots[None, :] == slot[:, None]).astype(bf16)

    def to_experts(rows):
        sent = jnp.dot(place, rows, preferred_element_type=f32).astype(bf16)
        return exchange_exp(sent)

    grad_rows = out_grad.reshape(tokens, width)
    dy = to_experts(grad_rows)
    da = lax.dot_general(dy, down, (((1,), (1,)), ((), ())), preferred_element_type=f32)
    da = da.astype(bf16)

    head_full = (3 * pair + 2 * parity) % HEADS
    head_half = (3 * pair + 1) % HEADS
    w_heads = w_qkv.reshape(width, 3, HEADS, HEAD_DIM)

    def of_head(x, axis):
        return jnp.stack(
            [
                lax.dynamic_index_in_dim(x, head_full, axis, keepdims=False),
                lax.dynamic_index_in_dim(x, head_half, axis, keepdims=False),
            ]
        )

    w_mine = of_head(w_heads, 2)
    qb = of_head(q_bias.reshape(HEADS, HEAD_DIM), 0)
    vb = of_head(v_bias.reshape(HEADS, HEAD_DIM), 0)
    bias = jnp.stack([qb, jnp.zeros_like(qb), vb], axis=1)
    wt = w_mine.transpose(0, 2, 3, 1).reshape(6 * HEAD_DIM, width)
    wn = w_mine[:, :, 1:].transpose(1, 2, 0, 3).reshape(width, 4 * HEAD_DIM)
    bn = row(bias[:, 1:].transpose(1, 0, 2))
    params = (row(ln1_gain), row(ln1_bias), wt, bias.reshape(-1, 1), wn, bn)
    places = me ^ lax.iota(jnp.int32, cycle)
    chips, _ = gather_chips(inputs)
    far, params, pick, place, places = lax.optimization_barrier(
        (chips[-1], params, pick, place, places)
    )
    blocks = []
    for block in chips[:-1] + [far]:
        blocks += [block, swap(block, "seq", 1)]
    h1, q, kt, vt, k, v = prep(of_sequence(blocks), places, parity, *params)

    full = [(0, i, (i * QT + QT + KC - 1) // KC) for i in range(nk // QT)]
    half = [(1, i, (2 * (i * QT + QT) + KC - 1) // KC) for i in range(nk // (2 * QT))]
    tiles = sorted(full + half, key=lambda t: t[2])
    wide = [(0, i, i + 1) for i in range(nk // KC)]
    attn, attn_low, linv, p = attn_fwd(q, k, vt, parity, tiles, span)

    got = from_owners(exchange(attn_low, "seq"), span).reshape(nseq, width, span)
    x_rows = inputs.reshape(tokens, width).astype(f32)
    middle = (
        x_rows
        + jnp.einsum("nht,hd->ntd", got, w_out, preferred_element_type=f32).reshape(tokens, width)
        + out_bias
    )
    h2 = layer_norm(middle, ln2_gain, ln2_bias).astype(bf16)

    h2, da, pick = lax.optimization_barrier((h2, da, pick))
    rows = lax.optimization_barrier(to_experts(h2))
    z = jnp.dot(rows, up, preferred_element_type=f32) + up_bias
    phi = 0.5 * (1.0 + lax.erf(z * (1.0 / math.sqrt(2.0))))
    hidden = (z * phi).astype(bf16)
    slope = phi + z * jnp.exp(-0.5 * z * z) * (1.0 / math.sqrt(2.0 * math.pi))
    dz = (da.astype(f32) * slope).astype(bf16)
    dh2 = lax.dot_general(dz, up, (((1,), (1,)), ((), ())), preferred_element_type=f32)
    back = exchange_exp(dh2.astype(bf16))
    shares = expert_sums(rows, dy, dz, hidden)
    y = jnp.dot(hidden, down, preferred_element_type=f32) + down_bias[0]
    back, shares, y = lax.optimization_barrier((back, shares, y.astype(bf16)))

    grad_middle, branch, do_home, small2 = pull(
        back, pick, grad_rows, middle, row(ln2_gain), w_out, span
    )
    do = exchange(do_home, "seq")
    low_rows = got.transpose(0, 2, 1).reshape(tokens, width)
    grad_w_out = lax.dot_general(
        low_rows, branch, (((0,), (0,)), ((), ())), preferred_element_type=f32
    ).astype(bf16)
    small2 = jnp.pad(small2, ((0, 13), (0, 0))).astype(bf16)
    out_rows = width // cycle
    cut = -(-out_rows // 32) * 16
    do, grad_w_out, small2, shares = lax.optimization_barrier((do, grad_w_out, small2, shares))
    shares = lax.psum_scatter(
        shares.reshape(-1, width), "seq", scatter_dimension=0, tiled=True
    )
    w_out_part = jnp.concatenate(
        [
            grad_w_out.reshape(cycle, width // cycle, width),
            jnp.broadcast_to(small2[None], (cycle, 16, width)),
        ],
        axis=1,
    )
    w_out_part = jnp.sum(exchange(w_out_part, "seq"), axis=0, dtype=f32)
    small2 = w_out_part[out_rows : out_rows + 8]
    w_out_part = w_out_part[:out_rows].astype(bf16)

    slot_of = {t[:2]: j for j, t in enumerate(tiles)}
    dq_half, sums_mine, sums_other = attn_bwd(
        1, q, do, attn, linv, kt, v, p, parity, half, [slot_of[t[:2]] for t in half], span
    )
    sums = (sums_mine + swap(sums_other, "seq", 1).astype(f32)).astype(bf16)
    part_half = jnp.concatenate([dq_half, sums], axis=1)
    home_half = exchange(part_half, "seq")
    packed = pack(part_half, h1, parity, True, w_out_part[:cut], small2)
    both = jnp.concatenate([packed, y.reshape(experts, cap, width)], axis=1)
    both, late = lax.optimization_barrier((both, do))
    both = [both[0]] + [swap(both[d], "exp", d) for d in range(1, experts)]
    count = packed.shape[1]
    sum_half = sum(part[:count].astype(f32) for part in both).astype(bf16)
    y_back = jnp.concatenate([part[count:] for part in both])
    part_full = attn_bwd(
        0, q, late, attn, linv, kt, v, p, parity, wide, [slot_of[t[:2]] for t in full], span
    )[0]
    part_full, home_half, sum_half = lax.optimization_barrier((part_full, home_half, sum_half))

    packed = pack(part_full, h1, parity, False, w_out_part[cut:], jnp.zeros_like(small2))
    column_half, packed, part_full = lax.optimization_barrier(
        (gather_exp(sum_half), packed, part_full)
    )
    halves = lax.all_gather(column_half, "seq")
    home_full = exchange(part_full, "seq")
    sum_full = sum_exp(packed)
    input_grad = home(
        home_full,
        home_half,
        w_qkv,
        inputs,
        row(ln1_gain),
        grad_middle.reshape(nseq, span, width),
    )
    output = middle + jnp.dot(pick, y_back, preferred_element_type=f32)
    output = output.astype(bf16).reshape(nseq, span, width)
    up_grad, down_grad, lines = part_shares(shares, share)
    down_share = lax.dynamic_slice_in_dim(lines[16], me * (width // cycle), width // cycle, 0)
    expert_grads = (up_grad[None], lines[:1, :share], down_grad[None], down_share[None])
    column, output, expert_grads = lax.optimization_barrier(
        (gather_exp(sum_full), output, expert_grads)
    )
    fulls, input_grad = gather_seq(column, input_grad)
    grad_w_qkv, grad_w_out, small = build(
        halves, fulls, cut, w_qkv.T, row(ln1_gain), row(ln1_bias), nseq
    )
    return (
        output,
        input_grad,
        small[0],
        small[1],
        grad_w_qkv,
        small[2],
        small[3],
        grad_w_out,
        small[4],
        small[5],
        small[6],
        *expert_grads,
    )


def solution(mesh):
    in_specs = (
        P("exp", "seq", None),
        P("exp", "seq"),
        P(),
        P(),
        P(),
        P(),
        P(),
        P(),
        P(),
        P(),
        P(),
        P(),
        P(),
        P("exp", None, None),
        P("exp", None),
        P("exp", None, None),
        P("exp", None),
        P("exp", "seq", None),
    )
    out_specs = (
        P("exp", "seq", None),
        P("exp", "seq", None),
        P(),
        P(),
        P(),
        P(),
        P(),
        P(),
        P(),
        P(),
        P(),
        P("exp", None, "seq"),
        P("exp", "seq"),
        P("exp", "seq", None),
        P("exp", "seq"),
    )
    return jax.shard_map(local, mesh=mesh, in_specs=in_specs, out_specs=out_specs, check_vma=False)
```
